256 devices in a mesh: span: 8 (over x, y_hi), seq: 32 (over y_lo, z, core).
Axes of the slice: x: 4, y: 4 (y_hi: 2, y_lo: 2; y = y_hi * 2 + y_lo), z: 8, core: 2. Of those that a mesh axis runs over, the one named last changes fastest.
Arguments:
- hidden: bfloat16 [8, 1024, 3072], P('span', 'seq'), may hold values from -6 to 6
- levels: int32 [8], P('span'), may hold values from 0 to 15
- span_order: int32 [8], replicated, may hold values from 0 to 7, each once
- modulation: float32 [16, 3, 3072], replicated, may hold values from -1 to 4
- in_weight: bfloat16 [32, 3072, 384], P('seq'), may hold values from -1 to 1
- out_weight: bfloat16 [32, 128, 3072], P('seq'), may hold values from -0.109375 to 0.109375
- latent_weight: bfloat16 [3072, 64], replicated, may hold values from -0.109375 to 0.109375
- decoder_weight: bfloat16 [3, 3, 3, 16, 512], P(None, None, None, None, 'span'), may hold values from -0.3125 to 0.3125
Outputs:
- block_out: bfloat16 [8, 1024, 3072], P('span', 'seq')
- decoded: bfloat16 [32, 2, 64, 512], P('seq', None, None, 'span')
The draws below stay inside these ranges and needn't reach their ends.
Inputs may be any that keep to these rules, and one draw needn't show every extreme that they name: `span_order`: each span has a different place in time.
All inputs are finite; a program needn't handle non-finite values.
Results may differ from the reference program's by a relative error of at most 0.03.
Values may be sent and summed in bfloat16 or wider, within the bound.
No kernel may reach another device: no remote copies, remote signals or barrier semaphores. Data moves between devices by JAX's collectives and lax.ppermute only.
A program may use at most 64 MiB of HBM per device.

```python
import math
import jax
import jax.numpy as jnp
from jax import lax

D = 3072
HEADS = 24
HD = 128
LEVELS = 16
FR = 4
P_SIZE = 2
C = 16
CO = 512
SPANS = 8
TOKENS = 1024
SLOTS = 32
PV = 64
N_SEQ = 32


def draw_hidden(key, part):
    key = jax.random.fold_in(key, 23)
    base_key = jax.random.fold_in(key, 0)
    shape = (SPANS, TOKENS, D)
    return jnp.clip(jax.random.normal(base_key, shape, jnp.float32), -6.0, 6.0).astype(jnp.bfloat16)


def draw_in_weight(key, part):
    key = jax.random.fold_in(key, 31)
    base_key = jax.random.fold_in(key, 0)
    base = jnp.clip(jax.random.normal(base_key, (SLOTS, D, 3 * HD), jnp.float32), -4.0, 4.0) * D ** (-0.5)
    return base.astype(jnp.bfloat16)


def draw_modulation(key, part):
    key = jax.random.fold_in(key, 11)
    first_key, second_key, third_key = jax.random.split(key, 3)
    shape = (LEVELS, 1, D)
    shift_rows = jax.random.uniform(first_key, shape, jnp.float32, -1.0, 1.0)
    scale_rows = jax.random.uniform(second_key, shape, jnp.float32, 0.2, 2.0)
    gate_rows = jnp.exp(jax.random.uniform(third_key, shape, jnp.float32, math.log(0.5), math.log(4.0)))
    return jnp.concatenate([shift_rows, scale_rows, gate_rows], axis=1)


def touch_ends(entries, rng, least, top_value):
    index_at = [jax.random.randint(jax.random.fold_in(rng, axis), (), 0, length) for axis, length in enumerate(entries.shape)]
    main_axis = entries.shape.index(max(entries.shape))
    next_to = index_at[:main_axis] + [(index_at[main_axis] + 1) % entries.shape[main_axis]] + index_at[main_axis + 1:]
    return entries.at[tuple(index_at)].set(least).at[tuple(next_to)].set(top_value)


def block_scale(own_key, extent, shards, least, largest):
    def one(dim, blocks):
        heights = jax.random.uniform(jax.random.fold_in(jax.random.fold_in(own_key, 6), dim), (blocks,), jnp.float32, least / len(shards), largest / len(shards))
        return jnp.repeat(jnp.exp(heights), extent[dim] // blocks).reshape((-1,) + (1,) * (len(extent) - dim - 1))

    gain = one(*shards[0])
    for cut in shards[1:]:
        gain = gain * one(*cut)
    return gain


def normal_values(own_key, extent, scale, bound, cuts=(), held_as=jnp.bfloat16):
    result = scale * jax.random.normal(own_key, extent, jnp.float32)
    if cuts:
        result = result * block_scale(own_key, extent, cuts, -0.22, 0.18)
    return jnp.clip(result, -bound, bound).astype(held_as)


def setup_inputs(seed: int = 0) -> dict:
    key_list = jax.random.split(jax.random.key(seed), 9)
    hidden = draw_hidden(jax.random.fold_in(key_list[8], 71), 0)
    levels = touch_ends(jax.random.randint(key_list[1], (SPANS,), 0, LEVELS), jax.random.fold_in(key_list[1], 1), 0, LEVELS - 1).astype(jnp.int32)
    span_order = jax.random.permutation(key_list[2], SPANS).astype(jnp.int32)
    modulation = draw_modulation(jax.random.fold_in(key_list[8], 71), 0)
    in_weight = draw_in_weight(jax.random.fold_in(key_list[8], 71), 0)
    out_weight = normal_values(key_list[5], (SLOTS, HD, D), D ** -0.5, 0.109375, ((0, 32),))
    latent_weight = normal_values(key_list[6], (D, PV), D ** -0.5, 0.109375)
    decoder_weight = normal_values(key_list[7], (3, 3, 3, C, CO), (27 * C) ** -0.5, 0.3125, ((4, 8),))
    return dict(hidden=hidden, levels=levels, span_order=span_order, modulation=modulation, in_weight=in_weight, out_weight=out_weight, latent_weight=latent_weight, decoder_weight=decoder_weight)


EPSILON = 1e-06

def normalize(rows, shift_row, scale_row):
    values = rows.astype(jnp.float32)
    center = values - lax.optimization_barrier(jnp.mean(values, axis=-1, keepdims=True))
    spread = lax.optimization_barrier(jnp.mean(center * center, axis=-1, keepdims=True))
    return (center * lax.rsqrt(spread + EPSILON) * (1.0 + scale_row) + shift_row).astype(jnp.bfloat16)

def reference(hidden, levels, span_order, modulation, in_weight, out_weight, latent_weight, decoder_weight):
    span_count, span_len, model_width = hidden.shape
    head_dim = in_weight.shape[2] // 3
    slot_count = in_weight.shape[0]
    per_group = slot_count // N_SEQ
    mods = jnp.take(modulation, levels, axis=0)
    normed = normalize(hidden, mods[:, 0][:, None, :], mods[:, 1][:, None, :])
    triples = jnp.einsum('ctd,hde->hcte', normed.astype(jnp.float32), in_weight[:HEADS].astype(jnp.float32)).astype(jnp.bfloat16)
    triples = lax.optimization_barrier(triples)
    ranks = span_order.astype(jnp.float32)
    visible = jnp.repeat(ranks[None, :] <= ranks[:, None], span_len, axis=1)
    scale_factor = 1.0 / math.sqrt(head_dim)

    def head_attention(head_triple):
        queries = head_triple[:, :, :head_dim].astype(jnp.float32)
        key_rows = head_triple[:, :, head_dim:2 * head_dim].reshape(-1, head_dim).astype(jnp.float32)
        value_rows = head_triple[:, :, 2 * head_dim:].reshape(-1, head_dim).astype(jnp.float32)

        def span_attention(entry):
            query_rows, seen = entry
            scores = jnp.dot(query_rows, key_rows.T, preferred_element_type=jnp.float32) * scale_factor
            best_score = lax.optimization_barrier(jnp.max(jnp.where(seen[None, :], scores, -jnp.inf), axis=1, keepdims=True))
            weights = jnp.where(seen[None, :], jnp.exp(scores - best_score), 0.0)
            rounded = lax.optimization_barrier(weights.astype(jnp.bfloat16))
            numer = jnp.dot(rounded.astype(jnp.float32), value_rows, preferred_element_type=jnp.float32)
            return (numer / lax.optimization_barrier(jnp.sum(weights, axis=1, keepdims=True))).astype(jnp.bfloat16)
        return lax.map(span_attention, (queries, visible))
    attended = lax.map(head_attention, triples)
    filler = jnp.zeros((slot_count - HEADS, span_count, span_len, head_dim), jnp.bfloat16)
    padded = jnp.concatenate([attended, filler], axis=0)
    grouped = padded.reshape(N_SEQ, per_group, span_count, span_len, head_dim)
    group_weights = out_weight.reshape(N_SEQ, per_group, head_dim, model_width)

    def add_group(running, entry):
        group_heads, group_weight = entry
        partial_sum = jnp.einsum('hctd,hde->cte', group_heads.astype(jnp.float32), group_weight.astype(jnp.float32)).astype(jnp.bfloat16)
        partial_sum = lax.optimization_barrier(partial_sum)
        return (running + partial_sum.astype(jnp.float32), None)
    summed, _ = lax.scan(add_group, jnp.zeros((span_count, span_len, model_width), jnp.float32), (grouped, group_weights))
    block_out = (hidden.astype(jnp.float32) + mods[:, 2][:, None, :] * summed).astype(jnp.bfloat16)
    clean_index = jnp.sum(jnp.where(span_order == 0, jnp.arange(span_count, dtype=jnp.int32), 0)).astype(jnp.int32)
    clean_rows = lax.dynamic_index_in_dim(block_out, clean_index, 0, keepdims=False)
    latents = jnp.dot(clean_rows, latent_weight, preferred_element_type=jnp.float32).astype(jnp.bfloat16)
    row_patches = N_SEQ // FR
    col_patches = span_len // N_SEQ
    rotate = row_patches // 2
    blocks = jnp.roll(latents.reshape(N_SEQ, col_patches, P_SIZE * P_SIZE * C), -rotate, axis=0)
    height = row_patches * P_SIZE
    width_cols = col_patches * P_SIZE
    grid = blocks.reshape(FR, row_patches, col_patches, P_SIZE, P_SIZE, C).transpose(0, 1, 3, 2, 4, 5).reshape(FR, height, width_cols, C)
    padded_grid = jnp.pad(grid.astype(jnp.float32), ((2, 0), (1, 1), (1, 1), (0, 0)))
    out_channels = decoder_weight.shape[4]
    conv = jnp.zeros((FR, height, width_cols, out_channels), jnp.float32)
    for time_off in range(3):
        for row_off in range(3):
            for col_off in range(3):
                window = padded_grid[2 - time_off:2 - time_off + FR, row_off:row_off + height, col_off:col_off + width_cols]
                conv = conv + jnp.einsum('fywc,co->fywo', window, decoder_weight[time_off, row_off, col_off].astype(jnp.float32))
    ordered = conv.reshape(FR * row_patches, P_SIZE, width_cols, out_channels)
    decoded = jnp.roll(ordered, rotate, axis=0).astype(jnp.bfloat16)
    return (block_out, decoded)
```

```python
import functools
import math

import jax
import jax.numpy as jnp
from jax import lax
from jax.experimental import pallas as pl
from jax.experimental.pallas import tpu as pltpu
from jax.sharding import PartitionSpec as P

HEADS = 24
FR = 4
P_SIZE = 2
C = 16
HD = 128

EPSILON = 1e-06
NEG_LARGE = 1e30

NX, NH, NY, NZ, NC = 4, 2, 2, 8, 2
BLK = 32
QUARTER = NZ * BLK
TAIL = 16


def seq_at(y, z, c):
    return ((y % NY) * NZ + z % NZ) * NC + c % NC


def span_at(x, h):
    return (x % NX) * NH + h % NH


def seq_route(dy=0, dz=0, dc=0):
    return [
        (seq_at(y, z, c), seq_at(y + dy, z + dz, c + dc))
        for y in range(NY)
        for z in range(NZ)
        for c in range(NC)
    ]


def span_route(dx=0, dh=0):
    return [(span_at(x, h), span_at(x + dx, h + dh)) for x in range(NX) for h in range(NH)]


def move_z(a, d):
    return lax.ppermute(a, "seq", seq_route(dz=d))


def move_y(a):
    return lax.ppermute(a, "seq", seq_route(dy=1))


def move_core(a):
    return lax.ppermute(a, "seq", seq_route(dc=1))


def move_x(a, d):
    return lax.ppermute(a, "span", span_route(dx=d))


def move_hi(a):
    return lax.ppermute(a, "span", span_route(dh=1))


def normalize(rows, shift_row, scale_row):
    values = rows.astype(jnp.float32)
    center = values - jnp.mean(values, axis=-1, keepdims=True)
    spread = jnp.mean(center * center, axis=-1, keepdims=True)
    return (center * lax.rsqrt(spread + EPSILON) * (1.0 + scale_row) + shift_row).astype(
        jnp.bfloat16
    )


def gather_class(b):
    n = b.shape[0] // 2
    up1, dn1, y0 = move_z(b, 1), move_z(b, -1), move_y(b)
    up2, dn2 = move_z(up1, 1), move_z(dn1, -1)
    yu1, yd1 = move_y(up1), move_y(dn1)
    up3, dn3 = move_z(up2, 1), move_z(dn2, -1)
    yu2, yd2 = move_y(up2), move_y(dn2)
    f4a, f4b = move_z(up3[:n], 1), move_z(dn3[n:], -1)
    yu3, yd3 = move_z(yu2, 1), move_z(yd2, -1)
    y4a, y4b = move_z(yu3[:n], 1), move_z(yd3[n:], -1)
    mine = [b, dn1, dn2, dn3, f4a, f4b, up3, up2, up1]
    other = [y0, yd1, yd2, yd3, y4a, y4b, yu3, yu2, yu1]
    return jnp.concatenate(mine + other, axis=0)


def dot_t(a, b):
    return lax.dot_general(a, b, (((1,), (1,)), ((), ())), preferred_element_type=jnp.float32)


EXP_SCALE = math.log2(math.e) / math.sqrt(HD)


def self_kernel(q_ref, kv_ref, o_ref):
    s = dot_t(q_ref[...], kv_ref[:, :HD])
    m = jnp.max(s, axis=1, keepdims=True)
    p = jnp.exp2((s - m) * EXP_SCALE)
    total = jnp.sum(p, axis=1, keepdims=True)
    acc = jnp.dot(p.astype(jnp.bfloat16), kv_ref[:, HD:], preferred_element_type=jnp.float32)
    o_ref[...] = (acc / total).astype(jnp.bfloat16)


def self_attention(q, kv):
    rows = q.shape[0]
    return pl.pallas_call(
        self_kernel,
        grid=(rows // QUARTER,),
        in_specs=[
            pl.BlockSpec((QUARTER, HD), lambda i: (i, 0)),
            pl.BlockSpec(kv.shape, lambda i: (0, 0)),
        ],
        out_specs=pl.BlockSpec((QUARTER, HD), lambda i: (i, 0)),
        out_shape=jax.ShapeDtypeStruct((rows, HD), jnp.bfloat16),
        compiler_params=pltpu.CompilerParams(vmem_limit_bytes=32 * 2**20),
        name="self_attention",
    )(q, kv)


def main_kernel(s_ref, qa_ref, qb_ref, k0, k1, k2, k3a, k3b, o_ref, acc, m_s, l_s):
    r = pl.program_id(0)
    dh = r // 4
    q = jnp.where(dh == 0, qa_ref[...], qb_ref[...])
    acc[...] = jnp.zeros_like(acc)
    m_s[...] = jnp.full_like(m_s, -NEG_LARGE)
    l_s[...] = jnp.zeros_like(l_s)

    def update(refs):
        ss = [dot_t(q, ref[:, :HD]) for ref in refs]
        m_old = m_s[:, :1]
        m_new = m_old
        for s in ss:
            m_new = jnp.maximum(m_new, jnp.max(s, axis=1, keepdims=True))
        alpha = jnp.exp2((m_old - m_new) * EXP_SCALE)
        total = l_s[:, :1] * alpha
        out = acc[...] * alpha
        for s, ref in zip(ss, refs):
            p = jnp.exp2((s - m_new) * EXP_SCALE)
            total = total + jnp.sum(p, axis=1, keepdims=True)
            out = out + jnp.dot(
                p.astype(jnp.bfloat16), ref[:, HD:], preferred_element_type=jnp.float32
            )
        acc[...] = out
        m_s[...] = jnp.broadcast_to(m_new, m_s.shape)
        l_s[...] = jnp.broadcast_to(total, l_s.shape)

    for i, refs in enumerate(((k0,), (k1,), (k2,), (k3a, k3b))):
        pl.when(s_ref[dh * 4 + i] == 1)(functools.partial(update, refs))

    total = l_s[...]
    some = total > 0.0
    safe = jnp.where(some, total, 1.0)
    o_ref[0, :QUARTER, :] = (acc[...] / safe).astype(jnp.bfloat16)
    lse = jnp.where(some, m_s[...] * EXP_SCALE + jnp.log2(safe), -NEG_LARGE)
    row = lse.T[0:1, :]
    row = jnp.concatenate([row[:, :128], row[:, 128:]], axis=0)
    hi = row.astype(jnp.bfloat16).astype(jnp.float32)
    rest = row - hi
    mid = rest.astype(jnp.bfloat16).astype(jnp.float32)
    low = rest - mid
    pad = jnp.zeros((TAIL - 6, 128), jnp.float32)
    o_ref[0, QUARTER:, :] = jnp.concatenate([hi, mid, low, pad], axis=0).astype(jnp.bfloat16)


def main_attention(flags, place, qa, qb, blocks):
    scalars = jnp.concatenate([flags, place.reshape(1)])
    whole = [pl.BlockSpec(b.shape, lambda r, s: (0, 0)) for b in blocks]
    return pl.pallas_call(
        main_kernel,
        grid_spec=pltpu.PrefetchScalarGridSpec(
            num_scalar_prefetch=1,
            grid=(8,),
            in_specs=[
                pl.BlockSpec((QUARTER, HD), lambda r, s: (r % 4, 0)),
                pl.BlockSpec((QUARTER, HD), lambda r, s: (r % 4, 0)),
            ]
            + whole,
            out_specs=pl.BlockSpec((1, QUARTER + TAIL, HD), lambda r, s: (r ^ s[8], 0, 0)),
            scratch_shapes=[
                pltpu.VMEM((QUARTER, HD), jnp.float32),
                pltpu.VMEM((QUARTER, 128), jnp.float32),
                pltpu.VMEM((QUARTER, 128), jnp.float32),
            ],
        ),
        out_shape=jax.ShapeDtypeStruct((8, QUARTER + TAIL, HD), jnp.bfloat16),
        compiler_params=pltpu.CompilerParams(vmem_limit_bytes=32 * 2**20),
        name="main_attention",
    )(scalars, qa, qb, *blocks)


def join_kernel(s_ref, in_ref, a_ref):
    place = s_ref[0]
    z = s_ref[1]
    for r in range(4):
        parts = []
        for dh in range(2):
            at = (dh * 4 + r) ^ place
            rows = in_ref[at, QUARTER:, :].astype(jnp.float32)
            parts.append((at, rows[0:2] + rows[2:4] + rows[4:6]))
        top = jnp.maximum(parts[0][1], parts[1][1])
        e = [jnp.exp2(lse - top) for _, lse in parts]
        norm = e[0] + e[1]
        for half in range(2):
            out = None
            for (at, _), weight in zip(parts, e):
                w = (weight / norm)[half : half + 1, :]
                col = jnp.broadcast_to(w, (128, 128)).T
                term = in_ref[at, half * 128 : half * 128 + 128, :].astype(jnp.float32) * col
                out = term if out is None else out + term
            out = out.astype(jnp.bfloat16)
            slot = (r % 2) * 2 + r // 2
            for j in range(4):
                d = half * 4 + j
                start = pl.multiple_of(((z + d) % NZ) * BLK, BLK)
                a_ref[pl.ds(start, BLK), slot * HD : slot * HD + HD] = out[j * BLK : j * BLK + BLK]


def join_heads(place, z, received):
    return pl.pallas_call(
        join_kernel,
        grid_spec=pltpu.PrefetchScalarGridSpec(
            num_scalar_prefetch=1,
            grid=(1,),
            in_specs=[pl.BlockSpec(received.shape, lambda i, s: (0, 0, 0))],
            out_specs=pl.BlockSpec((QUARTER, 4 * HD), lambda i, s: (0, 0)),
        ),
        out_shape=jax.ShapeDtypeStruct((QUARTER, 4 * HD), jnp.bfloat16),
        name="join_heads",
    )(jnp.stack([place, z]), received)


def decode(latents, root_kernel):
    seq_count = latents.shape[0]
    row_patches = seq_count // FR
    me = lax.axis_index("seq")
    ringed = jnp.concatenate([latents[-1:], latents, latents[:1]], axis=0)
    position = (me - row_patches // 2 + seq_count) % seq_count
    patch_row = position % row_patches
    frame_index = position // row_patches
    row_ids = jnp.arange(P_SIZE + 2, dtype=jnp.int32)
    keep = jnp.where(
        row_ids == 0,
        patch_row > 0,
        jnp.where(row_ids == P_SIZE + 1, patch_row < row_patches - 1, True),
    )
    width_cols = BLK * P_SIZE
    windows = []
    for lag in range(3):
        start = (me - lag * row_patches + seq_count) % seq_count
        three = lax.dynamic_slice_in_dim(ringed, start, 3, axis=0)
        slab = (
            three.reshape(3, BLK, P_SIZE, P_SIZE, C)
            .transpose(0, 2, 1, 3, 4)
            .reshape(3 * P_SIZE, width_cols, C)
        )[P_SIZE - 1 : 2 * P_SIZE + 1]
        ok = keep & (frame_index >= lag)
        slab = jnp.where(ok[:, None, None], slab, jnp.zeros_like(slab))
        framed = jnp.pad(slab, ((0, 0), (1, 1), (0, 0)))
        for row_off in range(3):
            for col_off in range(3):
                windows.append(framed[row_off : row_off + P_SIZE, col_off : col_off + width_cols])
    stacked = jnp.concatenate(windows, axis=-1).reshape(P_SIZE * width_cols, 27 * C)
    decoded = jnp.dot(stacked, root_kernel, preferred_element_type=jnp.float32)
    return decoded.reshape(P_SIZE, width_cols, root_kernel.shape[1]).astype(jnp.bfloat16)[None]


def per_device(
    hidden, levels, span_order, modulation, in_weight, out_weight, latent_weight, decoder_weight
):
    span_me = lax.axis_index("span")
    seq_me = lax.axis_index("seq")
    x, h = span_me // NH, span_me % NH
    y, z, core = seq_me // (NZ * NC), (seq_me // NC) % NZ, seq_me % NC
    mod_row = lax.dynamic_index_in_dim(modulation, levels[0], 0, keepdims=False)
    shift_row, scale_row, gate_row = mod_row[0], mod_row[1], mod_row[2]

    w_own = in_weight[0]
    w_oth = move_core(w_own)
    out_w = jnp.where(seq_me < HEADS, out_weight[0], jnp.zeros_like(out_weight[0]))

    rows = gather_class(normalize(hidden[0], shift_row, scale_row))
    mine = jnp.dot(rows, w_own, preferred_element_type=jnp.float32).astype(jnp.bfloat16)
    theirs = jnp.dot(rows, w_oth, preferred_element_type=jnp.float32).astype(jnp.bfloat16)
    triples = jnp.concatenate([mine, move_core(theirs)], axis=0)
    q = triples[:, :HD]
    kv = triples[:, HD:]

    q_hi = move_hi(q)
    half = kv.shape[0] // 2
    kv_up, kv_dn = move_x(kv, 1), move_x(kv, -1)
    kv_2a, kv_2b = move_x(kv_up[:half], 1), move_x(kv_dn[half:], -1)

    pair = jnp.concatenate([out_w, move_core(out_w)], axis=0)
    far_pair = move_y(lax.optimization_barrier((pair, rows))[0])

    own = self_attention(q, kv)
    gated = out_w.astype(jnp.float32) * gate_row
    head_latent = jnp.dot(
        gated, latent_weight.astype(jnp.float32), precision=lax.Precision.HIGHEST
    )
    part = jnp.dot(own.astype(jnp.float32), head_latent, precision=lax.Precision.HIGHEST)
    pv = latent_weight.shape[1]
    part = part.astype(jnp.bfloat16).reshape(NC, NY, NZ, BLK, pv)
    part = jnp.where(core == 1, part[::-1], part)
    part = jnp.where(y == 1, part[:, ::-1], part)
    twice = jnp.concatenate([part, part], axis=2)
    part = lax.dynamic_slice_in_dim(twice, (NZ - z) % NZ, NZ, axis=2)
    part = part.transpose(1, 2, 0, 3, 4).reshape(NY * NZ * NC, BLK, pv)
    part = lax.all_to_all(part, "seq", 0, 0, tiled=True)
    latents = jnp.sum(part.astype(jnp.float32), axis=0) + jnp.dot(
        hidden[0], latent_weight, preferred_element_type=jnp.float32
    )
    latents = latents.astype(jnp.bfloat16)
    group_ids = jnp.arange(span_order.shape[0], dtype=jnp.int32)
    root = jnp.sum(jnp.where(span_order == 0, group_ids, 0))
    spread = lax.all_to_all(
        jnp.broadcast_to(latents[None], (NX * NH, BLK, pv)), "span", 0, 0, tiled=True
    )
    latents = lax.dynamic_index_in_dim(spread, root, 0, keepdims=True)
    every = lax.all_to_all(
        jnp.broadcast_to(latents, (NY * NZ * NC, BLK, pv)), "seq", 0, 0, tiled=True
    )
    decoded = decode(every, decoder_weight.reshape(27 * C, decoder_weight.shape[4]))

    order_of = lambda dx, dh: span_order[((x + dx) % NX) * NH + (h + dh) % NH]
    seen = [order_of(d, 0) for d in (0, -1, 1, 2)]
    flags = jnp.stack([(s <= order_of(0, dh)).astype(jnp.int32) for dh in range(2) for s in seen])
    place = h * 4 + core * 2 + y
    chunks = main_attention(flags, place, q, q_hi, (kv, kv_up, kv_dn, kv_2a, kv_2b))
    groups = [
        [
            span_at(i, hh) * (NY * NZ * NC) + seq_at(yy, j, cc)
            for hh in range(NH)
            for cc in range(NC)
            for yy in range(NY)
        ]
        for i in range(NX)
        for j in range(NZ)
    ]
    received = lax.all_to_all(
        chunks, ("span", "seq"), 0, 0, tiled=True, axis_index_groups=groups
    )
    heads = join_heads(place, z, received)
    partial = jnp.dot(heads[:, : 2 * HD], pair, preferred_element_type=jnp.float32) + jnp.dot(
        heads[:, 2 * HD :], far_pair, preferred_element_type=jnp.float32
    )
    z_groups = [[seq_at(yy, j, cc) for j in range(NZ)] for yy in range(NY) for cc in range(NC)]
    summed = lax.psum_scatter(
        partial.astype(jnp.bfloat16),
        "seq",
        scatter_dimension=0,
        tiled=True,
        axis_index_groups=z_groups,
    ).astype(jnp.float32)
    block_out = (hidden[0].astype(jnp.float32) + gate_row * summed).astype(jnp.bfloat16)[None]
    return (block_out, decoded)


def solution(mesh):
    placed = (
        P("span", "seq", None),
        P("span"),
        P(),
        P(),
        P("seq", None, None),
        P("seq", None, None),
        P(),
        P(None, None, None, None, "span"),
    )
    return jax.shard_map(
        per_device,
        mesh=mesh,
        in_specs=placed,
        out_specs=(P("span", "seq", None), P("seq", None, None, "span")),
        check_vma=False,
    )
```

```python
import functools
import math

import jax
import jax.numpy as jnp
from jax import lax
from jax.experimental import pallas as pl
from jax.experimental.pallas import tpu as pltpu
from jax.sharding import PartitionSpec as P

HEADS = 24
FR = 4
P_SIZE = 2
C = 16
HD = 128

EPSILON = 1e-06
NEG_LARGE = 1e30

NX, NH, NY, NZ, NC = 4, 2, 2, 8, 2
BLK = 32
QUARTER = NZ * BLK
TAIL = 16


def seq_at(y, z, c):
    return ((y % NY) * NZ + z % NZ) * NC + c % NC


def span_at(x, h):
    return (x % NX) * NH + h % NH


def seq_route(dy=0, dz=0, dc=0):
    return [
        (seq_at(y, z, c), seq_at(y + dy, z + dz, c + dc))
        for y in range(NY)
        for z in range(NZ)
        for c in range(NC)
    ]


def span_route(dx=0, dh=0):
    return [(span_at(x, h), span_at(x + dx, h + dh)) for x in range(NX) for h in range(NH)]


def move_z(a, d):
    return lax.ppermute(a, "seq", seq_route(dz=d))


def move_y(a):
    return lax.ppermute(a, "seq", seq_route(dy=1))


def move_core(a):
    return lax.ppermute(a, "seq", seq_route(dc=1))


def move_x(a, d):
    return lax.ppermute(a, "span", span_route(dx=d))


def move_hi(a):
    return lax.ppermute(a, "span", span_route(dh=1))


def gather_class(b):
    up1, dn1, y0 = move_z(b, 1), move_z(b, -1), move_y(b)
    up2, dn2 = move_z(up1, 1), move_z(dn1, -1)
    yu1, yd1 = move_y(up1), move_y(dn1)
    up3, dn3 = move_z(up2, 1), move_z(dn2, -1)
    yu2, yd2 = move_y(up2), move_y(dn2)
    far = move_z(up3, 1)
    yu3, yd3 = move_z(yu2, 1), move_z(yd2, -1)
    yfar = move_y(far)
    return (b, dn1, dn2, dn3, far, up3, up2, up1), (y0, yd1, yd2, yd3, yfar, yu3, yu2, yu1)


VMEM_LIMIT = 40 * 2**20
EXP_SCALE = math.log2(math.e) / math.sqrt(HD)


def norm_kernel(level_ref, hidden_ref, mod_ref, out_ref, gate_ref):
    values = hidden_ref[...].astype(jnp.float32)
    center = values - jnp.mean(values, axis=-1, keepdims=True)
    spread = jnp.mean(center * center, axis=-1, keepdims=True)
    scaled = center * lax.rsqrt(spread + EPSILON)
    out_ref[...] = (scaled * (1.0 + mod_ref[0, 1:2, :]) + mod_ref[0, 0:1, :]).astype(jnp.bfloat16)
    gate_ref[...] = mod_ref[0, 2:3, :]


def normalize(levels, rows, modulation):
    width = rows.shape[1]
    return pl.pallas_call(
        norm_kernel,
        grid_spec=pltpu.PrefetchScalarGridSpec(
            num_scalar_prefetch=1,
            grid=(1,),
            in_specs=[
                pl.BlockSpec(rows.shape, lambda i, s: (0, 0)),
                pl.BlockSpec((1, 3, width), lambda i, s: (s[0], 0, 0)),
            ],
            out_specs=[
                pl.BlockSpec(rows.shape, lambda i, s: (0, 0)),
                pl.BlockSpec((1, width), lambda i, s: (0, 0)),
            ],
        ),
        out_shape=[
            jax.ShapeDtypeStruct(rows.shape, jnp.bfloat16),
            jax.ShapeDtypeStruct((1, width), jnp.float32),
        ],
        name="normalize",
    )(levels, rows, modulation)


def project_kernel(*refs):
    blocks, (own_ref, oth_ref, mine_ref, theirs_ref, rows) = refs[:NZ], refs[NZ:]
    for i, block in enumerate(blocks):
        rows[i * BLK : i * BLK + BLK, :] = block[...]
    for w_ref, o_ref in ((oth_ref, theirs_ref), (own_ref, mine_ref)):
        out = jnp.dot(rows[...], w_ref[...], preferred_element_type=jnp.float32)
        o_ref[:, :HD] = (out[:, :HD] * EXP_SCALE).astype(jnp.bfloat16)
        o_ref[:, HD:] = out[:, HD:].astype(jnp.bfloat16)


def project(blocks, w_own, w_oth):
    width, cols = w_own.shape
    rows = len(blocks) * BLK
    vmem = pl.BlockSpec(memory_space=pltpu.VMEM)
    return pl.pallas_call(
        project_kernel,
        in_specs=[vmem] * (len(blocks) + 2),
        out_specs=[vmem, vmem],
        out_shape=[jax.ShapeDtypeStruct((rows, cols), jnp.bfloat16)] * 2,
        scratch_shapes=[pltpu.VMEM((rows, width), jnp.bfloat16)],
        compiler_params=pltpu.CompilerParams(vmem_limit_bytes=VMEM_LIMIT),
        cost_estimate=pl.CostEstimate(
            flops=4 * rows * width * cols,
            bytes_accessed=4 * width * cols + 2 * rows * width,
            transcendentals=0,
        ),
        name="project",
    )(*blocks, w_own, w_oth)


def dot_t(a, b):
    return lax.dot_general(a, b, (((1,), (1,)), ((), ())), preferred_element_type=jnp.float32)


TILE = 128


def self_kernel(s_ref, q_ref, kv_ref, hi_ref, lo_ref, o_ref, values):
    y, z, core = s_ref[1], s_ref[2], s_ref[3]
    values[:, :HD] = kv_ref[:, HD:]
    values[:, HD:] = jnp.ones((values.shape[0], HD), jnp.bfloat16)
    for t in range(q_ref.shape[0] // TILE):
        s = dot_t(q_ref[t * TILE : t * TILE + TILE, :], kv_ref[:, :HD])
        p = jnp.exp2(s - jnp.max(s, axis=1, keepdims=True)).astype(jnp.bfloat16)
        acc = jnp.dot(p, values[...], preferred_element_type=jnp.float32)
        att = (acc[:, :HD] / acc[:, HD:]).astype(jnp.bfloat16)
        part = jnp.dot(att, hi_ref[...], preferred_element_type=jnp.float32) + jnp.dot(
            att, lo_ref[...], preferred_element_type=jnp.float32
        )
        part = part.astype(jnp.bfloat16)
        for j in range(TILE // BLK):
            i = t * (TILE // BLK) + j
            d, quarter = i % NZ, i // NZ
            at = ((y ^ (quarter // 2)) * NZ + (z + d) % NZ) * NC + (core ^ (quarter % 2))
            o_ref[at] = part[j * BLK : j * BLK + BLK]


def self_attention(place, q, kv, hi, lo):
    pv = hi.shape[1]
    rows = q.shape[0]
    return pl.pallas_call(
        self_kernel,
        grid_spec=pltpu.PrefetchScalarGridSpec(
            num_scalar_prefetch=1,
            grid=(1,),
            in_specs=[pl.BlockSpec(a.shape, lambda i, s: (0, 0)) for a in (q, kv, hi, lo)],
            out_specs=pl.BlockSpec((rows // BLK, BLK, pv), lambda i, s: (0, 0, 0)),
            scratch_shapes=[pltpu.VMEM((rows, 2 * HD), jnp.bfloat16)],
        ),
        out_shape=jax.ShapeDtypeStruct((rows // BLK, BLK, pv), jnp.bfloat16),
        compiler_params=pltpu.CompilerParams(vmem_limit_bytes=VMEM_LIMIT),
        cost_estimate=pl.CostEstimate(
            flops=6 * rows * rows * HD, bytes_accessed=2**20, transcendentals=rows * rows
        ),
        name="self_attention",
    )(place, q, kv, hi, lo)


def visit(refs, q, keys, values, acc, top):
    at = 0
    for ref in refs:
        n = ref.shape[0]
        keys[at : at + n, :] = ref[:, :HD]
        values[at : at + n, :HD] = ref[:, HD:]
        at += n
    for t in range(q.shape[0] // TILE):
        rows = slice(t * TILE, t * TILE + TILE)
        s = dot_t(q[rows, :], keys[...])
        old = top[rows, :1]
        new = jnp.maximum(old, jnp.max(s, axis=1, keepdims=True))
        p = jnp.exp2(s - new).astype(jnp.bfloat16)
        acc[rows, :] = acc[rows, :] * jnp.exp2(old - new) + jnp.dot(
            p, values[...], preferred_element_type=jnp.float32
        )
        top[rows, :] = jnp.broadcast_to(new, (TILE, 128))


def sees(order_ref, s_ref, dh, dx):
    x, h = s_ref[4], s_ref[0]
    mine = order_ref[x * NH + (h ^ dh)]
    return order_ref[((x + dx) % NX) * NH + h] <= mine


def near_kernel(counts, order_ref, s_ref, qa_ref, qb_ref, *refs):
    blocks, (acc_ref, top_ref, q, keys, values) = refs[: sum(counts)], refs[sum(counts) :]
    dh = pl.program_id(0)
    q[...] = jnp.where(dh == 0, qa_ref[...], qb_ref[...])
    values[:, HD:] = jnp.ones((values.shape[0], HD), jnp.bfloat16)
    acc_ref[...] = jnp.zeros_like(acc_ref)
    top_ref[...] = jnp.full_like(top_ref, -NEG_LARGE)
    at = 0
    for count, dx in zip(counts, (0, NX - 1, 1)):
        unit = blocks[at : at + count]
        at += count
        pl.when(sees(order_ref, s_ref, dh, dx))(
            functools.partial(visit, unit, q, keys, values, acc_ref.at[0], top_ref.at[0])
        )


def far_kernel(order_ref, s_ref, qa_ref, qb_ref, acc_in, top_in, *refs):
    blocks, (o_ref, q, keys, values, acc, top) = refs[:-6], refs[-6:]
    dh = pl.program_id(0)
    q[...] = jnp.where(dh == 0, qa_ref[...], qb_ref[...])
    values[:, HD:] = jnp.ones((values.shape[0], HD), jnp.bfloat16)
    acc[...] = acc_in[0]
    top[...] = top_in[0]
    pl.when(sees(order_ref, s_ref, dh, 2))(
        functools.partial(visit, blocks, q, keys, values, acc, top)
    )
    y, core = s_ref[1], s_ref[3]
    for quarter in range(4):
        rows = slice(quarter * QUARTER, quarter * QUARTER + QUARTER)
        total = acc[rows, HD:]
        some = total > 0.0
        safe = jnp.where(some, total, 1.0)
        at = quarter ^ (y * 2 + core)
        o_ref[at, :QUARTER, :] = (acc[rows, :HD] / safe).astype(jnp.bfloat16)
        lse = jnp.where(some, top[rows, :] + jnp.log2(safe), -NEG_LARGE)
        row = lse.T[0:1, :]
        row = jnp.concatenate([row[:, :128], row[:, 128:]], axis=0)
        hi = row.astype(jnp.bfloat16).astype(jnp.float32)
        rest = row - hi
        mid = rest.astype(jnp.bfloat16).astype(jnp.float32)
        pad = jnp.zeros((TAIL - 6, 128), jnp.float32)
        o_ref[at, QUARTER:, :] = jnp.concatenate([hi, mid, rest - mid, pad], axis=0).astype(
            jnp.bfloat16
        )


def whole(a):
    return pl.BlockSpec(a.shape, lambda i, *s: (0,) * a.ndim)


def attention_cost(units, rows):
    pairs = 2 * units * rows * rows
    return pl.CostEstimate(flops=6 * pairs * HD, bytes_accessed=4 * 2**20, transcendentals=pairs)


def near_attention(order, place, qa, qb, units):
    rows = qa.shape[0]
    blocks = [b for unit in units for b in unit]
    out = lambda cols: pl.BlockSpec((1, rows, cols), lambda i, *s: (i, 0, 0))
    return pl.pallas_call(
        functools.partial(near_kernel, [len(unit) for unit in units]),
        grid_spec=pltpu.PrefetchScalarGridSpec(
            num_scalar_prefetch=2,
            grid=(NH,),
            in_specs=[whole(a) for a in (qa, qb, *blocks)],
            out_specs=[out(2 * HD), out(128)],
            scratch_shapes=[
                pltpu.VMEM((rows, HD), jnp.bfloat16),
                pltpu.VMEM((rows, HD), jnp.bfloat16),
                pltpu.VMEM((rows, 2 * HD), jnp.bfloat16),
            ],
        ),
        out_shape=[
            jax.ShapeDtypeStruct((NH, rows, 2 * HD), jnp.float32),
            jax.ShapeDtypeStruct((NH, rows, 128), jnp.float32),
        ],
        compiler_params=pltpu.CompilerParams(vmem_limit_bytes=VMEM_LIMIT),
        cost_estimate=attention_cost(3, rows),
        name="near_attention",
    )(order, place, qa, qb, *blocks)


def far_attention(order, place, qa, qb, acc, top, blocks):
    rows = qa.shape[0]
    chunk = QUARTER + TAIL
    part = lambda a: pl.BlockSpec((1,) + a.shape[1:], lambda i, *s: (i, 0, 0))
    return pl.pallas_call(
        far_kernel,
        grid_spec=pltpu.PrefetchScalarGridSpec(
            num_scalar_prefetch=2,
            grid=(NH,),
            in_specs=[whole(qa), whole(qb), part(acc), part(top)] + [whole(b) for b in blocks],
            out_specs=pl.BlockSpec((4, chunk, HD), lambda i, o, s: (i ^ s[0], 0, 0)),
            scratch_shapes=[
                pltpu.VMEM((rows, HD), jnp.bfloat16),
                pltpu.VMEM((rows, HD), jnp.bfloat16),
                pltpu.VMEM((rows, 2 * HD), jnp.bfloat16),
                pltpu.VMEM((rows, 2 * HD), jnp.float32),
                pltpu.VMEM((rows, 128), jnp.float32),
            ],
        ),
        out_shape=jax.ShapeDtypeStruct((NH * 4, chunk, HD), jnp.bfloat16),
        compiler_params=pltpu.CompilerParams(vmem_limit_bytes=VMEM_LIMIT),
        cost_estimate=attention_cost(1, rows),
        name="far_attention",
    )(order, place, qa, qb, acc, top, *blocks)


def join_kernel(s_ref, in_ref, near_ref, far_ref, o_ref, a_ref):
    h, y, z, core = s_ref[0], s_ref[1], s_ref[2], s_ref[3]
    place = h * 4 + y * 2 + core

    @pl.when(pl.program_id(0) == 0)
    def _():
        for r in range(4):
            parts = []
            for dh in range(NH):
                at = (dh * 4 + r) ^ place
                rows = in_ref[at, QUARTER:, :].astype(jnp.float32)
                parts.append((at, rows[0:2] + rows[2:4] + rows[4:6]))
            top = jnp.maximum(parts[0][1], parts[1][1])
            e = [jnp.exp2(lse - top) for _, lse in parts]
            norm = e[0] + e[1]
            for half in range(2):
                out = None
                for (at, _), weight in zip(parts, e):
                    w = (weight / norm)[half : half + 1, :]
                    col = jnp.broadcast_to(w, (128, 128)).T
                    term = in_ref[at, half * 128 : half * 128 + 128, :].astype(jnp.float32) * col
                    out = term if out is None else out + term
                out = out.astype(jnp.bfloat16)
                for j in range(4):
                    start = pl.multiple_of(((z + half * 4 + j) % NZ) * BLK, BLK)
                    a_ref[pl.ds(start, BLK), r * HD : r * HD + HD] = out[j * BLK : j * BLK + BLK]

    o_ref[...] = (
        jnp.dot(a_ref[:, : 2 * HD], near_ref[...], preferred_element_type=jnp.float32)
        + jnp.dot(a_ref[:, 2 * HD :], far_ref[...], preferred_element_type=jnp.float32)
    ).astype(jnp.bfloat16)


def join_heads(place, received, near, far):
    width = near.shape[1]
    step = width // 4
    cut = pl.BlockSpec((2 * HD, step), lambda i, s: (0, i))
    return pl.pallas_call(
        join_kernel,
        grid_spec=pltpu.PrefetchScalarGridSpec(
            num_scalar_prefetch=1,
            grid=(4,),
            in_specs=[whole(received), cut, cut],
            out_specs=pl.BlockSpec((QUARTER, step), lambda i, s: (0, i)),
            scratch_shapes=[pltpu.VMEM((QUARTER, 4 * HD), jnp.bfloat16)],
        ),
        out_shape=jax.ShapeDtypeStruct((QUARTER, width), jnp.bfloat16),
        compiler_params=pltpu.CompilerParams(vmem_limit_bytes=VMEM_LIMIT),
        name="join_heads",
    )(place, received, near, far)


def decode(latents, root_kernel):
    seq_count = latents.shape[0]
    row_patches = seq_count // FR
    me = lax.axis_index("seq")
    ringed = jnp.concatenate([latents[-1:], latents, latents[:1]], axis=0)
    position = (me - row_patches // 2 + seq_count) % seq_count
    patch_row = position % row_patches
    frame_index = position // row_patches
    row_ids = jnp.arange(P_SIZE + 2, dtype=jnp.int32)
    keep = jnp.where(
        row_ids == 0,
        patch_row > 0,
        jnp.where(row_ids == P_SIZE + 1, patch_row < row_patches - 1, True),
    )
    width_cols = BLK * P_SIZE
    windows = []
    for lag in range(3):
        start = (me - lag * row_patches + seq_count) % seq_count
        three = lax.dynamic_slice_in_dim(ringed, start, 3, axis=0)
        slab = (
            three.reshape(3, BLK, P_SIZE, P_SIZE, C)
            .transpose(0, 2, 1, 3, 4)
            .reshape(3 * P_SIZE, width_cols, C)
        )[P_SIZE - 1 : 2 * P_SIZE + 1]
        ok = keep & (frame_index >= lag)
        slab = jnp.where(ok[:, None, None], slab, jnp.zeros_like(slab))
        framed = jnp.pad(slab, ((0, 0), (1, 1), (0, 0)))
        for row_off in range(3):
            for col_off in range(3):
                windows.append(framed[row_off : row_off + P_SIZE, col_off : col_off + width_cols])
    stacked = jnp.concatenate(windows, axis=-1).reshape(P_SIZE * width_cols, 27 * C)
    decoded = jnp.dot(stacked, root_kernel, preferred_element_type=jnp.float32)
    return decoded.reshape(P_SIZE, width_cols, root_kernel.shape[1]).astype(jnp.bfloat16)[None]


def per_device(
    hidden, levels, span_order, modulation, in_weight, out_weight, latent_weight, decoder_weight
):
    span_me = lax.axis_index("span")
    seq_me = lax.axis_index("seq")
    x, h = span_me // NH, span_me % NH
    y, z, core = seq_me // (NZ * NC), (seq_me // NC) % NZ, seq_me % NC
    place = jnp.stack([h, y, z, core, x])
    pv = latent_weight.shape[1]
    seq_count = NY * NZ * NC

    normed, gate_row = normalize(levels, hidden[0], modulation)
    w_own = in_weight[0]
    own_blocks, other_blocks = gather_class(normed)
    w_oth = move_core(w_own)
    out_w = jnp.where(seq_me < HEADS, out_weight[0], jnp.zeros_like(out_weight[0]))
    pair = jnp.concatenate([out_w, move_core(out_w)], axis=0)
    head_latent = jnp.dot(
        out_w.astype(jnp.float32) * gate_row,
        latent_weight.astype(jnp.float32),
        precision=lax.Precision.HIGH,
    )
    latent_hi = head_latent.astype(jnp.bfloat16)
    latent_lo = (head_latent - latent_hi.astype(jnp.float32)).astype(jnp.bfloat16)
    own_latents = jnp.dot(hidden[0], latent_weight, preferred_element_type=jnp.float32)

    mine_a, theirs_a = project(own_blocks, w_own, w_oth)
    mine_b, theirs_b = project(other_blocks, w_own, w_oth)
    triples = jnp.concatenate([mine_a, move_core(theirs_a), mine_b, move_core(theirs_b)], axis=0)
    q = triples[:, :HD]
    kv = triples[:, HD:]

    half = kv.shape[0] // 2
    kv_up, kv_dn = move_x(kv, 1), move_x(kv, -1)
    q_hi = move_hi(q)
    kv_far = (move_x(kv_up[:half], 1), move_x(kv_dn[half:], -1))

    far_pair = move_y(lax.optimization_barrier((pair, other_blocks[4]))[0])

    part = self_attention(place, q, kv, latent_hi, latent_lo)
    q_hi, part = lax.optimization_barrier((q_hi, part))
    acc, top = near_attention(span_order, place, q, q_hi, ((kv,), (kv_up,), (kv_dn,)))
    part = lax.all_to_all(part, "seq", 0, 0, tiled=True)
    acc, part = lax.optimization_barrier((acc, part))
    chunks = far_attention(span_order, place, q, q_hi, acc, top, kv_far)
    groups = [
        [
            span_at(i, hh) * seq_count + seq_at(yy, j, cc)
            for hh in range(NH)
            for yy in range(NY)
            for cc in range(NC)
        ]
        for i in range(NX)
        for j in range(NZ)
    ]
    received = lax.all_to_all(
        chunks, ("span", "seq"), 0, 0, tiled=True, axis_index_groups=groups
    )
    partial = join_heads(place, received, pair, far_pair)
    z_groups = [[seq_at(yy, j, cc) for j in range(NZ)] for yy in range(NY) for cc in range(NC)]
    summed = lax.psum_scatter(
        partial, "seq", scatter_dimension=0, tiled=True, axis_index_groups=z_groups
    ).astype(jnp.float32)
    block_out = (hidden[0].astype(jnp.float32) + gate_row * summed).astype(jnp.bfloat16)[None]

    latents = (jnp.sum(part.astype(jnp.float32), axis=0) + own_latents).astype(jnp.bfloat16)
    group_ids = jnp.arange(span_order.shape[0], dtype=jnp.int32)
    root = jnp.sum(jnp.where(span_order == 0, group_ids, 0))
    spread = lax.all_to_all(
        jnp.broadcast_to(latents[None], (NX * NH, BLK, pv)), "span", 0, 0, tiled=True
    )
    latents = lax.dynamic_index_in_dim(spread, root, 0, keepdims=True)
    every = lax.all_to_all(
        jnp.broadcast_to(latents, (seq_count, BLK, pv)), "seq", 0, 0, tiled=True
    )
    decoded = decode(every, decoder_weight.reshape(27 * C, decoder_weight.shape[4]))
    return (block_out, decoded)


def solution(mesh):
    placed = (
        P("span", "seq", None),
        P("span"),
        P(),
        P(),
        P("seq", None, None),
        P("seq", None, None),
        P(),
        P(None, None, None, None, "span"),
    )
    return jax.shard_map(
        per_device,
        mesh=mesh,
        in_specs=placed,
        out_specs=(P("span", "seq", None), P("seq", None, None, "span")),
        check_vma=False,
    )
```

```python
import functools
import math

import jax
import jax.numpy as jnp
from jax import lax
from jax.experimental import pallas as pl
from jax.experimental.pallas import tpu as pltpu
from jax.sharding import PartitionSpec as P

HEADS = 24
FR = 4
P_SIZE = 2
C = 16
HD = 128

EPSILON = 1e-06
NEG_LARGE = 1e30

NX, NH, NY, NZ, NC = 4, 2, 2, 8, 2
BLK = 32
QUARTER = NZ * BLK
TAIL = 16


def seq_at(y, z, c):
    return ((y % NY) * NZ + z % NZ) * NC + c % NC


def span_at(x, h):
    return (x % NX) * NH + h % NH


def seq_route(dy=0, dz=0, dc=0):
    return [
        (seq_at(y, z, c), seq_at(y + dy, z + dz, c + dc))
        for y in range(NY)
        for z in range(NZ)
        for c in range(NC)
    ]


def span_route(dx=0, dh=0):
    return [(span_at(x, h), span_at(x + dx, h + dh)) for x in range(NX) for h in range(NH)]


def move_z(a, d):
    return lax.ppermute(a, "seq", seq_route(dz=d))


def move_y(a):
    return lax.ppermute(a, "seq", seq_route(dy=1))


def move_core(a):
    return lax.ppermute(a, "seq", seq_route(dc=1))


def move_x(a, d):
    return lax.ppermute(a, "span", span_route(dx=d))


def move_hi(a):
    return lax.ppermute(a, "span", span_route(dh=1))


def gather_class(b):
    up1, dn1, y0 = move_z(b, 1), move_z(b, -1), move_y(b)
    up2, dn2 = move_z(up1, 1), move_z(dn1, -1)
    yu1, yd1 = move_y(up1), move_y(dn1)
    up3, dn3 = move_z(up2, 1), move_z(dn2, -1)
    yu2, yd2 = move_y(up2), move_y(dn2)
    far = move_z(up3, 1)
    yu3, yd3 = move_z(yu2, 1), move_z(yd2, -1)
    yfar = move_y(far)
    return (b, dn1, dn2, dn3, far, up3, up2, up1), (y0, yd1, yd2, yd3, yfar, yu3, yu2, yu1)


VMEM_LIMIT = 40 * 2**20
EXP_SCALE = math.log2(math.e) / math.sqrt(HD)


def norm_kernel(level_ref, hidden_ref, mod_ref, out_ref, gate_ref):
    values = hidden_ref[...].astype(jnp.float32)
    row = pl.ds(level_ref[0] % MOD_ROWS, 1)
    center = values - jnp.mean(values, axis=-1, keepdims=True)
    spread = jnp.mean(center * center, axis=-1, keepdims=True)
    scaled = center * lax.rsqrt(spread + EPSILON)
    out_ref[...] = (scaled * (1.0 + mod_ref[1, row, :]) + mod_ref[0, row, :]).astype(jnp.bfloat16)
    gate_ref[...] = mod_ref[2, row, :]


MOD_ROWS = 8


def normalize(levels, rows, modulation):
    width = rows.shape[1]
    return pl.pallas_call(
        norm_kernel,
        grid_spec=pltpu.PrefetchScalarGridSpec(
            num_scalar_prefetch=1,
            grid=(1,),
            in_specs=[
                pl.BlockSpec(rows.shape, lambda i, s: (0, 0)),
                pl.BlockSpec((3, MOD_ROWS, width), lambda i, s: (0, s[0] // MOD_ROWS, 0)),
            ],
            out_specs=[
                pl.BlockSpec(rows.shape, lambda i, s: (0, 0)),
                pl.BlockSpec((1, width), lambda i, s: (0, 0)),
            ],
        ),
        out_shape=[
            jax.ShapeDtypeStruct(rows.shape, jnp.bfloat16),
            jax.ShapeDtypeStruct((1, width), jnp.float32),
        ],
        name="normalize",
    )(levels, rows, modulation.transpose(1, 0, 2))


def latent_kernel(w_ref, gate_ref, lw_ref, o_ref):
    gated = w_ref[...].astype(jnp.float32) * gate_ref[...]
    hi = gated.astype(jnp.bfloat16)
    lo = (gated - hi.astype(jnp.float32)).astype(jnp.bfloat16)
    out = dot_t(hi, lw_ref[...]) + dot_t(lo, lw_ref[...])
    top = out.astype(jnp.bfloat16)
    pv = out.shape[1]
    o_ref[:, :pv] = top
    o_ref[:, pv:] = (out - top.astype(jnp.float32)).astype(jnp.bfloat16)


def latent_matrix(w, gate_row, latent_weight):
    pv = latent_weight.shape[1]
    return pl.pallas_call(
        latent_kernel,
        out_shape=jax.ShapeDtypeStruct((w.shape[0], 2 * pv), jnp.bfloat16),
        compiler_params=pltpu.CompilerParams(vmem_limit_bytes=VMEM_LIMIT),
        name="latent_matrix",
    )(w, gate_row, latent_weight.T)


def project_kernel(*refs):
    blocks, (own_ref, oth_ref, mine_ref, theirs_ref, rows) = refs[:NZ], refs[NZ:]
    for i, block in enumerate(blocks):
        rows[i * BLK : i * BLK + BLK, :] = block[...]
    for w_ref, o_ref in ((oth_ref, theirs_ref), (own_ref, mine_ref)):
        out = jnp.dot(rows[...], w_ref[...], preferred_element_type=jnp.float32)
        o_ref[:, :HD] = (out[:, :HD] * EXP_SCALE).astype(jnp.bfloat16)
        o_ref[:, HD:] = out[:, HD:].astype(jnp.bfloat16)


def project(blocks, w_own, w_oth):
    width, cols = w_own.shape
    rows = len(blocks) * BLK
    vmem = pl.BlockSpec(memory_space=pltpu.VMEM)
    return pl.pallas_call(
        project_kernel,
        in_specs=[vmem] * (len(blocks) + 2),
        out_specs=[vmem, vmem],
        out_shape=[jax.ShapeDtypeStruct((rows, cols), jnp.bfloat16)] * 2,
        scratch_shapes=[pltpu.VMEM((rows, width), jnp.bfloat16)],
        compiler_params=pltpu.CompilerParams(vmem_limit_bytes=VMEM_LIMIT),
        cost_estimate=pl.CostEstimate(
            flops=4 * rows * width * cols,
            bytes_accessed=4 * width * cols + 2 * rows * width,
            transcendentals=0,
        ),
        name="project",
    )(*blocks, w_own, w_oth)


def dot_t(a, b):
    return lax.dot_general(a, b, (((1,), (1,)), ((), ())), preferred_element_type=jnp.float32)


TILE = 128


def used_slots(y, z):
    return (y * NZ + z) * NC < HEADS


def self_kernel(s_ref, q_ref, kv_ref, m_ref, o_ref, values):
    y, z, core = s_ref[1], s_ref[2], s_ref[3]
    used = used_slots(y, z)
    pv = o_ref.shape[2]
    values[:, :HD] = kv_ref[:, HD:]
    values[:, HD:] = jnp.ones((values.shape[0], HD), jnp.bfloat16)
    for t in range(q_ref.shape[0] // TILE):
        s = dot_t(q_ref[t * TILE : t * TILE + TILE, :], kv_ref[:, :HD])
        p = jnp.exp2(s - jnp.max(s, axis=1, keepdims=True)).astype(jnp.bfloat16)
        acc = jnp.dot(p, values[...], preferred_element_type=jnp.float32)
        att = (acc[:, :HD] / acc[:, HD:]).astype(jnp.bfloat16)
        part = jnp.dot(att, m_ref[...], preferred_element_type=jnp.float32)
        part = jnp.where(used, part[:, :pv] + part[:, pv:], 0.0).astype(jnp.bfloat16)
        for j in range(TILE // BLK):
            i = t * (TILE // BLK) + j
            d, quarter = i % NZ, i // NZ
            at = ((y ^ (quarter // 2)) * NZ + (z + d) % NZ) * NC + (core ^ (quarter % 2))
            o_ref[at] = part[j * BLK : j * BLK + BLK]


def self_attention(place, q, kv, matrix):
    pv = matrix.shape[1] // 2
    rows = q.shape[0]
    return pl.pallas_call(
        self_kernel,
        grid_spec=pltpu.PrefetchScalarGridSpec(
            num_scalar_prefetch=1,
            grid=(1,),
            in_specs=[pl.BlockSpec(a.shape, lambda i, s: (0, 0)) for a in (q, kv, matrix)],
            out_specs=pl.BlockSpec((rows // BLK, BLK, pv), lambda i, s: (0, 0, 0)),
            scratch_shapes=[pltpu.VMEM((rows, 2 * HD), jnp.bfloat16)],
        ),
        out_shape=jax.ShapeDtypeStruct((rows // BLK, BLK, pv), jnp.bfloat16),
        compiler_params=pltpu.CompilerParams(vmem_limit_bytes=VMEM_LIMIT),
        cost_estimate=pl.CostEstimate(
            flops=6 * rows * rows * HD, bytes_accessed=2**20, transcendentals=rows * rows
        ),
        name="self_attention",
    )(place, q, kv, matrix)


def visit(refs, q, keys, values, acc, top):
    at = 0
    for ref in refs:
        n = ref.shape[0]
        keys[at : at + n, :] = ref[:, :HD]
        values[at : at + n, :HD] = ref[:, HD:]
        at += n
    for t in range(q.shape[0] // TILE):
        rows = slice(t * TILE, t * TILE + TILE)
        s = dot_t(q[rows, :], keys[...])
        old = top[rows, :1]
        new = jnp.maximum(old, jnp.max(s, axis=1, keepdims=True))
        p = jnp.exp2(s - new).astype(jnp.bfloat16)
        acc[rows, :] = acc[rows, :] * jnp.exp2(old - new) + jnp.dot(
            p, values[...], preferred_element_type=jnp.float32
        )
        top[rows, :] = jnp.broadcast_to(new, (TILE, 128))


def sees(order_ref, s_ref, dh, dx):
    x, h = s_ref[4], s_ref[0]
    mine = order_ref[x * NH + (h ^ dh)]
    return order_ref[((x + dx) % NX) * NH + h] <= mine


def near_kernel(counts, order_ref, s_ref, qa_ref, qb_ref, *refs):
    blocks, (acc_ref, top_ref, q, keys, values) = refs[: sum(counts)], refs[sum(counts) :]
    dh = pl.program_id(0)
    q[...] = jnp.where(dh == 0, qa_ref[...], qb_ref[...])
    values[:, HD:] = jnp.ones((values.shape[0], HD), jnp.bfloat16)
    acc_ref[...] = jnp.zeros_like(acc_ref)
    top_ref[...] = jnp.full_like(top_ref, -NEG_LARGE)
    at = 0
    for count, dx in zip(counts, (0, NX - 1, 1)):
        unit = blocks[at : at + count]
        at += count
        pl.when(sees(order_ref, s_ref, dh, dx))(
            functools.partial(visit, unit, q, keys, values, acc_ref.at[0], top_ref.at[0])
        )


def far_kernel(order_ref, s_ref, qa_ref, qb_ref, acc_in, top_in, *refs):
    blocks, (o_ref, q, keys, values, acc, top) = refs[:-6], refs[-6:]
    dh = pl.program_id(0)
    q[...] = jnp.where(dh == 0, qa_ref[...], qb_ref[...])
    values[:, HD:] = jnp.ones((values.shape[0], HD), jnp.bfloat16)
    acc[...] = acc_in[0]
    top[...] = top_in[0]
    pl.when(sees(order_ref, s_ref, dh, 2))(
        functools.partial(visit, blocks, q, keys, values, acc, top)
    )
    y, core = s_ref[1], s_ref[3]
    for quarter in range(4):
        rows = slice(quarter * QUARTER, quarter * QUARTER + QUARTER)
        total = acc[rows, HD:]
        some = total > 0.0
        safe = jnp.where(some, total, 1.0)
        at = quarter ^ (y * 2 + core)
        o_ref[at, :QUARTER, :] = (acc[rows, :HD] / safe).astype(jnp.bfloat16)
        lse = jnp.where(some, top[rows, :] + jnp.log2(safe), -NEG_LARGE)
        row = lse.T[0:1, :]
        row = jnp.concatenate([row[:, :128], row[:, 128:]], axis=0)
        hi = row.astype(jnp.bfloat16).astype(jnp.float32)
        rest = row - hi
        mid = rest.astype(jnp.bfloat16).astype(jnp.float32)
        pad = jnp.zeros((TAIL - 6, 128), jnp.float32)
        o_ref[at, QUARTER:, :] = jnp.concatenate([hi, mid, rest - mid, pad], axis=0).astype(
            jnp.bfloat16
        )


def whole(a):
    return pl.BlockSpec(a.shape, lambda i, *s: (0,) * a.ndim)


def attention_cost(units, rows):
    pairs = 2 * units * rows * rows
    return pl.CostEstimate(flops=6 * pairs * HD, bytes_accessed=4 * 2**20, transcendentals=pairs)


def near_attention(order, place, qa, qb, units):
    rows = qa.shape[0]
    blocks = [b for unit in units for b in unit]
    out = lambda cols: pl.BlockSpec((1, rows, cols), lambda i, *s: (i, 0, 0))
    return pl.pallas_call(
        functools.partial(near_kernel, [len(unit) for unit in units]),
        grid_spec=pltpu.PrefetchScalarGridSpec(
            num_scalar_prefetch=2,
            grid=(NH,),
            in_specs=[whole(a) for a in (qa, qb, *blocks)],
            out_specs=[out(2 * HD), out(128)],
            scratch_shapes=[
                pltpu.VMEM((rows, HD), jnp.bfloat16),
                pltpu.VMEM((rows, HD), jnp.bfloat16),
                pltpu.VMEM((rows, 2 * HD), jnp.bfloat16),
            ],
        ),
        out_shape=[
            jax.ShapeDtypeStruct((NH, rows, 2 * HD), jnp.float32),
            jax.ShapeDtypeStruct((NH, rows, 128), jnp.float32),
        ],
        compiler_params=pltpu.CompilerParams(vmem_limit_bytes=VMEM_LIMIT),
        cost_estimate=attention_cost(3, rows),
        name="near_attention",
    )(order, place, qa, qb, *blocks)


def far_attention(order, place, qa, qb, acc, top, blocks):
    rows = qa.shape[0]
    chunk = QUARTER + TAIL
    part = lambda a: pl.BlockSpec((1,) + a.shape[1:], lambda i, *s: (i, 0, 0))
    return pl.pallas_call(
        far_kernel,
        grid_spec=pltpu.PrefetchScalarGridSpec(
            num_scalar_prefetch=2,
            grid=(NH,),
            in_specs=[whole(qa), whole(qb), part(acc), part(top)] + [whole(b) for b in blocks],
            out_specs=pl.BlockSpec((4, chunk, HD), lambda i, o, s: (i ^ s[0], 0, 0)),
            scratch_shapes=[
                pltpu.VMEM((rows, HD), jnp.bfloat16),
                pltpu.VMEM((rows, HD), jnp.bfloat16),
                pltpu.VMEM((rows, 2 * HD), jnp.bfloat16),
                pltpu.VMEM((rows, 2 * HD), jnp.float32),
                pltpu.VMEM((rows, 128), jnp.float32),
            ],
        ),
        out_shape=jax.ShapeDtypeStruct((NH * 4, chunk, HD), jnp.bfloat16),
        compiler_params=pltpu.CompilerParams(vmem_limit_bytes=VMEM_LIMIT),
        cost_estimate=attention_cost(1, rows),
        name="far_attention",
    )(order, place, qa, qb, acc, top, *blocks)


def join_kernel(s_ref, in_ref, w0_ref, w1_ref, w2_ref, w3_ref, o_ref, a_ref, w_ref):
    h, y, z, core = s_ref[0], s_ref[1], s_ref[2], s_ref[3]
    place = h * 4 + y * 2 + core

    @pl.when(pl.program_id(0) == 0)
    def _():
        for r in range(4):
            used = used_slots(y ^ (r // 2), z)
            parts = []
            for dh in range(NH):
                at = (dh * 4 + r) ^ place
                rows = in_ref[at, QUARTER:, :].astype(jnp.float32)
                parts.append((at, rows[0:2] + rows[2:4] + rows[4:6]))
            top = jnp.maximum(parts[0][1], parts[1][1])
            e = [jnp.exp2(lse - top) for _, lse in parts]
            norm = e[0] + e[1]
            for half in range(2):
                out = None
                for (at, _), weight in zip(parts, e):
                    w = jnp.where(used, weight / norm, 0.0)[half : half + 1, :]
                    col = jnp.broadcast_to(w, (128, 128)).T
                    term = in_ref[at, half * 128 : half * 128 + 128, :].astype(jnp.float32) * col
                    out = term if out is None else out + term
                out = out.astype(jnp.bfloat16)
                for j in range(4):
                    start = pl.multiple_of(((z + half * 4 + j) % NZ) * BLK, BLK)
                    a_ref[pl.ds(start, BLK), r * HD : r * HD + HD] = out[j * BLK : j * BLK + BLK]

    for r, ref in enumerate((w0_ref, w1_ref, w2_ref, w3_ref)):
        w_ref[r * HD : r * HD + HD, :] = ref[...]
    o_ref[...] = jnp.dot(a_ref[...], w_ref[...], preferred_element_type=jnp.float32).astype(
        jnp.bfloat16
    )


def join_heads(place, received, weights):
    width = weights[0].shape[1]
    step = width // 4
    return pl.pallas_call(
        join_kernel,
        grid_spec=pltpu.PrefetchScalarGridSpec(
            num_scalar_prefetch=1,
            grid=(4,),
            in_specs=[whole(received)] + [pl.BlockSpec((HD, step), lambda i, s: (0, i))] * 4,
            out_specs=pl.BlockSpec((QUARTER, step), lambda i, s: (0, i)),
            scratch_shapes=[
                pltpu.VMEM((QUARTER, 4 * HD), jnp.bfloat16),
                pltpu.VMEM((4 * HD, step), jnp.bfloat16),
            ],
        ),
        out_shape=jax.ShapeDtypeStruct((QUARTER, width), jnp.bfloat16),
        compiler_params=pltpu.CompilerParams(vmem_limit_bytes=VMEM_LIMIT),
        name="join_heads",
    )(place, received, *weights)


def decode(latents, root_kernel):
    seq_count = latents.shape[0]
    row_patches = seq_count // FR
    me = lax.axis_index("seq")
    ringed = jnp.concatenate([latents[-1:], latents, latents[:1]], axis=0)
    position = (me - row_patches // 2 + seq_count) % seq_count
    patch_row = position % row_patches
    frame_index = position // row_patches
    row_ids = jnp.arange(P_SIZE + 2, dtype=jnp.int32)
    keep = jnp.where(
        row_ids == 0,
        patch_row > 0,
        jnp.where(row_ids == P_SIZE + 1, patch_row < row_patches - 1, True),
    )
    width_cols = BLK * P_SIZE
    windows = []
    for lag in range(3):
        start = (me - lag * row_patches + seq_count) % seq_count
        three = lax.dynamic_slice_in_dim(ringed, start, 3, axis=0)
        slab = (
            three.reshape(3, BLK, P_SIZE, P_SIZE, C)
            .transpose(0, 2, 1, 3, 4)
            .reshape(3 * P_SIZE, width_cols, C)
        )[P_SIZE - 1 : 2 * P_SIZE + 1]
        ok = keep & (frame_index >= lag)
        slab = jnp.where(ok[:, None, None], slab, jnp.zeros_like(slab))
        framed = jnp.pad(slab, ((0, 0), (1, 1), (0, 0)))
        for row_off in range(3):
            for col_off in range(3):
                windows.append(framed[row_off : row_off + P_SIZE, col_off : col_off + width_cols])
    stacked = jnp.concatenate(windows, axis=-1).reshape(P_SIZE * width_cols, 27 * C)
    decoded = jnp.dot(stacked, root_kernel, preferred_element_type=jnp.float32)
    return decoded.reshape(P_SIZE, width_cols, root_kernel.shape[1]).astype(jnp.bfloat16)[None]


def per_device(
    hidden, levels, span_order, modulation, in_weight, out_weight, latent_weight, decoder_weight
):
    span_me = lax.axis_index("span")
    seq_me = lax.axis_index("seq")
    x, h = span_me // NH, span_me % NH
    y, z, core = seq_me // (NZ * NC), (seq_me // NC) % NZ, seq_me % NC
    place = jnp.stack([h, y, z, core, x])
    pv = latent_weight.shape[1]
    seq_count = NY * NZ * NC

    normed, gate_row = normalize(levels, hidden[0], modulation)
    w_own = in_weight[0]
    own_blocks, other_blocks = gather_class(normed)
    w_oth = move_core(w_own)
    mine_a, theirs_a = project(own_blocks, w_own, w_oth)
    mine_b, theirs_b = project(other_blocks, w_own, w_oth)
    triples = jnp.concatenate([mine_a, move_core(theirs_a), mine_b, move_core(theirs_b)], axis=0)
    q = triples[:, :HD]
    kv = triples[:, HD:]

    half = kv.shape[0] // 2
    kv_up, kv_dn = move_x(kv, 1), move_x(kv, -1)
    q_hi = move_hi(q)
    kv_far = (move_x(kv_up[:half], 1), move_x(kv_dn[half:], -1))

    out_w, q = lax.optimization_barrier((out_weight[0], q))
    part = self_attention(place, q, kv, latent_matrix(out_w, gate_row, latent_weight))
    q_hi, part = lax.optimization_barrier((q_hi, part))

    out_w, q_hi = lax.optimization_barrier((out_w, q_hi))
    w_core, w_far = move_core(out_w), move_y(out_w)
    weights = (out_w, w_core, w_far, move_core(w_far))

    acc, top = near_attention(span_order, place, q, q_hi, ((kv,), (kv_up,), (kv_dn,)))
    chunks = far_attention(span_order, place, q, q_hi, acc, top, kv_far)
    groups = [
        [
            span_at(i, hh) * seq_count + seq_at(yy, j, cc)
            for hh in range(NH)
            for yy in range(NY)
            for cc in range(NC)
        ]
        for i in range(NX)
        for j in range(NZ)
    ]
    received = lax.all_to_all(
        chunks, ("span", "seq"), 0, 0, tiled=True, axis_index_groups=groups
    )
    partial = join_heads(place, received, weights)
    z_groups = [[seq_at(yy, j, cc) for j in range(NZ)] for yy in range(NY) for cc in range(NC)]
    summed = lax.psum_scatter(
        partial, "seq", scatter_dimension=0, tiled=True, axis_index_groups=z_groups
    ).astype(jnp.float32)
    block_out = (hidden[0].astype(jnp.float32) + gate_row * summed).astype(jnp.bfloat16)[None]

    part = lax.all_to_all(part, "seq", 0, 0, tiled=True)
    own_latents = jnp.dot(hidden[0], latent_weight, preferred_element_type=jnp.float32)
    latents = (jnp.sum(part.astype(jnp.float32), axis=0) + own_latents).astype(jnp.bfloat16)
    group_ids = jnp.arange(span_order.shape[0], dtype=jnp.int32)
    root = jnp.sum(jnp.where(span_order == 0, group_ids, 0))
    spread = lax.all_to_all(
        jnp.broadcast_to(latents[None], (NX * NH, BLK, pv)), "span", 0, 0, tiled=True
    )
    latents = lax.dynamic_index_in_dim(spread, root, 0, keepdims=True)
    every = lax.all_to_all(
        jnp.broadcast_to(latents, (seq_count, BLK, pv)), "seq", 0, 0, tiled=True
    )
    decoded = decode(every, decoder_weight.reshape(27 * C, decoder_weight.shape[4]))
    return (block_out, decoded)


def solution(mesh):
    placed = (
        P("span", "seq", None),
        P("span"),
        P(),
        P(),
        P("seq", None, None),
        P("seq", None, None),
        P(),
        P(None, None, None, None, "span"),
    )
    return jax.shard_map(
        per_device,
        mesh=mesh,
        in_specs=placed,
        out_specs=(P("span", "seq", None), P("seq", None, None, "span")),
        check_vma=False,
    )
```

```python
import functools
import math

import jax
import jax.numpy as jnp
from jax import lax
from jax.experimental import pallas as pl
from jax.experimental.pallas import tpu as pltpu
from jax.sharding import PartitionSpec as P

HEADS = 24
FR = 4
P_SIZE = 2
C = 16
HD = 128

EPSILON = 1e-06
NEG_LARGE = 1e30

NX, NH, NY, NZ, NC = 4, 2, 2, 8, 2
BLK = 32
QUARTER = NZ * BLK
TAIL = 16


def seq_at(y, z, c):
    return ((y % NY) * NZ + z % NZ) * NC + c % NC


def span_at(x, h):
    return (x % NX) * NH + h % NH


def seq_route(dy=0, dz=0, dc=0):
    return [
        (seq_at(y, z, c), seq_at(y + dy, z + dz, c + dc))
        for y in range(NY)
        for z in range(NZ)
        for c in range(NC)
    ]


def span_route(dx=0, dh=0):
    return [(span_at(x, h), span_at(x + dx, h + dh)) for x in range(NX) for h in range(NH)]


def move_z(a, d):
    return lax.ppermute(a, "seq", seq_route(dz=d))


def halve(part, bit, swap):
    order = part.reshape((2, part.shape[0] // 2) + part.shape[1:])
    keep = jnp.where(bit == 0, order[0], order[1])
    send = jnp.where(bit == 0, order[1], order[0])
    return (keep.astype(jnp.float32) + swap(send).astype(jnp.float32)).astype(part.dtype)


def move_y(a):
    return lax.ppermute(a, "seq", seq_route(dy=1))


def move_core(a):
    return lax.ppermute(a, "seq", seq_route(dc=1))


def move_x(a, d):
    return lax.ppermute(a, "span", span_route(dx=d))


def move_hi(a):
    return lax.ppermute(a, "span", span_route(dh=1))


HALVES = (
    ((0, 0), (0, 1), (0, 2), (0, 6), (0, 7), (1, 0), (1, 1), (1, 7)),
    ((0, 3), (0, 4), (0, 5), (1, 2), (1, 3), (1, 4), (1, 5), (1, 6)),
)


def block_at(y_apart, core_apart, d):
    half = 0 if (y_apart, d) in HALVES[0] else 1
    return half * 2 * NZ + core_apart * NZ + HALVES[half].index((y_apart, d))


def block_of(at):
    half, core_apart, i = at // (2 * NZ), at // NZ % 2, at % NZ
    y_apart, d = HALVES[half][i]
    return y_apart, core_apart, d


def gather_class(b):
    up1, dn1, y0 = move_z(b, 1), move_z(b, -1), move_y(b)
    up2, dn2 = move_z(up1, 1), move_z(dn1, -1)
    yu1, yd1 = move_y(up1), move_y(dn1)
    up3, dn3 = move_z(up2, 1), move_z(dn2, -1)
    yu2, yd2 = move_y(up2), move_y(dn2)
    far = move_z(up3, 1)
    yu3, yd3 = move_z(yu2, 1), move_z(yd2, -1)
    yfar = lax.ppermute(dn3, "seq", seq_route(dy=1, dz=-1))
    return (b, dn1, dn2, up2, up1, y0, yd1, yu1), (dn3, far, up3, yd2, yd3, yfar, yu3, yu2)


VMEM_LIMIT = 40 * 2**20
EXP_SCALE = math.log2(math.e) / math.sqrt(HD)


def norm_kernel(level_ref, hidden_ref, mod_ref, out_ref, gate_ref):
    values = hidden_ref[...].astype(jnp.float32)
    row = pl.ds(level_ref[0] % MOD_ROWS, 1)
    center = values - jnp.mean(values, axis=-1, keepdims=True)
    spread = jnp.mean(center * center, axis=-1, keepdims=True)
    scaled = center * lax.rsqrt(spread + EPSILON)
    out_ref[...] = (scaled * (1.0 + mod_ref[1, row, :]) + mod_ref[0, row, :]).astype(jnp.bfloat16)
    gate_ref[...] = mod_ref[2, row, :]


MOD_ROWS = 8


def normalize(levels, rows, modulation):
    width = rows.shape[1]
    return pl.pallas_call(
        norm_kernel,
        grid_spec=pltpu.PrefetchScalarGridSpec(
            num_scalar_prefetch=1,
            grid=(1,),
            in_specs=[
                pl.BlockSpec(rows.shape, lambda i, s: (0, 0)),
                pl.BlockSpec((3, MOD_ROWS, width), lambda i, s: (0, s[0] // MOD_ROWS, 0)),
            ],
            out_specs=[
                pl.BlockSpec(rows.shape, lambda i, s: (0, 0)),
                pl.BlockSpec((1, width), lambda i, s: (0, 0)),
            ],
        ),
        out_shape=[
            jax.ShapeDtypeStruct(rows.shape, jnp.bfloat16),
            jax.ShapeDtypeStruct((1, width), jnp.float32),
        ],
        name="normalize",
    )(levels, rows, modulation.transpose(1, 0, 2))


def latent_kernel(w_ref, gate_ref, lw_ref, o_ref):
    gated = w_ref[...].astype(jnp.float32) * gate_ref[...]
    hi = gated.astype(jnp.bfloat16)
    lo = (gated - hi.astype(jnp.float32)).astype(jnp.bfloat16)
    out = dot_t(hi, lw_ref[...]) + dot_t(lo, lw_ref[...])
    top = out.astype(jnp.bfloat16)
    o_ref[: w_ref.shape[0], :] = top
    o_ref[w_ref.shape[0] :, :] = (out - top.astype(jnp.float32)).astype(jnp.bfloat16)


def latent_matrix(w, gate_row, latent_weight):
    pv = latent_weight.shape[1]
    return pl.pallas_call(
        latent_kernel,
        out_shape=jax.ShapeDtypeStruct((2 * w.shape[0], pv), jnp.bfloat16),
        compiler_params=pltpu.CompilerParams(vmem_limit_bytes=VMEM_LIMIT),
        name="latent_matrix",
    )(w, gate_row, latent_weight.T)


def project_kernel(*refs):
    blocks, (own_ref, oth_ref, mine_ref, theirs_ref, rows) = refs[:NZ], refs[NZ:]
    for i, block in enumerate(blocks):
        rows[i * BLK : i * BLK + BLK, :] = block[...]
    for w_ref, o_ref in ((oth_ref, theirs_ref), (own_ref, mine_ref)):
        out = jnp.dot(rows[...], w_ref[...], preferred_element_type=jnp.float32)
        o_ref[:, :HD] = (out[:, :HD] * EXP_SCALE).astype(jnp.bfloat16)
        o_ref[:, HD:] = out[:, HD:].astype(jnp.bfloat16)


def project(blocks, w_own, w_oth):
    width, cols = w_own.shape
    rows = len(blocks) * BLK
    vmem = pl.BlockSpec(memory_space=pltpu.VMEM)
    return pl.pallas_call(
        project_kernel,
        in_specs=[vmem] * (len(blocks) + 2),
        out_specs=[vmem, vmem],
        out_shape=[jax.ShapeDtypeStruct((rows, cols), jnp.bfloat16)] * 2,
        scratch_shapes=[pltpu.VMEM((rows, width), jnp.bfloat16)],
        compiler_params=pltpu.CompilerParams(vmem_limit_bytes=VMEM_LIMIT),
        cost_estimate=pl.CostEstimate(
            flops=4 * rows * width * cols,
            bytes_accessed=4 * width * cols + 2 * rows * width,
            transcendentals=0,
        ),
        name="project",
    )(*blocks, w_own, w_oth)


def dot_t(a, b):
    return lax.dot_general(a, b, (((1,), (1,)), ((), ())), preferred_element_type=jnp.float32)


TILE = 128


def used_slots(y, z):
    return (y * NZ + z) * NC < HEADS


def self_kernel(s_ref, q_ref, kv_ref, m_ref, o_ref, values):
    y, z, core = s_ref[1], s_ref[2], s_ref[3]
    used = used_slots(y, z)
    values[:, :HD] = kv_ref[:, HD:]
    values[:, HD:] = jnp.ones((values.shape[0], HD), jnp.bfloat16)
    for t in range(q_ref.shape[0] // TILE):
        s = dot_t(q_ref[t * TILE : t * TILE + TILE, :], kv_ref[:, :HD])
        p = jnp.exp2(s - jnp.max(s, axis=1, keepdims=True)).astype(jnp.bfloat16)
        acc = jnp.dot(p, values[...], preferred_element_type=jnp.float32)
        att = (acc[:, :HD] / acc[:, HD:]).astype(jnp.bfloat16)
        att = jnp.concatenate([att, att], axis=1)
        part = jnp.dot(att, m_ref[...], preferred_element_type=jnp.float32)
        part = jnp.where(used, part, 0.0).astype(jnp.bfloat16)
        for j in range(TILE // BLK):
            y_apart, core_apart, d = block_of(t * (TILE // BLK) + j)
            at = ((z + d) % NZ * NC + (core ^ core_apart)) * NY + (y ^ y_apart)
            o_ref[at] = part[j * BLK : j * BLK + BLK]


def self_attention(place, q, kv, matrix):
    pv = matrix.shape[1]
    rows = q.shape[0]
    return pl.pallas_call(
        self_kernel,
        grid_spec=pltpu.PrefetchScalarGridSpec(
            num_scalar_prefetch=1,
            grid=(1,),
            in_specs=[pl.BlockSpec(a.shape, lambda i, s: (0, 0)) for a in (q, kv, matrix)],
            out_specs=pl.BlockSpec((rows // BLK, BLK, pv), lambda i, s: (0, 0, 0)),
            scratch_shapes=[pltpu.VMEM((rows, 2 * HD), jnp.bfloat16)],
        ),
        out_shape=jax.ShapeDtypeStruct((rows // BLK, BLK, pv), jnp.bfloat16),
        compiler_params=pltpu.CompilerParams(vmem_limit_bytes=VMEM_LIMIT),
        cost_estimate=pl.CostEstimate(
            flops=6 * rows * rows * HD, bytes_accessed=2**20, transcendentals=rows * rows
        ),
        name="self_attention",
    )(place, q, kv, matrix)


def visit(refs, q, keys, values, acc, top):
    at = 0
    for ref in refs:
        n = ref.shape[0]
        keys[at : at + n, :] = ref[:, :HD]
        values[at : at + n, :HD] = ref[:, HD:]
        at += n
    for t in range(q.shape[0] // TILE):
        rows = slice(t * TILE, t * TILE + TILE)
        s = dot_t(q[rows, :], keys[...])
        old = top[rows, :1]
        new = jnp.maximum(old, jnp.max(s, axis=1, keepdims=True))
        p = jnp.exp2(s - new).astype(jnp.bfloat16)
        acc[rows, :] = acc[rows, :] * jnp.exp2(old - new) + jnp.dot(
            p, values[...], preferred_element_type=jnp.float32
        )
        top[rows, :] = jnp.broadcast_to(new, (TILE, 128))


def sees(order_ref, s_ref, dh, dx):
    x, h = s_ref[4], s_ref[0]
    mine = order_ref[x * NH + (h ^ dh)]
    return order_ref[((x + dx) % NX) * NH + h] <= mine


def near_kernel(counts, order_ref, s_ref, qa_ref, qb_ref, *refs):
    blocks, (acc_ref, top_ref, q, keys, values) = refs[: sum(counts)], refs[sum(counts) :]
    dh = pl.program_id(0)
    q[...] = jnp.where(dh == 0, qa_ref[...], qb_ref[...])
    values[:, HD:] = jnp.ones((values.shape[0], HD), jnp.bfloat16)
    acc_ref[...] = jnp.zeros_like(acc_ref)
    top_ref[...] = jnp.full_like(top_ref, -NEG_LARGE)
    at = 0
    for count, dx in zip(counts, (0, NX - 1, 1)):
        unit = blocks[at : at + count]
        at += count
        pl.when(sees(order_ref, s_ref, dh, dx))(
            functools.partial(visit, unit, q, keys, values, acc_ref.at[0], top_ref.at[0])
        )


def far_kernel(order_ref, s_ref, qa_ref, qb_ref, acc_in, top_in, *refs):
    blocks, (o_ref, q, keys, values, acc, top) = refs[:-6], refs[-6:]
    dh = pl.program_id(0)
    q[...] = jnp.where(dh == 0, qa_ref[...], qb_ref[...])
    values[:, HD:] = jnp.ones((values.shape[0], HD), jnp.bfloat16)
    acc[...] = acc_in[0]
    top[...] = top_in[0]
    pl.when(sees(order_ref, s_ref, dh, 2))(
        functools.partial(visit, blocks, q, keys, values, acc, top)
    )
    y, core = s_ref[1], s_ref[3]
    for quarter in range(4):
        starts = [block_at(quarter // 2, quarter % 2, d) * BLK for d in range(NZ)]
        gather = lambda ref, cols: jnp.concatenate([ref[i : i + BLK, cols] for i in starts], axis=0)
        total = gather(acc, slice(HD, 2 * HD))
        some = total > 0.0
        safe = jnp.where(some, total, 1.0)
        at = quarter ^ (y * 2 + core)
        o_ref[at, :QUARTER, :] = (gather(acc, slice(0, HD)) / safe).astype(jnp.bfloat16)
        lse = jnp.where(some, gather(top, slice(0, 128)) + jnp.log2(safe), -NEG_LARGE)
        row = lse.T[0:1, :]
        row = jnp.concatenate([row[:, :128], row[:, 128:]], axis=0)
        hi = row.astype(jnp.bfloat16).astype(jnp.float32)
        rest = row - hi
        mid = rest.astype(jnp.bfloat16).astype(jnp.float32)
        pad = jnp.zeros((TAIL - 6, 128), jnp.float32)
        o_ref[at, QUARTER:, :] = jnp.concatenate([hi, mid, rest - mid, pad], axis=0).astype(
            jnp.bfloat16
        )


def whole(a):
    return pl.BlockSpec(a.shape, lambda i, *s: (0,) * a.ndim)


def attention_cost(units, rows):
    pairs = 2 * units * rows * rows
    return pl.CostEstimate(flops=6 * pairs * HD, bytes_accessed=4 * 2**20, transcendentals=pairs)


def near_attention(order, place, qa, qb, units):
    rows = qa.shape[0]
    blocks = [b for unit in units for b in unit]
    out = lambda cols: pl.BlockSpec((1, rows, cols), lambda i, *s: (i, 0, 0))
    return pl.pallas_call(
        functools.partial(near_kernel, [len(unit) for unit in units]),
        grid_spec=pltpu.PrefetchScalarGridSpec(
            num_scalar_prefetch=2,
            grid=(NH,),
            in_specs=[whole(a) for a in (qa, qb, *blocks)],
            out_specs=[out(2 * HD), out(128)],
            scratch_shapes=[
                pltpu.VMEM((rows, HD), jnp.bfloat16),
                pltpu.VMEM((rows, HD), jnp.bfloat16),
                pltpu.VMEM((rows, 2 * HD), jnp.bfloat16),
            ],
        ),
        out_shape=[
            jax.ShapeDtypeStruct((NH, rows, 2 * HD), jnp.float32),
            jax.ShapeDtypeStruct((NH, rows, 128), jnp.float32),
        ],
        compiler_params=pltpu.CompilerParams(vmem_limit_bytes=VMEM_LIMIT),
        cost_estimate=attention_cost(3, rows),
        name="near_attention",
    )(order, place, qa, qb, *blocks)


def far_attention(order, place, qa, qb, acc, top, blocks):
    rows = qa.shape[0]
    chunk = QUARTER + TAIL
    part = lambda a: pl.BlockSpec((1,) + a.shape[1:], lambda i, *s: (i, 0, 0))
    return pl.pallas_call(
        far_kernel,
        grid_spec=pltpu.PrefetchScalarGridSpec(
            num_scalar_prefetch=2,
            grid=(NH,),
            in_specs=[whole(qa), whole(qb), part(acc), part(top)] + [whole(b) for b in blocks],
            out_specs=pl.BlockSpec((4, chunk, HD), lambda i, o, s: (i ^ s[0], 0, 0)),
            scratch_shapes=[
                pltpu.VMEM((rows, HD), jnp.bfloat16),
                pltpu.VMEM((rows, HD), jnp.bfloat16),
                pltpu.VMEM((rows, 2 * HD), jnp.bfloat16),
                pltpu.VMEM((rows, 2 * HD), jnp.float32),
                pltpu.VMEM((rows, 128), jnp.float32),
            ],
        ),
        out_shape=jax.ShapeDtypeStruct((NH * 4, chunk, HD), jnp.bfloat16),
        compiler_params=pltpu.CompilerParams(vmem_limit_bytes=VMEM_LIMIT),
        cost_estimate=attention_cost(1, rows),
        name="far_attention",
    )(order, place, qa, qb, acc, top, *blocks)


def join_kernel(s_ref, in_ref, w0_ref, w1_ref, w2_ref, w3_ref, o_ref, a_ref, w_ref):
    h, y, z, core = s_ref[0], s_ref[1], s_ref[2], s_ref[3]
    place = h * 4 + y * 2 + core

    @pl.when(pl.program_id(0) == 0)
    def _():
        for r in range(4):
            used = used_slots(y ^ (r // 2), z)
            parts = []
            for dh in range(NH):
                at = (dh * 4 + r) ^ place
                rows = in_ref[at, QUARTER:, :].astype(jnp.float32)
                parts.append((at, rows[0:2] + rows[2:4] + rows[4:6]))
            top = jnp.maximum(parts[0][1], parts[1][1])
            e = [jnp.exp2(lse - top) for _, lse in parts]
            norm = e[0] + e[1]
            for half in range(2):
                out = None
                for (at, _), weight in zip(parts, e):
                    w = jnp.where(used, weight / norm, 0.0)[half : half + 1, :]
                    col = jnp.broadcast_to(w, (128, 128)).T
                    term = in_ref[at, half * 128 : half * 128 + 128, :].astype(jnp.float32) * col
                    out = term if out is None else out + term
                out = out.astype(jnp.bfloat16)
                for j in range(4):
                    start = pl.multiple_of(((z + half * 4 + j) % NZ) * BLK, BLK)
                    a_ref[pl.ds(start, BLK), r * HD : r * HD + HD] = out[j * BLK : j * BLK + BLK]

    for r, ref in enumerate((w0_ref, w1_ref, w2_ref, w3_ref)):
        w_ref[r * HD : r * HD + HD, :] = ref[...]
    o_ref[...] = jnp.dot(a_ref[...], w_ref[...], preferred_element_type=jnp.float32).astype(
        jnp.bfloat16
    )


def join_heads(place, received, weights):
    width = weights[0].shape[1]
    step = width // 4
    return pl.pallas_call(
        join_kernel,
        grid_spec=pltpu.PrefetchScalarGridSpec(
            num_scalar_prefetch=1,
            grid=(4,),
            in_specs=[whole(received)] + [pl.BlockSpec((HD, step), lambda i, s: (0, i))] * 4,
            out_specs=pl.BlockSpec((QUARTER, step), lambda i, s: (0, i)),
            scratch_shapes=[
                pltpu.VMEM((QUARTER, 4 * HD), jnp.bfloat16),
                pltpu.VMEM((4 * HD, step), jnp.bfloat16),
            ],
        ),
        out_shape=jax.ShapeDtypeStruct((QUARTER, width), jnp.bfloat16),
        compiler_params=pltpu.CompilerParams(vmem_limit_bytes=VMEM_LIMIT),
        name="join_heads",
    )(place, received, *weights)


def decode(latents, root_kernel):
    seq_count = latents.shape[0]
    row_patches = seq_count // FR
    me = lax.axis_index("seq")
    ringed = jnp.concatenate([latents[-1:], latents, latents[:1]], axis=0)
    position = (me - row_patches // 2 + seq_count) % seq_count
    patch_row = position % row_patches
    frame_index = position // row_patches
    row_ids = jnp.arange(P_SIZE + 2, dtype=jnp.int32)
    keep = jnp.where(
        row_ids == 0,
        patch_row > 0,
        jnp.where(row_ids == P_SIZE + 1, patch_row < row_patches - 1, True),
    )
    width_cols = BLK * P_SIZE
    windows = []
    for lag in range(3):
        start = (me - lag * row_patches + seq_count) % seq_count
        three = lax.dynamic_slice_in_dim(ringed, start, 3, axis=0)
        slab = (
            three.reshape(3, BLK, P_SIZE, P_SIZE, C)
            .transpose(0, 2, 1, 3, 4)
            .reshape(3 * P_SIZE, width_cols, C)
        )[P_SIZE - 1 : 2 * P_SIZE + 1]
        ok = keep & (frame_index >= lag)
        slab = jnp.where(ok[:, None, None], slab, jnp.zeros_like(slab))
        framed = jnp.pad(slab, ((0, 0), (1, 1), (0, 0)))
        for row_off in range(3):
            for col_off in range(3):
                windows.append(framed[row_off : row_off + P_SIZE, col_off : col_off + width_cols])
    stacked = jnp.concatenate(windows, axis=-1).reshape(P_SIZE * width_cols, 27 * C)
    decoded = jnp.dot(stacked, root_kernel, preferred_element_type=jnp.float32)
    return decoded.reshape(P_SIZE, width_cols, root_kernel.shape[1]).astype(jnp.bfloat16)[None]


def after(value, earlier):
    return lax.optimization_barrier((value, earlier))[0]


def per_device(
    hidden, levels, span_order, modulation, in_weight, out_weight, latent_weight, decoder_weight
):
    span_me = lax.axis_index("span")
    seq_me = lax.axis_index("seq")
    x, h = span_me // NH, span_me % NH
    y, z, core = seq_me // (NZ * NC), (seq_me // NC) % NZ, seq_me % NC
    place = jnp.stack([h, y, z, core, x])
    pv = latent_weight.shape[1]
    seq_count = NY * NZ * NC

    normed, gate_row = normalize(levels, hidden[0], modulation)
    w_own = in_weight[0]
    own_blocks, other_blocks = gather_class(normed)
    w_oth = move_core(w_own)
    mine_a, theirs_a = project(own_blocks, w_own, w_oth)
    mine_b, theirs_b = project(other_blocks, w_own, w_oth)
    triples = jnp.concatenate([mine_a, move_core(theirs_a), mine_b, move_core(theirs_b)], axis=0)
    q = triples[:, :HD]
    kv = triples[:, HD:]

    half = kv.shape[0] // 2
    kv_up, kv_dn = move_x(kv, 1), move_x(kv, -1)
    q_hi = move_hi(q)
    kv_far = (move_x(kv_up[:half], 1), move_x(kv_dn[half:], -1))

    part = self_attention(place, q, kv, latent_matrix(out_weight[0], gate_row, latent_weight))
    q_hi = after(q_hi, part)
    z_groups = [[seq_at(yy, j, cc) for j in range(NZ)] for yy in range(NY) for cc in range(NC)]
    part = lax.psum_scatter(
        part, "seq", scatter_dimension=0, tiled=True, axis_index_groups=z_groups
    )

    out_w = after(out_weight[0], kv_up)
    w_core, w_far = move_core(out_w), move_y(out_w)
    weights = (out_w, w_core, w_far, move_core(w_far))

    acc, top = near_attention(span_order, place, q, q_hi, ((kv,), (kv_up,), (kv_dn,)))
    chunks = far_attention(span_order, place, q, q_hi, acc, top, kv_far)
    part = after(part, chunks)
    part = halve(part, core, move_core)
    part = halve(part, y, move_y)
    groups = [
        [
            span_at(i, hh) * seq_count + seq_at(yy, j, cc)
            for hh in range(NH)
            for yy in range(NY)
            for cc in range(NC)
        ]
        for i in range(NX)
        for j in range(NZ)
    ]
    received = lax.all_to_all(
        chunks, ("span", "seq"), 0, 0, tiled=True, axis_index_groups=groups
    )
    received = after(received, part)
    partial = join_heads(place, received, weights)
    part = after(part, partial)
    summed = lax.psum_scatter(
        partial, "seq", scatter_dimension=0, tiled=True, axis_index_groups=z_groups
    ).astype(jnp.float32)
    block_out = (hidden[0].astype(jnp.float32) + gate_row * summed).astype(jnp.bfloat16)[None]

    own_latents = jnp.dot(hidden[0], latent_weight, preferred_element_type=jnp.float32)
    latents = (part[0].astype(jnp.float32) + own_latents).astype(jnp.bfloat16)
    group_ids = jnp.arange(span_order.shape[0], dtype=jnp.int32)
    root = jnp.sum(jnp.where(span_order == 0, group_ids, 0))
    spread = lax.all_to_all(
        jnp.broadcast_to(latents[None], (NX * NH, BLK, pv)), "span", 0, 0, tiled=True
    )
    latents = lax.dynamic_index_in_dim(spread, root, 0, keepdims=True)
    every = lax.all_to_all(
        jnp.broadcast_to(latents, (seq_count, BLK, pv)), "seq", 0, 0, tiled=True
    )
    decoded = decode(every, decoder_weight.reshape(27 * C, decoder_weight.shape[4]))
    return (block_out, decoded)


def solution(mesh):
    placed = (
        P("span", "seq", None),
        P("span"),
        P(),
        P(),
        P("seq", None, None),
        P("seq", None, None),
        P(),
        P(None, None, None, None, "span"),
    )
    return jax.shard_map(
        per_device,
        mesh=mesh,
        in_specs=placed,
        out_specs=(P("span", "seq", None), P("seq", None, None, "span")),
        check_vma=False,
    )
```

```python
import functools
import math

import jax
import jax.numpy as jnp
from jax import lax
from jax.experimental import pallas as pl
from jax.experimental.pallas import tpu as pltpu
from jax.sharding import PartitionSpec as P

HEADS = 24
FR = 4
P_SIZE = 2
C = 16
HD = 128

EPSILON = 1e-06
NEG_LARGE = 1e30

NX, NH, NY, NZ, NC = 4, 2, 2, 8, 2
BLK = 32
QUARTER = NZ * BLK
TAIL = 16


def seq_at(y, z, c):
    return ((y % NY) * NZ + z % NZ) * NC + c % NC


def span_at(x, h):
    return (x % NX) * NH + h % NH


def seq_route(dy=0, dz=0, dc=0):
    return [
        (seq_at(y, z, c), seq_at(y + dy, z + dz, c + dc))
        for y in range(NY)
        for z in range(NZ)
        for c in range(NC)
    ]


def span_route(dx=0, dh=0):
    return [(span_at(x, h), span_at(x + dx, h + dh)) for x in range(NX) for h in range(NH)]


def move_z(a, d):
    return lax.ppermute(a, "seq", seq_route(dz=d))


def swap_z(a, k):
    route = [
        (seq_at(y, z, c), seq_at(y, z ^ k, c)) for y in range(NY) for z in range(NZ) for c in range(NC)
    ]
    return lax.ppermute(a, "seq", route)


def halve(part, bit, swap):
    order = part.reshape((2, part.shape[0] // 2) + part.shape[1:])
    keep = jnp.where(bit == 0, order[0], order[1])
    send = jnp.where(bit == 0, order[1], order[0])
    return (keep.astype(jnp.float32) + swap(send).astype(jnp.float32)).astype(part.dtype)


def move_y(a):
    return lax.ppermute(a, "seq", seq_route(dy=1))


def move_core(a):
    return lax.ppermute(a, "seq", seq_route(dc=1))


def move_x(a, d):
    return lax.ppermute(a, "span", span_route(dx=d))


def move_hi(a):
    return lax.ppermute(a, "span", span_route(dh=1))


HALVES = (
    ((0, 0), (0, 1), (0, 2), (0, 6), (0, 7), (1, 0), (1, 1), (1, 7)),
    ((0, 3), (0, 4), (0, 5), (1, 2), (1, 3), (1, 4), (1, 5), (1, 6)),
)


def block_at(y_apart, core_apart, d):
    half = 0 if (y_apart, d) in HALVES[0] else 1
    return half * 2 * NZ + core_apart * NZ + HALVES[half].index((y_apart, d))


def block_of(at):
    half, core_apart, i = at // (2 * NZ), at // NZ % 2, at % NZ
    y_apart, d = HALVES[half][i]
    return y_apart, core_apart, d


def gather_class(b):
    up1, dn1, y0 = move_z(b, 1), move_z(b, -1), move_y(b)
    up2, dn2 = move_z(up1, 1), move_z(dn1, -1)
    yu1, yd1 = move_y(up1), move_y(dn1)
    up3, dn3 = move_z(up2, 1), move_z(dn2, -1)
    yu2, yd2 = move_y(up2), move_y(dn2)
    far = move_z(up3, 1)
    yu3, yd3 = move_z(yu2, 1), move_z(yd2, -1)
    yfar = lax.ppermute(dn3, "seq", seq_route(dy=1, dz=-1))
    return (b, dn1, dn2, up2, up1, y0, yd1, yu1), (dn3, far, up3, yd2, yd3, yfar, yu3, yu2)


VMEM_LIMIT = 40 * 2**20
EXP_SCALE = math.log2(math.e) / math.sqrt(HD)


def norm_kernel(level_ref, hidden_ref, mod_ref, out_ref, gate_ref):
    values = hidden_ref[...].astype(jnp.float32)
    row = pl.ds(level_ref[0] % MOD_ROWS, 1)
    center = values - jnp.mean(values, axis=-1, keepdims=True)
    spread = jnp.mean(center * center, axis=-1, keepdims=True)
    scaled = center * lax.rsqrt(spread + EPSILON)
    out_ref[...] = (scaled * (1.0 + mod_ref[1, row, :]) + mod_ref[0, row, :]).astype(jnp.bfloat16)
    gate_ref[...] = mod_ref[2, row, :]


MOD_ROWS = 8


def normalize(levels, rows, modulation):
    width = rows.shape[1]
    return pl.pallas_call(
        norm_kernel,
        grid_spec=pltpu.PrefetchScalarGridSpec(
            num_scalar_prefetch=1,
            grid=(1,),
            in_specs=[
                pl.BlockSpec(rows.shape, lambda i, s: (0, 0)),
                pl.BlockSpec((3, MOD_ROWS, width), lambda i, s: (0, s[0] // MOD_ROWS, 0)),
            ],
            out_specs=[
                pl.BlockSpec(rows.shape, lambda i, s: (0, 0)),
                pl.BlockSpec((1, width), lambda i, s: (0, 0)),
            ],
        ),
        out_shape=[
            jax.ShapeDtypeStruct(rows.shape, jnp.bfloat16),
            jax.ShapeDtypeStruct((1, width), jnp.float32),
        ],
        name="normalize",
    )(levels, rows, modulation.transpose(1, 0, 2))


def latent_kernel(w_ref, gate_ref, lw_ref, o_ref):
    gated = w_ref[...].astype(jnp.float32) * gate_ref[...]
    hi = gated.astype(jnp.bfloat16)
    lo = (gated - hi.astype(jnp.float32)).astype(jnp.bfloat16)
    out = dot_t(hi, lw_ref[...]) + dot_t(lo, lw_ref[...])
    top = out.astype(jnp.bfloat16)
    o_ref[: w_ref.shape[0], :] = top
    o_ref[w_ref.shape[0] :, :] = (out - top.astype(jnp.float32)).astype(jnp.bfloat16)


def latent_matrix(w, gate_row, latent_weight):
    pv = latent_weight.shape[1]
    return pl.pallas_call(
        latent_kernel,
        out_shape=jax.ShapeDtypeStruct((2 * w.shape[0], pv), jnp.bfloat16),
        compiler_params=pltpu.CompilerParams(vmem_limit_bytes=VMEM_LIMIT),
        name="latent_matrix",
    )(w, gate_row, latent_weight.T)


def project_kernel(*refs):
    blocks, (own_ref, oth_ref, mine_ref, theirs_ref, rows) = refs[:NZ], refs[NZ:]
    for i, block in enumerate(blocks):
        rows[i * BLK : i * BLK + BLK, :] = block[...]
    for w_ref, o_ref in ((oth_ref, theirs_ref), (own_ref, mine_ref)):
        out = jnp.dot(rows[...], w_ref[...], preferred_element_type=jnp.float32)
        o_ref[:, :HD] = (out[:, :HD] * EXP_SCALE).astype(jnp.bfloat16)
        o_ref[:, HD:] = out[:, HD:].astype(jnp.bfloat16)


def project(blocks, w_own, w_oth):
    width, cols = w_own.shape
    rows = len(blocks) * BLK
    vmem = pl.BlockSpec(memory_space=pltpu.VMEM)
    return pl.pallas_call(
        project_kernel,
        in_specs=[vmem] * (len(blocks) + 2),
        out_specs=[vmem, vmem],
        out_shape=[jax.ShapeDtypeStruct((rows, cols), jnp.bfloat16)] * 2,
        scratch_shapes=[pltpu.VMEM((rows, width), jnp.bfloat16)],
        compiler_params=pltpu.CompilerParams(vmem_limit_bytes=VMEM_LIMIT),
        cost_estimate=pl.CostEstimate(
            flops=4 * rows * width * cols,
            bytes_accessed=4 * width * cols + 2 * rows * width,
            transcendentals=0,
        ),
        name="project",
    )(*blocks, w_own, w_oth)


def dot_t(a, b):
    return lax.dot_general(a, b, (((1,), (1,)), ((), ())), preferred_element_type=jnp.float32)


TILE = 128


def used_slots(y, z):
    return (y * NZ + z) * NC < HEADS


def self_kernel(s_ref, q_ref, kv_ref, m_ref, o_ref, values):
    y, z, core = s_ref[1], s_ref[2], s_ref[3]
    used = used_slots(y, z)
    values[:, :HD] = kv_ref[:, HD:]
    values[:, HD:] = jnp.ones((values.shape[0], HD), jnp.bfloat16)
    for t in range(q_ref.shape[0] // TILE):
        s = dot_t(q_ref[t * TILE : t * TILE + TILE, :], kv_ref[:, :HD])
        p = jnp.exp2(s - jnp.max(s, axis=1, keepdims=True)).astype(jnp.bfloat16)
        acc = jnp.dot(p, values[...], preferred_element_type=jnp.float32)
        att = (acc[:, :HD] / acc[:, HD:]).astype(jnp.bfloat16)
        att = jnp.concatenate([att, att], axis=1)
        part = jnp.dot(att, m_ref[...], preferred_element_type=jnp.float32)
        part = jnp.where(used, part, 0.0).astype(jnp.bfloat16)
        for j in range(TILE // BLK):
            y_apart, core_apart, d = block_of(t * (TILE // BLK) + j)
            at = ((core ^ core_apart) * NY + (y ^ y_apart)) * NZ + (z + d) % NZ
            o_ref[at] = part[j * BLK : j * BLK + BLK]


def self_attention(place, q, kv, matrix):
    pv = matrix.shape[1]
    rows = q.shape[0]
    return pl.pallas_call(
        self_kernel,
        grid_spec=pltpu.PrefetchScalarGridSpec(
            num_scalar_prefetch=1,
            grid=(1,),
            in_specs=[pl.BlockSpec(a.shape, lambda i, s: (0, 0)) for a in (q, kv, matrix)],
            out_specs=pl.BlockSpec((rows // BLK, BLK, pv), lambda i, s: (0, 0, 0)),
            scratch_shapes=[pltpu.VMEM((rows, 2 * HD), jnp.bfloat16)],
        ),
        out_shape=jax.ShapeDtypeStruct((rows // BLK, BLK, pv), jnp.bfloat16),
        compiler_params=pltpu.CompilerParams(vmem_limit_bytes=VMEM_LIMIT),
        cost_estimate=pl.CostEstimate(
            flops=6 * rows * rows * HD, bytes_accessed=2**20, transcendentals=rows * rows
        ),
        name="self_attention",
    )(place, q, kv, matrix)


def visit(refs, q, keys, values, acc, top):
    at = 0
    for ref in refs:
        n = ref.shape[0]
        keys[at : at + n, :] = ref[:, :HD]
        values[at : at + n, :HD] = ref[:, HD:]
        at += n
    for t in range(q.shape[0] // TILE):
        rows = slice(t * TILE, t * TILE + TILE)
        s = dot_t(q[rows, :], keys[...])
        old = top[rows, :1]
        new = jnp.maximum(old, jnp.max(s, axis=1, keepdims=True))
        p = jnp.exp2(s - new).astype(jnp.bfloat16)
        acc[rows, :] = acc[rows, :] * jnp.exp2(old - new) + jnp.dot(
            p, values[...], preferred_element_type=jnp.float32
        )
        top[rows, :] = jnp.broadcast_to(new, (TILE, 128))


def sees(order_ref, s_ref, dh, dx):
    x, h = s_ref[4], s_ref[0]
    mine = order_ref[x * NH + (h ^ dh)]
    return order_ref[((x + dx) % NX) * NH + h] <= mine


def near_kernel(counts, order_ref, s_ref, qa_ref, qb_ref, *refs):
    blocks, (acc_ref, top_ref, q, keys, values) = refs[: sum(counts)], refs[sum(counts) :]
    dh = pl.program_id(0)
    q[...] = jnp.where(dh == 0, qa_ref[...], qb_ref[...])
    values[:, HD:] = jnp.ones((values.shape[0], HD), jnp.bfloat16)
    acc_ref[...] = jnp.zeros_like(acc_ref)
    top_ref[...] = jnp.full_like(top_ref, -NEG_LARGE)
    at = 0
    for count, dx in zip(counts, (0, NX - 1, 1)):
        unit = blocks[at : at + count]
        at += count
        pl.when(sees(order_ref, s_ref, dh, dx))(
            functools.partial(visit, unit, q, keys, values, acc_ref.at[0], top_ref.at[0])
        )


def far_kernel(order_ref, s_ref, qa_ref, qb_ref, acc_in, top_in, *refs):
    blocks, (o_ref, q, keys, values, acc, top) = refs[:-6], refs[-6:]
    dh = pl.program_id(0)
    q[...] = jnp.where(dh == 0, qa_ref[...], qb_ref[...])
    values[:, HD:] = jnp.ones((values.shape[0], HD), jnp.bfloat16)
    acc[...] = acc_in[0]
    top[...] = top_in[0]
    pl.when(sees(order_ref, s_ref, dh, 2))(
        functools.partial(visit, blocks, q, keys, values, acc, top)
    )
    y, core = s_ref[1], s_ref[3]
    for quarter in range(4):
        starts = [block_at(quarter // 2, quarter % 2, d) * BLK for d in range(NZ)]
        gather = lambda ref, cols: jnp.concatenate([ref[i : i + BLK, cols] for i in starts], axis=0)
        total = gather(acc, slice(HD, 2 * HD))
        some = total > 0.0
        safe = jnp.where(some, total, 1.0)
        at = quarter ^ (y * 2 + core)
        o_ref[at, :QUARTER, :] = (gather(acc, slice(0, HD)) / safe).astype(jnp.bfloat16)
        lse = jnp.where(some, gather(top, slice(0, 128)) + jnp.log2(safe), -NEG_LARGE)
        row = lse.T[0:1, :]
        row = jnp.concatenate([row[:, :128], row[:, 128:]], axis=0)
        hi = row.astype(jnp.bfloat16).astype(jnp.float32)
        rest = row - hi
        mid = rest.astype(jnp.bfloat16).astype(jnp.float32)
        pad = jnp.zeros((TAIL - 6, 128), jnp.float32)
        o_ref[at, QUARTER:, :] = jnp.concatenate([hi, mid, rest - mid, pad], axis=0).astype(
            jnp.bfloat16
        )


def whole(a):
    return pl.BlockSpec(a.shape, lambda i, *s: (0,) * a.ndim)


def attention_cost(units, rows):
    pairs = 2 * units * rows * rows
    return pl.CostEstimate(flops=6 * pairs * HD, bytes_accessed=4 * 2**20, transcendentals=pairs)


def near_attention(order, place, qa, qb, units):
    rows = qa.shape[0]
    blocks = [b for unit in units for b in unit]
    out = lambda cols: pl.BlockSpec((1, rows, cols), lambda i, *s: (i, 0, 0))
    return pl.pallas_call(
        functools.partial(near_kernel, [len(unit) for unit in units]),
        grid_spec=pltpu.PrefetchScalarGridSpec(
            num_scalar_prefetch=2,
            grid=(NH,),
            in_specs=[whole(a) for a in (qa, qb, *blocks)],
            out_specs=[out(2 * HD), out(128)],
            scratch_shapes=[
                pltpu.VMEM((rows, HD), jnp.bfloat16),
                pltpu.VMEM((rows, HD), jnp.bfloat16),
                pltpu.VMEM((rows, 2 * HD), jnp.bfloat16),
            ],
        ),
        out_shape=[
            jax.ShapeDtypeStruct((NH, rows, 2 * HD), jnp.float32),
            jax.ShapeDtypeStruct((NH, rows, 128), jnp.float32),
        ],
        compiler_params=pltpu.CompilerParams(vmem_limit_bytes=VMEM_LIMIT),
        cost_estimate=attention_cost(3, rows),
        name="near_attention",
    )(order, place, qa, qb, *blocks)


def far_attention(order, place, qa, qb, acc, top, blocks):
    rows = qa.shape[0]
    chunk = QUARTER + TAIL
    part = lambda a: pl.BlockSpec((1,) + a.shape[1:], lambda i, *s: (i, 0, 0))
    return pl.pallas_call(
        far_kernel,
        grid_spec=pltpu.PrefetchScalarGridSpec(
            num_scalar_prefetch=2,
            grid=(NH,),
            in_specs=[whole(qa), whole(qb), part(acc), part(top)] + [whole(b) for b in blocks],
            out_specs=pl.BlockSpec((4, chunk, HD), lambda i, o, s: (i ^ s[0], 0, 0)),
            scratch_shapes=[
                pltpu.VMEM((rows, HD), jnp.bfloat16),
                pltpu.VMEM((rows, HD), jnp.bfloat16),
                pltpu.VMEM((rows, 2 * HD), jnp.bfloat16),
                pltpu.VMEM((rows, 2 * HD), jnp.float32),
                pltpu.VMEM((rows, 128), jnp.float32),
            ],
        ),
        out_shape=jax.ShapeDtypeStruct((NH * 4, chunk, HD), jnp.bfloat16),
        compiler_params=pltpu.CompilerParams(vmem_limit_bytes=VMEM_LIMIT),
        cost_estimate=attention_cost(1, rows),
        name="far_attention",
    )(order, place, qa, qb, acc, top, *blocks)


def join_kernel(s_ref, in_ref, w0_ref, w1_ref, w2_ref, w3_ref, o_ref, a_ref, w_ref):
    h, y, z, core = s_ref[0], s_ref[1], s_ref[2], s_ref[3]
    place = h * 4 + y * 2 + core

    @pl.when(pl.program_id(0) == 0)
    def _():
        for r in range(4):
            used = used_slots(y ^ (r // 2), z)
            parts = []
            for dh in range(NH):
                at = (dh * 4 + r) ^ place
                rows = in_ref[at, QUARTER:, :].astype(jnp.float32)
                parts.append((at, rows[0:2] + rows[2:4] + rows[4:6]))
            top = jnp.maximum(parts[0][1], parts[1][1])
            e = [jnp.exp2(lse - top) for _, lse in parts]
            norm = e[0] + e[1]
            for half in range(2):
                out = None
                for (at, _), weight in zip(parts, e):
                    w = jnp.where(used, weight / norm, 0.0)[half : half + 1, :]
                    col = jnp.broadcast_to(w, (128, 128)).T
                    term = in_ref[at, half * 128 : half * 128 + 128, :].astype(jnp.float32) * col
                    out = term if out is None else out + term
                out = out.astype(jnp.bfloat16)
                for j in range(4):
                    start = pl.multiple_of(((z + half * 4 + j) % NZ) * BLK, BLK)
                    a_ref[pl.ds(start, BLK), r * HD : r * HD + HD] = out[j * BLK : j * BLK + BLK]

    for r, ref in enumerate((w0_ref, w1_ref, w2_ref, w3_ref)):
        w_ref[r * HD : r * HD + HD, :] = ref[...]
    o_ref[...] = jnp.dot(a_ref[...], w_ref[...], preferred_element_type=jnp.float32).astype(
        jnp.bfloat16
    )


def join_heads(place, received, weights):
    width = weights[0].shape[1]
    step = width // 4
    return pl.pallas_call(
        join_kernel,
        grid_spec=pltpu.PrefetchScalarGridSpec(
            num_scalar_prefetch=1,
            grid=(4,),
            in_specs=[whole(received)] + [pl.BlockSpec((HD, step), lambda i, s: (0, i))] * 4,
            out_specs=pl.BlockSpec((QUARTER, step), lambda i, s: (0, i)),
            scratch_shapes=[
                pltpu.VMEM((QUARTER, 4 * HD), jnp.bfloat16),
                pltpu.VMEM((4 * HD, step), jnp.bfloat16),
            ],
        ),
        out_shape=jax.ShapeDtypeStruct((QUARTER, width), jnp.bfloat16),
        compiler_params=pltpu.CompilerParams(vmem_limit_bytes=VMEM_LIMIT),
        name="join_heads",
    )(place, received, *weights)


def decode(latents, root_kernel):
    seq_count = latents.shape[0]
    row_patches = seq_count // FR
    me = lax.axis_index("seq")
    ringed = jnp.concatenate([latents[-1:], latents, latents[:1]], axis=0)
    position = (me - row_patches // 2 + seq_count) % seq_count
    patch_row = position % row_patches
    frame_index = position // row_patches
    row_ids = jnp.arange(P_SIZE + 2, dtype=jnp.int32)
    keep = jnp.where(
        row_ids == 0,
        patch_row > 0,
        jnp.where(row_ids == P_SIZE + 1, patch_row < row_patches - 1, True),
    )
    width_cols = BLK * P_SIZE
    windows = []
    for lag in range(3):
        start = (me - lag * row_patches + seq_count) % seq_count
        three = lax.dynamic_slice_in_dim(ringed, start, 3, axis=0)
        slab = (
            three.reshape(3, BLK, P_SIZE, P_SIZE, C)
            .transpose(0, 2, 1, 3, 4)
            .reshape(3 * P_SIZE, width_cols, C)
        )[P_SIZE - 1 : 2 * P_SIZE + 1]
        ok = keep & (frame_index >= lag)
        slab = jnp.where(ok[:, None, None], slab, jnp.zeros_like(slab))
        framed = jnp.pad(slab, ((0, 0), (1, 1), (0, 0)))
        for row_off in range(3):
            for col_off in range(3):
                windows.append(framed[row_off : row_off + P_SIZE, col_off : col_off + width_cols])
    stacked = jnp.concatenate(windows, axis=-1).reshape(P_SIZE * width_cols, 27 * C)
    decoded = jnp.dot(stacked, root_kernel, preferred_element_type=jnp.float32)
    return decoded.reshape(P_SIZE, width_cols, root_kernel.shape[1]).astype(jnp.bfloat16)[None]


def after(value, earlier):
    return lax.optimization_barrier((value, earlier))[0]


def per_device(
    hidden, levels, span_order, modulation, in_weight, out_weight, latent_weight, decoder_weight
):
    span_me = lax.axis_index("span")
    seq_me = lax.axis_index("seq")
    x, h = span_me // NH, span_me % NH
    y, z, core = seq_me // (NZ * NC), (seq_me // NC) % NZ, seq_me % NC
    place = jnp.stack([h, y, z, core, x])
    pv = latent_weight.shape[1]
    seq_count = NY * NZ * NC

    normed, gate_row = normalize(levels, hidden[0], modulation)
    w_own = in_weight[0]
    own_blocks, other_blocks = gather_class(normed)
    w_oth = move_core(w_own)
    mine_a, theirs_a = project(own_blocks, w_own, w_oth)
    mine_b, theirs_b = project(other_blocks, w_own, w_oth)
    triples = jnp.concatenate([mine_a, move_core(theirs_a), mine_b, move_core(theirs_b)], axis=0)
    q = triples[:, :HD]
    kv = triples[:, HD:]

    half = kv.shape[0] // 2
    kv_up, kv_dn = move_x(kv, 1), move_x(kv, -1)
    q_hi = move_hi(q)
    kv_far = (move_x(kv_up[:half], 1), move_x(kv_dn[half:], -1))

    part = self_attention(place, q, kv, latent_matrix(out_weight[0], gate_row, latent_weight))

    out_w = after(out_weight[0], q_hi)
    q_hi = after(q_hi, part)
    w_core, w_far = move_core(out_w), move_y(out_w)
    weights = (out_w, w_core, w_far, move_core(w_far))

    acc, top = near_attention(span_order, place, q, q_hi, ((kv,), (kv_up,), (kv_dn,)))
    chunks = far_attention(span_order, place, q, q_hi, acc, top, kv_far)
    groups = [
        [
            span_at(i, hh) * seq_count + seq_at(yy, j, cc)
            for hh in range(NH)
            for yy in range(NY)
            for cc in range(NC)
        ]
        for i in range(NX)
        for j in range(NZ)
    ]
    received = lax.all_to_all(
        chunks, ("span", "seq"), 0, 0, tiled=True, axis_index_groups=groups
    )
    part = after(halve(part, core, move_core), chunks)
    part = halve(part, y, move_y)
    part = halve(part, z // 4, lambda a: swap_z(a, 4))
    part = halve(part, z // 2 % 2, lambda a: swap_z(a, 2))
    part = halve(part, z % 2, lambda a: swap_z(a, 1))
    partial = join_heads(place, received, weights)
    z_groups = [[seq_at(yy, j, cc) for j in range(NZ)] for yy in range(NY) for cc in range(NC)]
    summed = lax.psum_scatter(
        partial, "seq", scatter_dimension=0, tiled=True, axis_index_groups=z_groups
    ).astype(jnp.float32)
    block_out = (hidden[0].astype(jnp.float32) + gate_row * summed).astype(jnp.bfloat16)[None]

    own_latents = jnp.dot(hidden[0], latent_weight, preferred_element_type=jnp.float32)
    latents = (part[0].astype(jnp.float32) + own_latents).astype(jnp.bfloat16)
    group_ids = jnp.arange(span_order.shape[0], dtype=jnp.int32)
    root = jnp.sum(jnp.where(span_order == 0, group_ids, 0))
    spread = lax.all_to_all(
        jnp.broadcast_to(latents[None], (NX * NH, BLK, pv)), "span", 0, 0, tiled=True
    )
    latents = lax.dynamic_index_in_dim(spread, root, 0, keepdims=True)
    every = lax.all_to_all(
        jnp.broadcast_to(latents, (seq_count, BLK, pv)), "seq", 0, 0, tiled=True
    )
    decoded = decode(every, decoder_weight.reshape(27 * C, decoder_weight.shape[4]))
    return (block_out, decoded)


def solution(mesh):
    placed = (
        P("span", "seq", None),
        P("span"),
        P(),
        P(),
        P("seq", None, None),
        P("seq", None, None),
        P(),
        P(None, None, None, None, "span"),
    )
    return jax.shard_map(
        per_device,
        mesh=mesh,
        in_specs=placed,
        out_specs=(P("span", "seq", None), P("seq", None, None, "span")),
        check_vma=False,
    )
```

```python
import functools
import math

import jax
import jax.numpy as jnp
from jax import lax
from jax.experimental import pallas as pl
from jax.experimental.pallas import tpu as pltpu
from jax.sharding import PartitionSpec as P

HEADS = 24
FR = 4
P_SIZE = 2
C = 16
HD = 128

EPSILON = 1e-06
NEG_LARGE = 1e30

NX, NH, NY, NZ, NC = 4, 2, 2, 8, 2
BLK = 32
QUARTER = NZ * BLK
TAIL = 16


def seq_at(y, z, c):
    return ((y % NY) * NZ + z % NZ) * NC + c % NC


def span_at(x, h):
    return (x % NX) * NH + h % NH


def seq_route(dy=0, dz=0, dc=0):
    return [
        (seq_at(y, z, c), seq_at(y + dy, z + dz, c + dc))
        for y in range(NY)
        for z in range(NZ)
        for c in range(NC)
    ]


def span_route(dx=0, dh=0):
    return [(span_at(x, h), span_at(x + dx, h + dh)) for x in range(NX) for h in range(NH)]


def move_z(a, d):
    return lax.ppermute(a, "seq", seq_route(dz=d))


def move_y(a):
    return lax.ppermute(a, "seq", seq_route(dy=1))


def move_core(a):
    return lax.ppermute(a, "seq", seq_route(dc=1))


def move_x(a, d):
    return lax.ppermute(a, "span", span_route(dx=d))


def move_hi(a):
    return lax.ppermute(a, "span", span_route(dh=1))


HALVES = (
    ((0, 0), (0, 1), (0, 2), (0, 6), (0, 7), (1, 0), (1, 1), (1, 7)),
    ((0, 3), (0, 4), (0, 5), (1, 2), (1, 3), (1, 4), (1, 5), (1, 6)),
)


def block_at(y_apart, core_apart, d):
    half = 0 if (y_apart, d) in HALVES[0] else 1
    return half * 2 * NZ + core_apart * NZ + HALVES[half].index((y_apart, d))


def block_of(at):
    half, core_apart, i = at // (2 * NZ), at // NZ % 2, at % NZ
    y_apart, d = HALVES[half][i]
    return y_apart, core_apart, d


def gather_class(b):
    up1, dn1, y0 = move_z(b, 1), move_z(b, -1), move_y(b)
    up2, dn2 = move_z(up1, 1), move_z(dn1, -1)
    yu1, yd1 = move_y(up1), move_y(dn1)
    up3, dn3 = move_z(up2, 1), move_z(dn2, -1)
    yu2, yd2 = move_y(up2), move_y(dn2)
    far = move_z(up3, 1)
    yu3, yd3 = move_z(yu2, 1), move_z(yd2, -1)
    yfar = lax.ppermute(dn3, "seq", seq_route(dy=1, dz=-1))
    return (b, dn1, dn2, up2, up1, y0, yd1, yu1), (dn3, far, up3, yd2, yd3, yfar, yu3, yu2)


EXP_SCALE = math.log2(math.e) / math.sqrt(HD)


def norm_kernel(level_ref, hidden_ref, mod_ref, out_ref, gate_ref):
    values = hidden_ref[...].astype(jnp.float32)
    row = pl.ds(level_ref[0] % MOD_ROWS, 1)
    center = values - jnp.mean(values, axis=-1, keepdims=True)
    spread = jnp.mean(center * center, axis=-1, keepdims=True)
    scaled = center * lax.rsqrt(spread + EPSILON)
    out_ref[...] = (scaled * (1.0 + mod_ref[1, row, :]) + mod_ref[0, row, :]).astype(jnp.bfloat16)
    gate_ref[...] = mod_ref[2, row, :]


MOD_ROWS = 8


def normalize(levels, rows, modulation):
    width = rows.shape[1]
    return pl.pallas_call(
        norm_kernel,
        grid_spec=pltpu.PrefetchScalarGridSpec(
            num_scalar_prefetch=1,
            grid=(1,),
            in_specs=[
                pl.BlockSpec(rows.shape, lambda i, s: (0, 0)),
                pl.BlockSpec((3, MOD_ROWS, width), lambda i, s: (0, s[0] // MOD_ROWS, 0)),
            ],
            out_specs=[
                pl.BlockSpec(rows.shape, lambda i, s: (0, 0)),
                pl.BlockSpec((1, width), lambda i, s: (0, 0)),
            ],
        ),
        out_shape=[
            jax.ShapeDtypeStruct(rows.shape, jnp.bfloat16),
            jax.ShapeDtypeStruct((1, width), jnp.float32),
        ],
        name="normalize",
    )(levels, rows, modulation.transpose(1, 0, 2))


def latent_kernel(w_ref, gate_ref, lw_ref, o_ref):
    gated = w_ref[...].astype(jnp.float32) * gate_ref[...]
    hi = gated.astype(jnp.bfloat16)
    lo = (gated - hi.astype(jnp.float32)).astype(jnp.bfloat16)
    out = dot_t(hi, lw_ref[...]) + dot_t(lo, lw_ref[...])
    top = out.astype(jnp.bfloat16)
    o_ref[: w_ref.shape[0], :] = top
    o_ref[w_ref.shape[0] :, :] = (out - top.astype(jnp.float32)).astype(jnp.bfloat16)


def latent_matrix(w, gate_row, latent_weight):
    pv = latent_weight.shape[1]
    return pl.pallas_call(
        latent_kernel,
        out_shape=jax.ShapeDtypeStruct((2 * w.shape[0], pv), jnp.bfloat16),
        compiler_params=pltpu.CompilerParams(vmem_limit_bytes=16 * 2**20),
        name="latent_matrix",
    )(w, gate_row, latent_weight.T)


def project_kernel(*refs):
    blocks, (own_ref, oth_ref, mine_ref, theirs_ref, rows) = refs[:NZ], refs[NZ:]
    for i, block in enumerate(blocks):
        rows[i * BLK : i * BLK + BLK, :] = block[...]
    for w_ref, o_ref in ((oth_ref, theirs_ref), (own_ref, mine_ref)):
        out = jnp.dot(rows[...], w_ref[...], preferred_element_type=jnp.float32)
        o_ref[:, :HD] = (out[:, :HD] * EXP_SCALE).astype(jnp.bfloat16)
        o_ref[:, HD:] = out[:, HD:].astype(jnp.bfloat16)


def project(blocks, w_own, w_oth):
    width, cols = w_own.shape
    rows = len(blocks) * BLK
    vmem = pl.BlockSpec(memory_space=pltpu.VMEM)
    return pl.pallas_call(
        project_kernel,
        in_specs=[vmem] * (len(blocks) + 2),
        out_specs=[vmem, vmem],
        out_shape=[jax.ShapeDtypeStruct((rows, cols), jnp.bfloat16)] * 2,
        scratch_shapes=[pltpu.VMEM((rows, width), jnp.bfloat16)],
        compiler_params=pltpu.CompilerParams(vmem_limit_bytes=16 * 2**20),
        cost_estimate=pl.CostEstimate(
            flops=4 * rows * width * cols,
            bytes_accessed=4 * width * cols + 2 * rows * width,
            transcendentals=0,
        ),
        name="project",
    )(*blocks, w_own, w_oth)


def dot_t(a, b):
    return lax.dot_general(a, b, (((1,), (1,)), ((), ())), preferred_element_type=jnp.float32)


TILE = 128


def used_slots(y, z):
    return (y * NZ + z) * NC < HEADS


def self_kernel(s_ref, q_ref, kv_ref, m_ref, o_ref, values):
    y, z, core = s_ref[1], s_ref[2], s_ref[3]
    used = used_slots(y, z)
    values[:, :HD] = kv_ref[:, HD:]
    values[:, HD:] = jnp.ones((values.shape[0], HD), jnp.bfloat16)
    for t in range(q_ref.shape[0] // TILE):
        s = dot_t(q_ref[t * TILE : t * TILE + TILE, :], kv_ref[:, :HD])
        p = jnp.exp2(s - jnp.max(s, axis=1, keepdims=True)).astype(jnp.bfloat16)
        acc = jnp.dot(p, values[...], preferred_element_type=jnp.float32)
        att = (acc[:, :HD] / acc[:, HD:]).astype(jnp.bfloat16)
        att = jnp.concatenate([att, att], axis=1)
        part = jnp.dot(att, m_ref[...], preferred_element_type=jnp.float32)
        part = jnp.where(used, part, 0.0).astype(jnp.bfloat16)
        for j in range(TILE // BLK):
            y_apart, core_apart, d = block_of(t * (TILE // BLK) + j)
            at = ((y ^ y_apart) * NZ + (z + d) % NZ) * NC + (core ^ core_apart)
            o_ref[at] = part[j * BLK : j * BLK + BLK]


def self_attention(place, q, kv, matrix):
    pv = matrix.shape[1]
    rows = q.shape[0]
    return pl.pallas_call(
        self_kernel,
        grid_spec=pltpu.PrefetchScalarGridSpec(
            num_scalar_prefetch=1,
            grid=(1,),
            in_specs=[pl.BlockSpec(a.shape, lambda i, s: (0, 0)) for a in (q, kv, matrix)],
            out_specs=pl.BlockSpec((rows // BLK, BLK, pv), lambda i, s: (0, 0, 0)),
            scratch_shapes=[pltpu.VMEM((rows, 2 * HD), jnp.bfloat16)],
        ),
        out_shape=jax.ShapeDtypeStruct((rows // BLK, BLK, pv), jnp.bfloat16),
        compiler_params=pltpu.CompilerParams(vmem_limit_bytes=16 * 2**20),
        cost_estimate=pl.CostEstimate(
            flops=6 * rows * rows * HD, bytes_accessed=2**20, transcendentals=rows * rows
        ),
        name="self_attention",
    )(place, q, kv, matrix)


def visit(kv_ref, q, values, acc, top):
    values[:, :HD] = kv_ref[:, HD:]
    values[:, HD:] = jnp.ones((values.shape[0], HD), jnp.bfloat16)
    for t in range(q.shape[0] // TILE):
        rows = slice(t * TILE, t * TILE + TILE)
        s = dot_t(q[rows, :], kv_ref[:, :HD])
        old = top[rows, :1]
        new = jnp.maximum(old, jnp.max(s, axis=1, keepdims=True))
        p = jnp.exp2(s - new).astype(jnp.bfloat16)
        acc[rows, :] = acc[rows, :] * jnp.exp2(old - new) + jnp.dot(
            p, values[...], preferred_element_type=jnp.float32
        )
        top[rows, :] = jnp.broadcast_to(new, (TILE, 128))


def sees(order_ref, s_ref, dh, dx):
    x, h = s_ref[4], s_ref[0]
    mine = order_ref[x * NH + (h ^ dh)]
    return order_ref[((x + dx) % NX) * NH + h] <= mine


def own_kernel(order_ref, s_ref, qa_ref, qb_ref, kv_ref, acc_ref, top_ref, q, values):
    dh = pl.program_id(0)
    q[...] = jnp.where(dh == 0, qa_ref[...], qb_ref[...])
    acc_ref[...] = jnp.zeros_like(acc_ref)
    top_ref[...] = jnp.full_like(top_ref, -NEG_LARGE)
    pl.when(sees(order_ref, s_ref, dh, 0))(
        functools.partial(visit, kv_ref, q, values, acc_ref.at[0], top_ref.at[0])
    )


def other_kernel(order_ref, s_ref, qa_ref, qb_ref, acc_in, top_in, k1, k2, k3, o_ref, *scratch):
    q, values, acc, top = scratch
    dh = pl.program_id(0)
    q[...] = jnp.where(dh == 0, qa_ref[...], qb_ref[...])
    acc[...] = acc_in[0]
    top[...] = top_in[0]
    for dx, ref in ((NX - 1, k1), (1, k2), (2, k3)):
        pl.when(sees(order_ref, s_ref, dh, dx))(
            functools.partial(visit, ref, q, values, acc, top)
        )
    y, core = s_ref[1], s_ref[3]
    for quarter in range(4):
        starts = [block_at(quarter // 2, quarter % 2, d) * BLK for d in range(NZ)]
        gather = lambda ref, cols: jnp.concatenate([ref[i : i + BLK, cols] for i in starts], axis=0)
        total = gather(acc, slice(HD, 2 * HD))
        some = total > 0.0
        safe = jnp.where(some, total, 1.0)
        at = quarter ^ (y * 2 + core)
        o_ref[at, :QUARTER, :] = (gather(acc, slice(0, HD)) / safe).astype(jnp.bfloat16)
        lse = jnp.where(some, gather(top, slice(0, 128)) + jnp.log2(safe), -NEG_LARGE)
        row = lse.T[0:1, :]
        row = jnp.concatenate([row[:, :128], row[:, 128:]], axis=0)
        hi = row.astype(jnp.bfloat16).astype(jnp.float32)
        rest = row - hi
        mid = rest.astype(jnp.bfloat16).astype(jnp.float32)
        pad = jnp.zeros((TAIL - 6, 128), jnp.float32)
        o_ref[at, QUARTER:, :] = jnp.concatenate([hi, mid, rest - mid, pad], axis=0).astype(
            jnp.bfloat16
        )


def whole(a):
    return pl.BlockSpec(a.shape, lambda i, *s: (0,) * a.ndim)


def attention_cost(units, rows):
    pairs = 2 * units * rows * rows
    return pl.CostEstimate(flops=6 * pairs * HD, bytes_accessed=4 * 2**20, transcendentals=pairs)


def own_attention(order, place, qa, qb, kv):
    rows = qa.shape[0]
    out = lambda cols: pl.BlockSpec((1, rows, cols), lambda i, *s: (i, 0, 0))
    return pl.pallas_call(
        own_kernel,
        grid_spec=pltpu.PrefetchScalarGridSpec(
            num_scalar_prefetch=2,
            grid=(NH,),
            in_specs=[whole(a) for a in (qa, qb, kv)],
            out_specs=[out(2 * HD), out(128)],
            scratch_shapes=[
                pltpu.VMEM((rows, HD), jnp.bfloat16),
                pltpu.VMEM((rows, 2 * HD), jnp.bfloat16),
            ],
        ),
        out_shape=[
            jax.ShapeDtypeStruct((NH, rows, 2 * HD), jnp.float32),
            jax.ShapeDtypeStruct((NH, rows, 128), jnp.float32),
        ],
        compiler_params=pltpu.CompilerParams(vmem_limit_bytes=20 * 2**20),
        cost_estimate=attention_cost(1, rows),
        name="own_attention",
    )(order, place, qa, qb, kv)


def other_attention(order, place, qa, qb, acc, top, blocks):
    rows = qa.shape[0]
    chunk = QUARTER + TAIL
    part = lambda a: pl.BlockSpec((1,) + a.shape[1:], lambda i, *s: (i, 0, 0))
    return pl.pallas_call(
        other_kernel,
        grid_spec=pltpu.PrefetchScalarGridSpec(
            num_scalar_prefetch=2,
            grid=(NH,),
            in_specs=[whole(qa), whole(qb), part(acc), part(top)] + [whole(b) for b in blocks],
            out_specs=pl.BlockSpec((4, chunk, HD), lambda i, o, s: (i ^ s[0], 0, 0)),
            scratch_shapes=[
                pltpu.VMEM((rows, HD), jnp.bfloat16),
                pltpu.VMEM((rows, 2 * HD), jnp.bfloat16),
                pltpu.VMEM((rows, 2 * HD), jnp.float32),
                pltpu.VMEM((rows, 128), jnp.float32),
            ],
        ),
        out_shape=jax.ShapeDtypeStruct((NH * 4, chunk, HD), jnp.bfloat16),
        compiler_params=pltpu.CompilerParams(vmem_limit_bytes=24 * 2**20),
        cost_estimate=attention_cost(3, rows),
        name="other_attention",
    )(order, place, qa, qb, acc, top, *blocks)


def join_kernel(s_ref, in_ref, w0_ref, w1_ref, w2_ref, w3_ref, o_ref, a_ref, w_ref):
    h, y, z, core = s_ref[0], s_ref[1], s_ref[2], s_ref[3]
    place = h * 4 + y * 2 + core

    @pl.when(pl.program_id(0) == 0)
    def _():
        for r in range(4):
            used = used_slots(y ^ (r // 2), z)
            parts = []
            for dh in range(NH):
                at = (dh * 4 + r) ^ place
                rows = in_ref[at, QUARTER:, :].astype(jnp.float32)
                parts.append((at, rows[0:2] + rows[2:4] + rows[4:6]))
            top = jnp.maximum(parts[0][1], parts[1][1])
            e = [jnp.exp2(lse - top) for _, lse in parts]
            norm = e[0] + e[1]
            for half in range(2):
                out = None
                for (at, _), weight in zip(parts, e):
                    w = jnp.where(used, weight / norm, 0.0)[half : half + 1, :]
                    col = jnp.broadcast_to(w, (128, 128)).T
                    term = in_ref[at, half * 128 : half * 128 + 128, :].astype(jnp.float32) * col
                    out = term if out is None else out + term
                out = out.astype(jnp.bfloat16)
                for j in range(4):
                    start = pl.multiple_of(((z + half * 4 + j) % NZ) * BLK, BLK)
                    a_ref[pl.ds(start, BLK), r * HD : r * HD + HD] = out[j * BLK : j * BLK + BLK]

    for r, ref in enumerate((w0_ref, w1_ref, w2_ref, w3_ref)):
        w_ref[r * HD : r * HD + HD, :] = ref[...]
    o_ref[...] = jnp.dot(a_ref[...], w_ref[...], preferred_element_type=jnp.float32).astype(
        jnp.bfloat16
    )


def join_heads(place, received, weights):
    width = weights[0].shape[1]
    step = width // 4
    return pl.pallas_call(
        join_kernel,
        grid_spec=pltpu.PrefetchScalarGridSpec(
            num_scalar_prefetch=1,
            grid=(4,),
            in_specs=[whole(received)] + [pl.BlockSpec((HD, step), lambda i, s: (0, i))] * 4,
            out_specs=pl.BlockSpec((QUARTER, step), lambda i, s: (0, i)),
            scratch_shapes=[
                pltpu.VMEM((QUARTER, 4 * HD), jnp.bfloat16),
                pltpu.VMEM((4 * HD, step), jnp.bfloat16),
            ],
        ),
        out_shape=jax.ShapeDtypeStruct((QUARTER, width), jnp.bfloat16),
        compiler_params=pltpu.CompilerParams(vmem_limit_bytes=16 * 2**20),
        name="join_heads",
    )(place, received, *weights)


def decode(latents, root_kernel):
    seq_count = latents.shape[0]
    row_patches = seq_count // FR
    me = lax.axis_index("seq")
    ringed = jnp.concatenate([latents[-1:], latents, latents[:1]], axis=0)
    position = (me - row_patches // 2 + seq_count) % seq_count
    patch_row = position % row_patches
    frame_index = position // row_patches
    row_ids = jnp.arange(P_SIZE + 2, dtype=jnp.int32)
    keep = jnp.where(
        row_ids == 0,
        patch_row > 0,
        jnp.where(row_ids == P_SIZE + 1, patch_row < row_patches - 1, True),
    )
    width_cols = BLK * P_SIZE
    windows = []
    for lag in range(3):
        start = (me - lag * row_patches + seq_count) % seq_count
        three = lax.dynamic_slice_in_dim(ringed, start, 3, axis=0)
        slab = (
            three.reshape(3, BLK, P_SIZE, P_SIZE, C)
            .transpose(0, 2, 1, 3, 4)
            .reshape(3 * P_SIZE, width_cols, C)
        )[P_SIZE - 1 : 2 * P_SIZE + 1]
        ok = keep & (frame_index >= lag)
        slab = jnp.where(ok[:, None, None], slab, jnp.zeros_like(slab))
        framed = jnp.pad(slab, ((0, 0), (1, 1), (0, 0)))
        for row_off in range(3):
            for col_off in range(3):
                windows.append(framed[row_off : row_off + P_SIZE, col_off : col_off + width_cols])
    stacked = jnp.concatenate(windows, axis=-1).reshape(P_SIZE * width_cols, 27 * C)
    decoded = jnp.dot(stacked, root_kernel, preferred_element_type=jnp.float32)
    return decoded.reshape(P_SIZE, width_cols, root_kernel.shape[1]).astype(jnp.bfloat16)[None]


def after(value, earlier):
    return lax.optimization_barrier((value, earlier))[0]


def per_device(
    hidden, levels, span_order, modulation, in_weight, out_weight, latent_weight, decoder_weight
):
    span_me = lax.axis_index("span")
    seq_me = lax.axis_index("seq")
    x, h = span_me // NH, span_me % NH
    y, z, core = seq_me // (NZ * NC), (seq_me // NC) % NZ, seq_me % NC
    place = jnp.stack([h, y, z, core, x])
    pv = latent_weight.shape[1]
    seq_count = NY * NZ * NC

    normed, gate_row = normalize(levels, hidden[0], modulation)
    w_own = in_weight[0]
    own_blocks, other_blocks = gather_class(normed)
    w_oth = move_core(w_own)
    mine_a, theirs_a = project(own_blocks, w_own, w_oth)
    mine_b, theirs_b = project(other_blocks, w_own, w_oth)
    triples = jnp.concatenate([mine_a, move_core(theirs_a), mine_b, move_core(theirs_b)], axis=0)
    q = triples[:, :HD]
    kv = triples[:, HD:]

    others = tuple(move_x(kv, d) for d in (1, NX - 1, 2))
    q_hi = move_hi(q)

    matrix = latent_matrix(after(out_weight[0], mine_b), gate_row, latent_weight)
    part = self_attention(place, q, kv, matrix)
    part = lax.all_to_all(part, "seq", 0, 0, tiled=True)

    out_w = after(out_weight[0], mine_b)
    w_core, w_far = move_core(out_w), move_y(out_w)
    weights = (out_w, w_core, w_far, move_core(w_far))

    acc, top = own_attention(span_order, place, q, q_hi, kv)
    acc = after(acc, part)
    chunks = other_attention(span_order, place, q, q_hi, acc, top, others)
    groups = [
        [
            span_at(i, hh) * seq_count + seq_at(yy, j, cc)
            for hh in range(NH)
            for yy in range(NY)
            for cc in range(NC)
        ]
        for i in range(NX)
        for j in range(NZ)
    ]
    received = lax.all_to_all(
        chunks, ("span", "seq"), 0, 0, tiled=True, axis_index_groups=groups
    )
    partial = join_heads(place, received, weights)
    z_groups = [[seq_at(yy, j, cc) for j in range(NZ)] for yy in range(NY) for cc in range(NC)]
    part = after(part, partial)
    summed = lax.psum_scatter(
        partial, "seq", scatter_dimension=0, tiled=True, axis_index_groups=z_groups
    ).astype(jnp.float32)
    block_out = (hidden[0].astype(jnp.float32) + gate_row * summed).astype(jnp.bfloat16)[None]

    own_latents = jnp.dot(hidden[0], latent_weight, preferred_element_type=jnp.float32)
    latents = (jnp.sum(part.astype(jnp.float32), axis=0) + own_latents).astype(jnp.bfloat16)
    group_ids = jnp.arange(span_order.shape[0], dtype=jnp.int32)
    root = jnp.sum(jnp.where(span_order == 0, group_ids, 0))
    spread = lax.all_to_all(
        jnp.broadcast_to(latents[None], (NX * NH, BLK, pv)), "span", 0, 0, tiled=True
    )
    latents = lax.dynamic_index_in_dim(spread, root, 0, keepdims=True)
    every = lax.all_to_all(
        jnp.broadcast_to(latents, (seq_count, BLK, pv)), "seq", 0, 0, tiled=True
    )
    decoded = decode(every, decoder_weight.reshape(27 * C, decoder_weight.shape[4]))
    return (block_out, decoded)


def solution(mesh):
    placed = (
        P("span", "seq", None),
        P("span"),
        P(),
        P(),
        P("seq", None, None),
        P("seq", None, None),
        P(),
        P(None, None, None, None, "span"),
    )
    return jax.shard_map(
        per_device,
        mesh=mesh,
        in_specs=placed,
        out_specs=(P("span", "seq", None), P("seq", None, None, "span")),
        check_vma=False,
    )
```

```python
import functools
import math

import jax
import jax.numpy as jnp
from jax import lax
from jax.experimental import pallas as pl
from jax.experimental.pallas import tpu as pltpu
from jax.sharding import PartitionSpec as P

HEADS = 24
FR = 4
P_SIZE = 2
C = 16
HD = 128

EPSILON = 1e-06
NEG_LARGE = 1e30

NX, NH, NY, NZ, NC = 4, 2, 2, 8, 2
BLK = 32
QUARTER = NZ * BLK
TAIL = 16


def seq_at(y, z, c):
    return ((y % NY) * NZ + z % NZ) * NC + c % NC


def span_at(x, h):
    return (x % NX) * NH + h % NH


def seq_route(dy=0, dz=0, dc=0):
    return [
        (seq_at(y, z, c), seq_at(y + dy, z + dz, c + dc))
        for y in range(NY)
        for z in range(NZ)
        for c in range(NC)
    ]


def span_route(dx=0, dh=0):
    return [(span_at(x, h), span_at(x + dx, h + dh)) for x in range(NX) for h in range(NH)]


def move_z(a, d):
    return lax.ppermute(a, "seq", seq_route(dz=d))


def swap_z(a, k):
    route = [
        (seq_at(y, z, c), seq_at(y, z ^ k, c)) for y in range(NY) for z in range(NZ) for c in range(NC)
    ]
    return lax.ppermute(a, "seq", route)


def halve(part, bit, swap):
    order = part.reshape((2, part.shape[0] // 2) + part.shape[1:])
    keep = jnp.where(bit == 0, order[0], order[1])
    send = jnp.where(bit == 0, order[1], order[0])
    return (keep.astype(jnp.float32) + swap(send).astype(jnp.float32)).astype(part.dtype)


def move_y(a):
    return lax.ppermute(a, "seq", seq_route(dy=1))


def move_core(a):
    return lax.ppermute(a, "seq", seq_route(dc=1))


def move_x(a, d):
    return lax.ppermute(a, "span", span_route(dx=d))


def move_hi(a):
    return lax.ppermute(a, "span", span_route(dh=1))


HALVES = (
    ((0, 0), (0, 1), (0, 2), (0, 6), (0, 7), (1, 0), (1, 1), (1, 7)),
    ((0, 3), (0, 4), (0, 5), (1, 2), (1, 3), (1, 4), (1, 5), (1, 6)),
)


def block_at(y_apart, core_apart, d):
    half = 0 if (y_apart, d) in HALVES[0] else 1
    return half * 2 * NZ + core_apart * NZ + HALVES[half].index((y_apart, d))


def block_of(at):
    half, core_apart, i = at // (2 * NZ), at // NZ % 2, at % NZ
    y_apart, d = HALVES[half][i]
    return y_apart, core_apart, d


def gather_class(b):
    up1, dn1, y0 = move_z(b, 1), move_z(b, -1), move_y(b)
    up2, dn2 = move_z(up1, 1), move_z(dn1, -1)
    yu1, yd1 = move_y(up1), move_y(dn1)
    up3, dn3 = move_z(up2, 1), move_z(dn2, -1)
    yu2, yd2 = move_y(up2), move_y(dn2)
    far = move_z(up3, 1)
    yu3, yd3 = move_z(yu2, 1), move_z(yd2, -1)
    yfar = lax.ppermute(dn3, "seq", seq_route(dy=1, dz=-1))
    return (b, dn1, dn2, up2, up1, y0, yd1, yu1), (dn3, far, up3, yd2, yd3, yfar, yu3, yu2)


EXP_SCALE = math.log2(math.e) / math.sqrt(HD)


def norm_kernel(level_ref, hidden_ref, mod_ref, out_ref, gate_ref):
    values = hidden_ref[...].astype(jnp.float32)
    row = pl.ds(level_ref[0] % MOD_ROWS, 1)
    center = values - jnp.mean(values, axis=-1, keepdims=True)
    spread = jnp.mean(center * center, axis=-1, keepdims=True)
    scaled = center * lax.rsqrt(spread + EPSILON)
    out_ref[...] = (scaled * (1.0 + mod_ref[1, row, :]) + mod_ref[0, row, :]).astype(jnp.bfloat16)
    gate_ref[...] = mod_ref[2, row, :]


MOD_ROWS = 8


def normalize(levels, rows, modulation):
    width = rows.shape[1]
    return pl.pallas_call(
        norm_kernel,
        grid_spec=pltpu.PrefetchScalarGridSpec(
            num_scalar_prefetch=1,
            grid=(1,),
            in_specs=[
                pl.BlockSpec(rows.shape, lambda i, s: (0, 0)),
                pl.BlockSpec((3, MOD_ROWS, width), lambda i, s: (0, s[0] // MOD_ROWS, 0)),
            ],
            out_specs=[
                pl.BlockSpec(rows.shape, lambda i, s: (0, 0)),
                pl.BlockSpec((1, width), lambda i, s: (0, 0)),
            ],
        ),
        out_shape=[
            jax.ShapeDtypeStruct(rows.shape, jnp.bfloat16),
            jax.ShapeDtypeStruct((1, width), jnp.float32),
        ],
        name="normalize",
    )(levels, rows, modulation.transpose(1, 0, 2))


def latent_kernel(w_ref, gate_ref, lw_ref, o_ref):
    gated = w_ref[...].astype(jnp.float32) * gate_ref[...]
    hi = gated.astype(jnp.bfloat16)
    lo = (gated - hi.astype(jnp.float32)).astype(jnp.bfloat16)
    out = dot_t(hi, lw_ref[...]) + dot_t(lo, lw_ref[...])
    top = out.astype(jnp.bfloat16)
    o_ref[: w_ref.shape[0], :] = top
    o_ref[w_ref.shape[0] :, :] = (out - top.astype(jnp.float32)).astype(jnp.bfloat16)


def latent_matrix(w, gate_row, latent_weight):
    pv = latent_weight.shape[1]
    return pl.pallas_call(
        latent_kernel,
        out_shape=jax.ShapeDtypeStruct((2 * w.shape[0], pv), jnp.bfloat16),
        compiler_params=pltpu.CompilerParams(vmem_limit_bytes=16 * 2**20),
        name="latent_matrix",
    )(w, gate_row, latent_weight.T)


def project_kernel(*refs):
    blocks, (own_ref, oth_ref, mine_ref, theirs_ref, rows) = refs[:NZ], refs[NZ:]
    for i, block in enumerate(blocks):
        rows[i * BLK : i * BLK + BLK, :] = block[...]
    for w_ref, o_ref in ((oth_ref, theirs_ref), (own_ref, mine_ref)):
        out = jnp.dot(rows[...], w_ref[...], preferred_element_type=jnp.float32)
        o_ref[:, :HD] = (out[:, :HD] * EXP_SCALE).astype(jnp.bfloat16)
        o_ref[:, HD:] = out[:, HD:].astype(jnp.bfloat16)


def project(blocks, w_own, w_oth):
    width, cols = w_own.shape
    rows = len(blocks) * BLK
    vmem = pl.BlockSpec(memory_space=pltpu.VMEM)
    return pl.pallas_call(
        project_kernel,
        in_specs=[vmem] * (len(blocks) + 2),
        out_specs=[vmem, vmem],
        out_shape=[jax.ShapeDtypeStruct((rows, cols), jnp.bfloat16)] * 2,
        scratch_shapes=[pltpu.VMEM((rows, width), jnp.bfloat16)],
        compiler_params=pltpu.CompilerParams(vmem_limit_bytes=16 * 2**20),
        cost_estimate=pl.CostEstimate(
            flops=4 * rows * width * cols,
            bytes_accessed=4 * width * cols + 2 * rows * width,
            transcendentals=0,
        ),
        name="project",
    )(*blocks, w_own, w_oth)


def dot_t(a, b):
    return lax.dot_general(a, b, (((1,), (1,)), ((), ())), preferred_element_type=jnp.float32)


TILE = 128


def used_slots(y, z):
    return (y * NZ + z) * NC < HEADS


def self_kernel(s_ref, q_ref, kv_ref, m_ref, o_ref, values):
    y, z, core = s_ref[1], s_ref[2], s_ref[3]
    used = used_slots(y, z)
    values[:, :HD] = kv_ref[:, HD:]
    values[:, HD:] = jnp.ones((values.shape[0], HD), jnp.bfloat16)
    for t in range(q_ref.shape[0] // TILE):
        s = dot_t(q_ref[t * TILE : t * TILE + TILE, :], kv_ref[:, :HD])
        p = jnp.exp2(s - jnp.max(s, axis=1, keepdims=True)).astype(jnp.bfloat16)
        acc = jnp.dot(p, values[...], preferred_element_type=jnp.float32)
        att = (acc[:, :HD] / acc[:, HD:]).astype(jnp.bfloat16)
        att = jnp.concatenate([att, att], axis=1)
        part = jnp.dot(att, m_ref[...], preferred_element_type=jnp.float32)
        part = jnp.where(used, part, 0.0).astype(jnp.bfloat16)
        for j in range(TILE // BLK):
            y_apart, core_apart, d = block_of(t * (TILE // BLK) + j)
            at = ((core ^ core_apart) * NY + (y ^ y_apart)) * NZ + (z + d) % NZ
            o_ref[at] = part[j * BLK : j * BLK + BLK]


def self_attention(place, q, kv, matrix):
    pv = matrix.shape[1]
    rows = q.shape[0]
    return pl.pallas_call(
        self_kernel,
        grid_spec=pltpu.PrefetchScalarGridSpec(
            num_scalar_prefetch=1,
            grid=(1,),
            in_specs=[pl.BlockSpec(a.shape, lambda i, s: (0, 0)) for a in (q, kv, matrix)],
            out_specs=pl.BlockSpec((rows // BLK, BLK, pv), lambda i, s: (0, 0, 0)),
            scratch_shapes=[pltpu.VMEM((rows, 2 * HD), jnp.bfloat16)],
        ),
        out_shape=jax.ShapeDtypeStruct((rows // BLK, BLK, pv), jnp.bfloat16),
        compiler_params=pltpu.CompilerParams(vmem_limit_bytes=16 * 2**20),
        cost_estimate=pl.CostEstimate(
            flops=6 * rows * rows * HD, bytes_accessed=2**20, transcendentals=rows * rows
        ),
        name="self_attention",
    )(place, q, kv, matrix)


def visit(refs, q, values, acc, top):
    at = 0
    for ref in refs:
        values[at : at + ref.shape[0], :HD] = ref[:, HD:]
        at += ref.shape[0]
    values[:, HD:] = jnp.ones((values.shape[0], HD), jnp.bfloat16)
    for t in range(q.shape[0] // TILE):
        rows = slice(t * TILE, t * TILE + TILE)
        parts = [dot_t(q[rows, :], ref[:, :HD]) for ref in refs]
        old = top[rows, :1]
        new = old
        for s in parts:
            new = jnp.maximum(new, jnp.max(s, axis=1, keepdims=True))
        total = acc[rows, :] * jnp.exp2(old - new)
        at = 0
        for s in parts:
            p = jnp.exp2(s - new).astype(jnp.bfloat16)
            n = s.shape[1]
            total = total + jnp.dot(
                p, values[at : at + n, :], preferred_element_type=jnp.float32
            )
            at += n
        acc[rows, :] = total
        top[rows, :] = jnp.broadcast_to(new, (TILE, 128))


def sees(order_ref, s_ref, dh, dx):
    x, h = s_ref[4], s_ref[0]
    mine = order_ref[x * NH + (h ^ dh)]
    return order_ref[((x + dx) % NX) * NH + h] <= mine


def near_kernel(order_ref, s_ref, qa_ref, qb_ref, k0, k1, k2, acc_ref, top_ref, q, values):
    dh = pl.program_id(0)
    q[...] = jnp.where(dh == 0, qa_ref[...], qb_ref[...])
    acc_ref[...] = jnp.zeros_like(acc_ref)
    top_ref[...] = jnp.full_like(top_ref, -NEG_LARGE)
    for dx, ref in ((0, k0), (NX - 1, k1), (1, k2)):
        pl.when(sees(order_ref, s_ref, dh, dx))(
            functools.partial(visit, (ref,), q, values, acc_ref.at[0], top_ref.at[0])
        )


def far_kernel(order_ref, s_ref, qa_ref, qb_ref, acc_in, top_in, k3a, k3b, o_ref, *scratch):
    q, values, acc, top = scratch
    dh = pl.program_id(0)
    q[...] = jnp.where(dh == 0, qa_ref[...], qb_ref[...])
    acc[...] = acc_in[0]
    top[...] = top_in[0]
    pl.when(sees(order_ref, s_ref, dh, 2))(
        functools.partial(visit, (k3a, k3b), q, values, acc, top)
    )
    y, core = s_ref[1], s_ref[3]
    for quarter in range(4):
        starts = [block_at(quarter // 2, quarter % 2, d) * BLK for d in range(NZ)]
        gather = lambda ref, cols: jnp.concatenate([ref[i : i + BLK, cols] for i in starts], axis=0)
        total = gather(acc, slice(HD, 2 * HD))
        some = total > 0.0
        safe = jnp.where(some, total, 1.0)
        at = quarter ^ (y * 2 + core)
        o_ref[at, :QUARTER, :] = (gather(acc, slice(0, HD)) / safe).astype(jnp.bfloat16)
        lse = jnp.where(some, gather(top, slice(0, 128)) + jnp.log2(safe), -NEG_LARGE)
        row = lse.T[0:1, :]
        row = jnp.concatenate([row[:, :128], row[:, 128:]], axis=0)
        hi = row.astype(jnp.bfloat16).astype(jnp.float32)
        rest = row - hi
        mid = rest.astype(jnp.bfloat16).astype(jnp.float32)
        pad = jnp.zeros((TAIL - 6, 128), jnp.float32)
        o_ref[at, QUARTER:, :] = jnp.concatenate([hi, mid, rest - mid, pad], axis=0).astype(
            jnp.bfloat16
        )


def whole(a):
    return pl.BlockSpec(a.shape, lambda i, *s: (0,) * a.ndim)


def attention_cost(units, rows):
    pairs = 2 * units * rows * rows
    return pl.CostEstimate(flops=6 * pairs * HD, bytes_accessed=4 * 2**20, transcendentals=pairs)


def near_attention(order, place, qa, qb, blocks):
    rows = qa.shape[0]
    out = lambda cols: pl.BlockSpec((1, rows, cols), lambda i, *s: (i, 0, 0))
    return pl.pallas_call(
        near_kernel,
        grid_spec=pltpu.PrefetchScalarGridSpec(
            num_scalar_prefetch=2,
            grid=(NH,),
            in_specs=[whole(a) for a in (qa, qb, *blocks)],
            out_specs=[out(2 * HD), out(128)],
            scratch_shapes=[
                pltpu.VMEM((rows, HD), jnp.bfloat16),
                pltpu.VMEM((rows, 2 * HD), jnp.bfloat16),
            ],
        ),
        out_shape=[
            jax.ShapeDtypeStruct((NH, rows, 2 * HD), jnp.float32),
            jax.ShapeDtypeStruct((NH, rows, 128), jnp.float32),
        ],
        compiler_params=pltpu.CompilerParams(vmem_limit_bytes=20 * 2**20),
        cost_estimate=attention_cost(3, rows),
        name="near_attention",
    )(order, place, qa, qb, *blocks)


def far_attention(order, place, qa, qb, acc, top, blocks):
    rows = qa.shape[0]
    chunk = QUARTER + TAIL
    part = lambda a: pl.BlockSpec((1,) + a.shape[1:], lambda i, *s: (i, 0, 0))
    return pl.pallas_call(
        far_kernel,
        grid_spec=pltpu.PrefetchScalarGridSpec(
            num_scalar_prefetch=2,
            grid=(NH,),
            in_specs=[whole(qa), whole(qb), part(acc), part(top)] + [whole(b) for b in blocks],
            out_specs=pl.BlockSpec((4, chunk, HD), lambda i, o, s: (i ^ s[0], 0, 0)),
            scratch_shapes=[
                pltpu.VMEM((rows, HD), jnp.bfloat16),
                pltpu.VMEM((rows, 2 * HD), jnp.bfloat16),
                pltpu.VMEM((rows, 2 * HD), jnp.float32),
                pltpu.VMEM((rows, 128), jnp.float32),
            ],
        ),
        out_shape=jax.ShapeDtypeStruct((NH * 4, chunk, HD), jnp.bfloat16),
        compiler_params=pltpu.CompilerParams(vmem_limit_bytes=24 * 2**20),
        cost_estimate=attention_cost(1, rows),
        name="far_attention",
    )(order, place, qa, qb, acc, top, *blocks)


def join_kernel(s_ref, in_ref, w0_ref, w1_ref, w2_ref, w3_ref, o_ref, a_ref, w_ref):
    h, y, z, core = s_ref[0], s_ref[1], s_ref[2], s_ref[3]
    place = h * 4 + y * 2 + core

    @pl.when(pl.program_id(0) == 0)
    def _():
        for r in range(4):
            used = used_slots(y ^ (r // 2), z)
            parts = []
            for dh in range(NH):
                at = (dh * 4 + r) ^ place
                rows = in_ref[at, QUARTER:, :].astype(jnp.float32)
                parts.append((at, rows[0:2] + rows[2:4] + rows[4:6]))
            top = jnp.maximum(parts[0][1], parts[1][1])
            e = [jnp.exp2(lse - top) for _, lse in parts]
            norm = e[0] + e[1]
            for half in range(2):
                out = None
                for (at, _), weight in zip(parts, e):
                    w = jnp.where(used, weight / norm, 0.0)[half : half + 1, :]
                    col = jnp.broadcast_to(w, (128, 128)).T
                    term = in_ref[at, half * 128 : half * 128 + 128, :].astype(jnp.float32) * col
                    out = term if out is None else out + term
                out = out.astype(jnp.bfloat16)
                for j in range(4):
                    start = pl.multiple_of(((z + half * 4 + j) % NZ) * BLK, BLK)
                    a_ref[pl.ds(start, BLK), r * HD : r * HD + HD] = out[j * BLK : j * BLK + BLK]

    for r, ref in enumerate((w0_ref, w1_ref, w2_ref, w3_ref)):
        w_ref[r * HD : r * HD + HD, :] = ref[...]
    o_ref[...] = jnp.dot(a_ref[...], w_ref[...], preferred_element_type=jnp.float32).astype(
        jnp.bfloat16
    )


def join_heads(place, received, weights):
    width = weights[0].shape[1]
    step = width // 4
    return pl.pallas_call(
        join_kernel,
        grid_spec=pltpu.PrefetchScalarGridSpec(
            num_scalar_prefetch=1,
            grid=(4,),
            in_specs=[whole(received)] + [pl.BlockSpec((HD, step), lambda i, s: (0, i))] * 4,
            out_specs=pl.BlockSpec((QUARTER, step), lambda i, s: (0, i)),
            scratch_shapes=[
                pltpu.VMEM((QUARTER, 4 * HD), jnp.bfloat16),
                pltpu.VMEM((4 * HD, step), jnp.bfloat16),
            ],
        ),
        out_shape=jax.ShapeDtypeStruct((QUARTER, width), jnp.bfloat16),
        compiler_params=pltpu.CompilerParams(vmem_limit_bytes=16 * 2**20),
        name="join_heads",
    )(place, received, *weights)


def decode(latents, root_kernel):
    seq_count = latents.shape[0]
    row_patches = seq_count // FR
    me = lax.axis_index("seq")
    ringed = jnp.concatenate([latents[-1:], latents, latents[:1]], axis=0)
    position = (me - row_patches // 2 + seq_count) % seq_count
    patch_row = position % row_patches
    frame_index = position // row_patches
    row_ids = jnp.arange(P_SIZE + 2, dtype=jnp.int32)
    keep = jnp.where(
        row_ids == 0,
        patch_row > 0,
        jnp.where(row_ids == P_SIZE + 1, patch_row < row_patches - 1, True),
    )
    width_cols = BLK * P_SIZE
    windows = []
    for lag in range(3):
        start = (me - lag * row_patches + seq_count) % seq_count
        three = lax.dynamic_slice_in_dim(ringed, start, 3, axis=0)
        slab = (
            three.reshape(3, BLK, P_SIZE, P_SIZE, C)
            .transpose(0, 2, 1, 3, 4)
            .reshape(3 * P_SIZE, width_cols, C)
        )[P_SIZE - 1 : 2 * P_SIZE + 1]
        ok = keep & (frame_index >= lag)
        slab = jnp.where(ok[:, None, None], slab, jnp.zeros_like(slab))
        framed = jnp.pad(slab, ((0, 0), (1, 1), (0, 0)))
        for row_off in range(3):
            for col_off in range(3):
                windows.append(framed[row_off : row_off + P_SIZE, col_off : col_off + width_cols])
    stacked = jnp.concatenate(windows, axis=-1).reshape(P_SIZE * width_cols, 27 * C)
    decoded = jnp.dot(stacked, root_kernel, preferred_element_type=jnp.float32)
    return decoded.reshape(P_SIZE, width_cols, root_kernel.shape[1]).astype(jnp.bfloat16)[None]


def after(value, earlier):
    return lax.optimization_barrier((value, earlier))[0]


def per_device(
    hidden, levels, span_order, modulation, in_weight, out_weight, latent_weight, decoder_weight
):
    span_me = lax.axis_index("span")
    seq_me = lax.axis_index("seq")
    x, h = span_me // NH, span_me % NH
    y, z, core = seq_me // (NZ * NC), (seq_me // NC) % NZ, seq_me % NC
    place = jnp.stack([h, y, z, core, x])
    pv = latent_weight.shape[1]
    seq_count = NY * NZ * NC

    normed, gate_row = normalize(levels, hidden[0], modulation)
    w_own = in_weight[0]
    own_blocks, other_blocks = gather_class(normed)
    w_oth = move_core(w_own)
    mine_a, theirs_a = project(own_blocks, w_own, w_oth)
    mine_b, theirs_b = project(other_blocks, w_own, w_oth)
    triples = jnp.concatenate([mine_a, move_core(theirs_a), mine_b, move_core(theirs_b)], axis=0)
    q = triples[:, :HD]
    kv = triples[:, HD:]

    half = kv.shape[0] // 2
    kv_up, kv_dn = move_x(kv, 1), move_x(kv, -1)
    q_hi = move_hi(q)
    kv_far = (move_x(kv_up[:half], 1), move_x(kv_dn[half:], -1))

    matrix = latent_matrix(after(out_weight[0], mine_b), gate_row, latent_weight)
    part = self_attention(place, q, kv, matrix)
    part = after(after(halve(part, core, move_core), kv_up), kv_dn)
    part = halve(part, y, move_y)

    out_w = after(out_weight[0], q_hi)
    w_core, w_far = move_core(out_w), move_y(out_w)
    weights = (out_w, w_core, w_far, move_core(w_far))

    q_hi = after(q_hi, part)
    acc, top = near_attention(span_order, place, q, q_hi, (kv, kv_up, kv_dn))
    chunks = far_attention(span_order, place, q, q_hi, acc, top, kv_far)
    part = after(part, chunks)
    part = halve(part, z // 4, lambda a: swap_z(a, 4))
    part = halve(part, z // 2 % 2, lambda a: swap_z(a, 2))
    part = halve(part, z % 2, lambda a: swap_z(a, 1))
    groups = [
        [
            span_at(i, hh) * seq_count + seq_at(yy, j, cc)
            for hh in range(NH)
            for yy in range(NY)
            for cc in range(NC)
        ]
        for i in range(NX)
        for j in range(NZ)
    ]
    received = lax.all_to_all(
        chunks, ("span", "seq"), 0, 0, tiled=True, axis_index_groups=groups
    )
    partial = join_heads(place, received, weights)
    z_groups = [[seq_at(yy, j, cc) for j in range(NZ)] for yy in range(NY) for cc in range(NC)]
    summed = lax.psum_scatter(
        partial, "seq", scatter_dimension=0, tiled=True, axis_index_groups=z_groups
    ).astype(jnp.float32)
    block_out = (hidden[0].astype(jnp.float32) + gate_row * summed).astype(jnp.bfloat16)[None]

    own_latents = jnp.dot(hidden[0], latent_weight, preferred_element_type=jnp.float32)
    latents = (part[0].astype(jnp.float32) + own_latents).astype(jnp.bfloat16)
    group_ids = jnp.arange(span_order.shape[0], dtype=jnp.int32)
    root = jnp.sum(jnp.where(span_order == 0, group_ids, 0))
    spread = lax.all_to_all(
        jnp.broadcast_to(latents[None], (NX * NH, BLK, pv)), "span", 0, 0, tiled=True
    )
    latents = lax.dynamic_index_in_dim(spread, root, 0, keepdims=True)
    every = lax.all_to_all(
        jnp.broadcast_to(latents, (seq_count, BLK, pv)), "seq", 0, 0, tiled=True
    )
    decoded = decode(every, decoder_weight.reshape(27 * C, decoder_weight.shape[4]))
    return (block_out, decoded)


def solution(mesh):
    placed = (
        P("span", "seq", None),
        P("span"),
        P(),
        P(),
        P("seq", None, None),
        P("seq", None, None),
        P(),
        P(None, None, None, None, "span"),
    )
    return jax.shard_map(
        per_device,
        mesh=mesh,
        in_specs=placed,
        out_specs=(P("span", "seq", None), P("seq", None, None, "span")),
        check_vma=False,
    )
```

```python
import functools
import math

import jax
import jax.numpy as jnp
from jax import lax
from jax.experimental import pallas as pl
from jax.experimental.pallas import tpu as pltpu
from jax.sharding import PartitionSpec as P

HEADS = 24
FR = 4
P_SIZE = 2
C = 16
HD = 128

EPSILON = 1e-06
NEG_LARGE = 1e30

NX, NH, NY, NZ, NC = 4, 2, 2, 8, 2
BLK = 32
QUARTER = NZ * BLK
TAIL = 16


def seq_at(y, z, c):
    return ((y % NY) * NZ + z % NZ) * NC + c % NC


def span_at(x, h):
    return (x % NX) * NH + h % NH


def seq_route(dy=0, dz=0, dc=0):
    return [
        (seq_at(y, z, c), seq_at(y + dy, z + dz, c + dc))
        for y in range(NY)
        for z in range(NZ)
        for c in range(NC)
    ]


def span_route(dx=0, dh=0):
    return [(span_at(x, h), span_at(x + dx, h + dh)) for x in range(NX) for h in range(NH)]


def move_z(a, d):
    return lax.ppermute(a, "seq", seq_route(dz=d))


def move_y(a):
    return lax.ppermute(a, "seq", seq_route(dy=1))


def move_core(a):
    return lax.ppermute(a, "seq", seq_route(dc=1))


def move_x(a, d):
    return lax.ppermute(a, "span", span_route(dx=d))


def move_hi(a):
    return lax.ppermute(a, "span", span_route(dh=1))


HALVES = (
    ((0, 0), (0, 1), (0, 2), (0, 6), (0, 7), (1, 0), (1, 1), (1, 7)),
    ((0, 3), (0, 4), (0, 5), (1, 2), (1, 3), (1, 4), (1, 5), (1, 6)),
)


def block_at(y_apart, core_apart, d):
    half = 0 if (y_apart, d) in HALVES[0] else 1
    return half * 2 * NZ + core_apart * NZ + HALVES[half].index((y_apart, d))


def block_of(at):
    half, core_apart, i = at // (2 * NZ), at // NZ % 2, at % NZ
    y_apart, d = HALVES[half][i]
    return y_apart, core_apart, d


def gather_class(b):
    up1, dn1, y0 = move_z(b, 1), move_z(b, -1), move_y(b)
    up2, dn2 = move_z(up1, 1), move_z(dn1, -1)
    yu1, yd1 = move_y(up1), move_y(dn1)
    up3, dn3 = move_z(up2, 1), move_z(dn2, -1)
    yu2, yd2 = move_y(up2), move_y(dn2)
    far = move_z(up3, 1)
    yu3, yd3 = move_z(yu2, 1), move_z(yd2, -1)
    yfar = lax.ppermute(dn3, "seq", seq_route(dy=1, dz=-1))
    return (b, dn1, dn2, up2, up1, y0, yd1, yu1), (dn3, far, up3, yd2, yd3, yfar, yu3, yu2)


EXP_SCALE = math.log2(math.e) / math.sqrt(HD)


def norm_kernel(level_ref, hidden_ref, mod_ref, out_ref, gate_ref):
    values = hidden_ref[...].astype(jnp.float32)
    row = pl.ds(level_ref[0] % MOD_ROWS, 1)
    center = values - jnp.mean(values, axis=-1, keepdims=True)
    spread = jnp.mean(center * center, axis=-1, keepdims=True)
    scaled = center * lax.rsqrt(spread + EPSILON)
    out_ref[...] = (scaled * (1.0 + mod_ref[1, row, :]) + mod_ref[0, row, :]).astype(jnp.bfloat16)
    gate_ref[...] = mod_ref[2, row, :]


MOD_ROWS = 8


def normalize(levels, rows, modulation):
    width = rows.shape[1]
    return pl.pallas_call(
        norm_kernel,
        grid_spec=pltpu.PrefetchScalarGridSpec(
            num_scalar_prefetch=1,
            grid=(1,),
            in_specs=[
                pl.BlockSpec(rows.shape, lambda i, s: (0, 0)),
                pl.BlockSpec((3, MOD_ROWS, width), lambda i, s: (0, s[0] // MOD_ROWS, 0)),
            ],
            out_specs=[
                pl.BlockSpec(rows.shape, lambda i, s: (0, 0)),
                pl.BlockSpec((1, width), lambda i, s: (0, 0)),
            ],
        ),
        out_shape=[
            jax.ShapeDtypeStruct(rows.shape, jnp.bfloat16),
            jax.ShapeDtypeStruct((1, width), jnp.float32),
        ],
        name="normalize",
    )(levels, rows, modulation.transpose(1, 0, 2))


def latent_kernel(w_ref, gate_ref, lw_ref, o_ref):
    gated = w_ref[...].astype(jnp.float32) * gate_ref[...]
    hi = gated.astype(jnp.bfloat16)
    lo = (gated - hi.astype(jnp.float32)).astype(jnp.bfloat16)
    out = dot_t(hi, lw_ref[...]) + dot_t(lo, lw_ref[...])
    top = out.astype(jnp.bfloat16)
    o_ref[: w_ref.shape[0], :] = top
    o_ref[w_ref.shape[0] :, :] = (out - top.astype(jnp.float32)).astype(jnp.bfloat16)


def latent_matrix(w, gate_row, latent_weight):
    pv = latent_weight.shape[1]
    return pl.pallas_call(
        latent_kernel,
        out_shape=jax.ShapeDtypeStruct((2 * w.shape[0], pv), jnp.bfloat16),
        compiler_params=pltpu.CompilerParams(vmem_limit_bytes=16 * 2**20),
        name="latent_matrix",
    )(w, gate_row, latent_weight.T)


def project_kernel(*refs):
    blocks, (own_ref, oth_ref, mine_ref, theirs_ref, rows) = refs[:NZ], refs[NZ:]
    for i, block in enumerate(blocks):
        rows[i * BLK : i * BLK + BLK, :] = block[...]
    for w_ref, o_ref in ((oth_ref, theirs_ref), (own_ref, mine_ref)):
        out = jnp.dot(rows[...], w_ref[...], preferred_element_type=jnp.float32)
        o_ref[:, :HD] = (out[:, :HD] * EXP_SCALE).astype(jnp.bfloat16)
        o_ref[:, HD:] = out[:, HD:].astype(jnp.bfloat16)


def project(blocks, w_own, w_oth):
    width, cols = w_own.shape
    rows = len(blocks) * BLK
    vmem = pl.BlockSpec(memory_space=pltpu.VMEM)
    return pl.pallas_call(
        project_kernel,
        in_specs=[vmem] * (len(blocks) + 2),
        out_specs=[vmem, vmem],
        out_shape=[jax.ShapeDtypeStruct((rows, cols), jnp.bfloat16)] * 2,
        scratch_shapes=[pltpu.VMEM((rows, width), jnp.bfloat16)],
        compiler_params=pltpu.CompilerParams(vmem_limit_bytes=16 * 2**20),
        cost_estimate=pl.CostEstimate(
            flops=4 * rows * width * cols,
            bytes_accessed=4 * width * cols + 2 * rows * width,
            transcendentals=0,
        ),
        name="project",
    )(*blocks, w_own, w_oth)


def dot_t(a, b):
    return lax.dot_general(a, b, (((1,), (1,)), ((), ())), preferred_element_type=jnp.float32)


TILE = 128


def used_slots(y, z):
    return (y * NZ + z) * NC < HEADS


def self_kernel(s_ref, q_ref, kv_ref, m_ref, o_ref, acc_ref, top_ref, values):
    y, z, core = s_ref[1], s_ref[2], s_ref[3]
    used = used_slots(y, z)
    values[:, :HD] = kv_ref[:, HD:]
    values[:, HD:] = jnp.ones((values.shape[0], HD), jnp.bfloat16)
    for t in range(q_ref.shape[0] // TILE):
        s = dot_t(q_ref[t * TILE : t * TILE + TILE, :], kv_ref[:, :HD])
        top = jnp.max(s, axis=1, keepdims=True)
        p = jnp.exp2(s - top).astype(jnp.bfloat16)
        acc = jnp.dot(p, values[...], preferred_element_type=jnp.float32)
        acc_ref[t * TILE : t * TILE + TILE, :] = acc
        top_ref[t * TILE : t * TILE + TILE, :] = jnp.broadcast_to(top, (TILE, 128))
        att = (acc[:, :HD] / acc[:, HD:]).astype(jnp.bfloat16)
        att = jnp.concatenate([att, att], axis=1)
        part = jnp.dot(att, m_ref[...], preferred_element_type=jnp.float32)
        part = jnp.where(used, part, 0.0).astype(jnp.bfloat16)
        for j in range(TILE // BLK):
            y_apart, core_apart, d = block_of(t * (TILE // BLK) + j)
            at = ((y ^ y_apart) * NZ + (z + d) % NZ) * NC + (core ^ core_apart)
            low, high = j * BLK, j * BLK + BLK // 2
            o_ref[at] = jnp.concatenate(
                [part[low:high, :], part[high : high + BLK // 2, :]], axis=1
            )


def self_attention(place, q, kv, matrix):
    pv = matrix.shape[1]
    rows = q.shape[0]
    return pl.pallas_call(
        self_kernel,
        grid_spec=pltpu.PrefetchScalarGridSpec(
            num_scalar_prefetch=1,
            grid=(1,),
            in_specs=[pl.BlockSpec(a.shape, lambda i, s: (0, 0)) for a in (q, kv, matrix)],
            out_specs=[
                pl.BlockSpec((rows // BLK, BLK // 2, 2 * pv), lambda i, s: (0, 0, 0)),
                pl.BlockSpec((rows, 2 * HD), lambda i, s: (0, 0)),
                pl.BlockSpec((rows, 128), lambda i, s: (0, 0)),
            ],
            scratch_shapes=[pltpu.VMEM((rows, 2 * HD), jnp.bfloat16)],
        ),
        out_shape=[
            jax.ShapeDtypeStruct((rows // BLK, BLK // 2, 2 * pv), jnp.bfloat16),
            jax.ShapeDtypeStruct((rows, 2 * HD), jnp.float32),
            jax.ShapeDtypeStruct((rows, 128), jnp.float32),
        ],
        compiler_params=pltpu.CompilerParams(vmem_limit_bytes=16 * 2**20),
        cost_estimate=pl.CostEstimate(
            flops=6 * rows * rows * HD, bytes_accessed=2**20, transcendentals=rows * rows
        ),
        name="self_attention",
    )(place, q, kv, matrix)


def visit(kv_ref, q, values, acc, top):
    values[:, :HD] = kv_ref[:, HD:]
    values[:, HD:] = jnp.ones((values.shape[0], HD), jnp.bfloat16)
    for t in range(q.shape[0] // TILE):
        rows = slice(t * TILE, t * TILE + TILE)
        s = dot_t(q[rows, :], kv_ref[:, :HD])
        old = top[rows, :1]
        new = jnp.maximum(old, jnp.max(s, axis=1, keepdims=True))
        p = jnp.exp2(s - new).astype(jnp.bfloat16)
        acc[rows, :] = acc[rows, :] * jnp.exp2(old - new) + jnp.dot(
            p, values[...], preferred_element_type=jnp.float32
        )
        top[rows, :] = jnp.broadcast_to(new, (TILE, 128))


def sees(order_ref, s_ref, dh, dx):
    x, h = s_ref[4], s_ref[0]
    mine = order_ref[x * NH + (h ^ dh)]
    return order_ref[((x + dx) % NX) * NH + h] <= mine


def other_kernel(order_ref, s_ref, qa_ref, qb_ref, acc_in, top_in, k0, k1, k2, k3, o_ref, *scratch):
    q, values, acc, top = scratch
    dh = pl.program_id(0)
    q[...] = jnp.where(dh == 0, qa_ref[...], qb_ref[...])

    @pl.when(dh == 0)
    def _():
        acc[...] = acc_in[...]
        top[...] = top_in[...]

    @pl.when(dh == 1)
    def _():
        acc[...] = jnp.zeros_like(acc)
        top[...] = jnp.full_like(top, -NEG_LARGE)

    pl.when((dh == 1) & sees(order_ref, s_ref, dh, 0))(
        functools.partial(visit, k0, q, values, acc, top)
    )
    for dx, ref in ((NX - 1, k1), (1, k2), (2, k3)):
        pl.when(sees(order_ref, s_ref, dh, dx))(
            functools.partial(visit, ref, q, values, acc, top)
        )
    y, core = s_ref[1], s_ref[3]
    for quarter in range(4):
        starts = [block_at(quarter // 2, quarter % 2, d) * BLK for d in range(NZ)]
        gather = lambda ref, cols: jnp.concatenate([ref[i : i + BLK, cols] for i in starts], axis=0)
        total = gather(acc, slice(HD, 2 * HD))
        some = total > 0.0
        safe = jnp.where(some, total, 1.0)
        at = quarter ^ (y * 2 + core)
        o_ref[at, :QUARTER, :] = (gather(acc, slice(0, HD)) / safe).astype(jnp.bfloat16)
        lse = jnp.where(some, gather(top, slice(0, 128)) + jnp.log2(safe), -NEG_LARGE)
        row = lse.T[0:1, :]
        row = jnp.concatenate([row[:, :128], row[:, 128:]], axis=0)
        hi = row.astype(jnp.bfloat16).astype(jnp.float32)
        rest = row - hi
        mid = rest.astype(jnp.bfloat16).astype(jnp.float32)
        pad = jnp.zeros((TAIL - 6, 128), jnp.float32)
        o_ref[at, QUARTER:, :] = jnp.concatenate([hi, mid, rest - mid, pad], axis=0).astype(
            jnp.bfloat16
        )


def whole(a):
    return pl.BlockSpec(a.shape, lambda i, *s: (0,) * a.ndim)


def attention_cost(units, rows):
    pairs = 2 * units * rows * rows
    return pl.CostEstimate(flops=6 * pairs * HD, bytes_accessed=4 * 2**20, transcendentals=pairs)


def other_attention(order, place, qa, qb, acc, top, blocks):
    rows = qa.shape[0]
    chunk = QUARTER + TAIL
    return pl.pallas_call(
        other_kernel,
        grid_spec=pltpu.PrefetchScalarGridSpec(
            num_scalar_prefetch=2,
            grid=(NH,),
            in_specs=[whole(a) for a in (qa, qb, acc, top, *blocks)],
            out_specs=pl.BlockSpec((4, chunk, HD), lambda i, o, s: (i ^ s[0], 0, 0)),
            scratch_shapes=[
                pltpu.VMEM((rows, HD), jnp.bfloat16),
                pltpu.VMEM((rows, 2 * HD), jnp.bfloat16),
                pltpu.VMEM((rows, 2 * HD), jnp.float32),
                pltpu.VMEM((rows, 128), jnp.float32),
            ],
        ),
        out_shape=jax.ShapeDtypeStruct((NH * 4, chunk, HD), jnp.bfloat16),
        compiler_params=pltpu.CompilerParams(vmem_limit_bytes=24 * 2**20),
        cost_estimate=attention_cost(3, rows),
        name="other_attention",
    )(order, place, qa, qb, acc, top, *blocks)


def join_kernel(s_ref, in_ref, w0_ref, w1_ref, w2_ref, w3_ref, o_ref, a_ref, w_ref):
    h, y, z, core = s_ref[0], s_ref[1], s_ref[2], s_ref[3]
    place = h * 4 + y * 2 + core

    @pl.when(pl.program_id(0) == 0)
    def _():
        for r in range(4):
            used = used_slots(y ^ (r // 2), z)
            parts = []
            for dh in range(NH):
                at = (dh * 4 + r) ^ place
                rows = in_ref[at, QUARTER:, :].astype(jnp.float32)
                parts.append((at, rows[0:2] + rows[2:4] + rows[4:6]))
            top = jnp.maximum(parts[0][1], parts[1][1])
            e = [jnp.exp2(lse - top) for _, lse in parts]
            norm = e[0] + e[1]
            for half in range(2):
                out = None
                for (at, _), weight in zip(parts, e):
                    w = jnp.where(used, weight / norm, 0.0)[half : half + 1, :]
                    col = jnp.broadcast_to(w, (128, 128)).T
                    term = in_ref[at, half * 128 : half * 128 + 128, :].astype(jnp.float32) * col
                    out = term if out is None else out + term
                out = out.astype(jnp.bfloat16)
                for j in range(4):
                    start = pl.multiple_of(((z + half * 4 + j) % NZ) * BLK, BLK)
                    a_ref[pl.ds(start, BLK), r * HD : r * HD + HD] = out[j * BLK : j * BLK + BLK]

    for r, ref in enumerate((w0_ref, w1_ref, w2_ref, w3_ref)):
        w_ref[r * HD : r * HD + HD, :] = ref[...]
    o_ref[...] = jnp.dot(a_ref[...], w_ref[...], preferred_element_type=jnp.float32).astype(
        jnp.bfloat16
    )


def join_heads(place, received, weights):
    width = weights[0].shape[1]
    step = width // 4
    return pl.pallas_call(
        join_kernel,
        grid_spec=pltpu.PrefetchScalarGridSpec(
            num_scalar_prefetch=1,
            grid=(4,),
            in_specs=[whole(received)] + [pl.BlockSpec((HD, step), lambda i, s: (0, i))] * 4,
            out_specs=pl.BlockSpec((QUARTER, step), lambda i, s: (0, i)),
            scratch_shapes=[
                pltpu.VMEM((QUARTER, 4 * HD), jnp.bfloat16),
                pltpu.VMEM((4 * HD, step), jnp.bfloat16),
            ],
        ),
        out_shape=jax.ShapeDtypeStruct((QUARTER, width), jnp.bfloat16),
        compiler_params=pltpu.CompilerParams(vmem_limit_bytes=16 * 2**20),
        name="join_heads",
    )(place, received, *weights)


def decode(latents, root_kernel):
    seq_count = latents.shape[0]
    row_patches = seq_count // FR
    me = lax.axis_index("seq")
    ringed = jnp.concatenate([latents[-1:], latents, latents[:1]], axis=0)
    position = (me - row_patches // 2 + seq_count) % seq_count
    patch_row = position % row_patches
    frame_index = position // row_patches
    row_ids = jnp.arange(P_SIZE + 2, dtype=jnp.int32)
    keep = jnp.where(
        row_ids == 0,
        patch_row > 0,
        jnp.where(row_ids == P_SIZE + 1, patch_row < row_patches - 1, True),
    )
    width_cols = BLK * P_SIZE
    windows = []
    for lag in range(3):
        start = (me - lag * row_patches + seq_count) % seq_count
        three = lax.dynamic_slice_in_dim(ringed, start, 3, axis=0)
        pv = three.shape[2] // 2
        three = jnp.concatenate([three[:, :, :pv], three[:, :, pv:]], axis=1)
        slab = (
            three.reshape(3, BLK, P_SIZE, P_SIZE, C)
            .transpose(0, 2, 1, 3, 4)
            .reshape(3 * P_SIZE, width_cols, C)
        )[P_SIZE - 1 : 2 * P_SIZE + 1]
        ok = keep & (frame_index >= lag)
        slab = jnp.where(ok[:, None, None], slab, jnp.zeros_like(slab))
        framed = jnp.pad(slab, ((0, 0), (1, 1), (0, 0)))
        for row_off in range(3):
            for col_off in range(3):
                windows.append(framed[row_off : row_off + P_SIZE, col_off : col_off + width_cols])
    stacked = jnp.concatenate(windows, axis=-1).reshape(P_SIZE * width_cols, 27 * C)
    decoded = jnp.dot(stacked, root_kernel, preferred_element_type=jnp.float32)
    return decoded.reshape(P_SIZE, width_cols, root_kernel.shape[1]).astype(jnp.bfloat16)[None]


def after(value, earlier):
    return lax.optimization_barrier((value, earlier))[0]


def per_device(
    hidden, levels, span_order, modulation, in_weight, out_weight, latent_weight, decoder_weight
):
    span_me = lax.axis_index("span")
    seq_me = lax.axis_index("seq")
    x, h = span_me // NH, span_me % NH
    y, z, core = seq_me // (NZ * NC), (seq_me // NC) % NZ, seq_me % NC
    place = jnp.stack([h, y, z, core, x])
    seq_count = NY * NZ * NC

    normed, gate_row = normalize(levels, hidden[0], modulation)
    w_own = in_weight[0]
    own_blocks, other_blocks = gather_class(normed)
    w_oth = move_core(w_own)
    mine_a, theirs_a = project(own_blocks, w_own, w_oth)
    mine_b, theirs_b = project(other_blocks, w_own, w_oth)
    triples = jnp.concatenate([mine_a, move_core(theirs_a), mine_b, move_core(theirs_b)], axis=0)
    q = triples[:, :HD]
    kv = triples[:, HD:]

    others = tuple(move_x(kv, d) for d in (1, NX - 1, 2))
    q_hi = move_hi(q)

    matrix = latent_matrix(after(out_weight[0], mine_b), gate_row, latent_weight)
    part, acc, top = self_attention(place, q, kv, matrix)
    part = lax.all_to_all(part, "seq", 0, 0, tiled=True)

    out_w = after(out_weight[0], mine_b)
    w_core, w_far = move_core(out_w), move_y(out_w)
    weights = (out_w, w_core, w_far, move_core(w_far))

    acc = after(acc, part)
    chunks = other_attention(span_order, place, q, q_hi, acc, top, (kv, *others))
    groups = [
        [
            span_at(i, hh) * seq_count + seq_at(yy, j, cc)
            for hh in range(NH)
            for yy in range(NY)
            for cc in range(NC)
        ]
        for i in range(NX)
        for j in range(NZ)
    ]
    received = lax.all_to_all(
        chunks, ("span", "seq"), 0, 0, tiled=True, axis_index_groups=groups
    )
    partial = join_heads(place, received, weights)
    z_groups = [[seq_at(yy, j, cc) for j in range(NZ)] for yy in range(NY) for cc in range(NC)]
    part = after(part, partial)
    summed = lax.psum_scatter(
        partial, "seq", scatter_dimension=0, tiled=True, axis_index_groups=z_groups
    ).astype(jnp.float32)
    block_out = (hidden[0].astype(jnp.float32) + gate_row * summed).astype(jnp.bfloat16)[None]

    own_latents = jnp.dot(hidden[0], latent_weight, preferred_element_type=jnp.float32)
    own_latents = jnp.concatenate([own_latents[: BLK // 2], own_latents[BLK // 2 :]], axis=1)
    latents = (jnp.sum(part.astype(jnp.float32), axis=0) + own_latents).astype(jnp.bfloat16)
    group_ids = jnp.arange(span_order.shape[0], dtype=jnp.int32)
    root = jnp.sum(jnp.where(span_order == 0, group_ids, 0))
    spread = lax.all_to_all(
        jnp.broadcast_to(latents[None], (NX * NH,) + latents.shape), "span", 0, 0, tiled=True
    )
    latents = lax.dynamic_index_in_dim(spread, root, 0, keepdims=True)
    every = lax.all_to_all(
        jnp.broadcast_to(latents, (seq_count,) + latents.shape[1:]), "seq", 0, 0, tiled=True
    )
    decoded = decode(every, decoder_weight.reshape(27 * C, decoder_weight.shape[4]))
    return (block_out, decoded)


def solution(mesh):
    placed = (
        P("span", "seq", None),
        P("span"),
        P(),
        P(),
        P("seq", None, None),
        P("seq", None, None),
        P(),
        P(None, None, None, None, "span"),
    )
    return jax.shard_map(
        per_device,
        mesh=mesh,
        in_specs=placed,
        out_specs=(P("span", "seq", None), P("seq", None, None, "span")),
        check_vma=False,
    )
```

```python
import functools
import math

import jax
import jax.numpy as jnp
from jax import lax
from jax.experimental import pallas as pl
from jax.experimental.pallas import tpu as pltpu
from jax.sharding import PartitionSpec as P

HEADS = 24
FR = 4
P_SIZE = 2
C = 16
HD = 128

EPSILON = 1e-06
NEG_LARGE = 1e30

NX, NH, NY, NZ, NC = 4, 2, 2, 8, 2
BLK = 32
QUARTER = NZ * BLK
TAIL = 16


def seq_at(y, z, c):
    return ((y % NY) * NZ + z % NZ) * NC + c % NC


def span_at(x, h):
    return (x % NX) * NH + h % NH


def seq_route(dy=0, dz=0, dc=0):
    return [
        (seq_at(y, z, c), seq_at(y + dy, z + dz, c + dc))
        for y in range(NY)
        for z in range(NZ)
        for c in range(NC)
    ]


def span_route(dx=0, dh=0):
    return [(span_at(x, h), span_at(x + dx, h + dh)) for x in range(NX) for h in range(NH)]


def move_z(a, d):
    return lax.ppermute(a, "seq", seq_route(dz=d))


def move_y(a):
    return lax.ppermute(a, "seq", seq_route(dy=1))


def move_core(a):
    return lax.ppermute(a, "seq", seq_route(dc=1))


def move_x(a, d):
    return lax.ppermute(a, "span", span_route(dx=d))


def move_hi(a):
    return lax.ppermute(a, "span", span_route(dh=1))


HALVES = (
    ((0, 0), (0, 1), (0, 2), (0, 6), (0, 7), (1, 0), (1, 1), (1, 7)),
    ((0, 3), (0, 4), (0, 5), (1, 2), (1, 3), (1, 4), (1, 5), (1, 6)),
)


def block_at(y_apart, core_apart, d):
    half = 0 if (y_apart, d) in HALVES[0] else 1
    return half * 2 * NZ + core_apart * NZ + HALVES[half].index((y_apart, d))


def block_of(at):
    half, core_apart, i = at // (2 * NZ), at // NZ % 2, at % NZ
    y_apart, d = HALVES[half][i]
    return y_apart, core_apart, d


def gather_class(b):
    up1, dn1, y0 = move_z(b, 1), move_z(b, -1), move_y(b)
    up2, dn2 = move_z(up1, 1), move_z(dn1, -1)
    yu1, yd1 = move_y(up1), move_y(dn1)
    up3, dn3 = move_z(up2, 1), move_z(dn2, -1)
    yu2, yd2 = move_y(up2), move_y(dn2)
    far = move_z(up3, 1)
    yu3, yd3 = move_z(yu2, 1), move_z(yd2, -1)
    yfar = lax.ppermute(dn3, "seq", seq_route(dy=1, dz=-1))
    return (b, dn1, dn2, up2, up1, y0, yd1, yu1), (dn3, far, up3, yd2, yd3, yfar, yu3, yu2)


EXP_SCALE = math.log2(math.e) / math.sqrt(HD)


def norm_kernel(level_ref, hidden_ref, mod_ref, out_ref, gate_ref):
    values = hidden_ref[...].astype(jnp.float32)
    row = pl.ds(level_ref[0] % MOD_ROWS, 1)
    center = values - jnp.mean(values, axis=-1, keepdims=True)
    spread = jnp.mean(center * center, axis=-1, keepdims=True)
    scaled = center * lax.rsqrt(spread + EPSILON)
    out_ref[...] = (scaled * (1.0 + mod_ref[1, row, :]) + mod_ref[0, row, :]).astype(jnp.bfloat16)
    gate_ref[...] = mod_ref[2, row, :]


MOD_ROWS = 8


def normalize(levels, rows, modulation):
    width = rows.shape[1]
    return pl.pallas_call(
        norm_kernel,
        grid_spec=pltpu.PrefetchScalarGridSpec(
            num_scalar_prefetch=1,
            grid=(1,),
            in_specs=[
                pl.BlockSpec(rows.shape, lambda i, s: (0, 0)),
                pl.BlockSpec((3, MOD_ROWS, width), lambda i, s: (0, s[0] // MOD_ROWS, 0)),
            ],
            out_specs=[
                pl.BlockSpec(rows.shape, lambda i, s: (0, 0)),
                pl.BlockSpec((1, width), lambda i, s: (0, 0)),
            ],
        ),
        out_shape=[
            jax.ShapeDtypeStruct(rows.shape, jnp.bfloat16),
            jax.ShapeDtypeStruct((1, width), jnp.float32),
        ],
        name="normalize",
    )(levels, rows, modulation.transpose(1, 0, 2))


def latent_kernel(w_ref, gate_ref, lw_ref, o_ref):
    gated = w_ref[...].astype(jnp.float32) * gate_ref[...]
    hi = gated.astype(jnp.bfloat16)
    lo = (gated - hi.astype(jnp.float32)).astype(jnp.bfloat16)
    out = dot_t(hi, lw_ref[...]) + dot_t(lo, lw_ref[...])
    top = out.astype(jnp.bfloat16)
    o_ref[: w_ref.shape[0], :] = top
    o_ref[w_ref.shape[0] :, :] = (out - top.astype(jnp.float32)).astype(jnp.bfloat16)


def latent_matrix(w, gate_row, latent_weight):
    pv = latent_weight.shape[1]
    return pl.pallas_call(
        latent_kernel,
        out_shape=jax.ShapeDtypeStruct((2 * w.shape[0], pv), jnp.bfloat16),
        compiler_params=pltpu.CompilerParams(vmem_limit_bytes=16 * 2**20),
        name="latent_matrix",
    )(w, gate_row, latent_weight.T)


def project_kernel(*refs):
    blocks, (own_ref, oth_ref, mine_ref, theirs_ref, rows) = refs[:NZ], refs[NZ:]
    for i, block in enumerate(blocks):
        rows[i * BLK : i * BLK + BLK, :] = block[...]
    for w_ref, o_ref in ((oth_ref, theirs_ref), (own_ref, mine_ref)):
        out = jnp.dot(rows[...], w_ref[...], preferred_element_type=jnp.float32)
        o_ref[:, :HD] = (out[:, :HD] * EXP_SCALE).astype(jnp.bfloat16)
        o_ref[:, HD:] = out[:, HD:].astype(jnp.bfloat16)


def project(blocks, w_own, w_oth):
    width, cols = w_own.shape
    rows = len(blocks) * BLK
    vmem = pl.BlockSpec(memory_space=pltpu.VMEM)
    return pl.pallas_call(
        project_kernel,
        in_specs=[vmem] * (len(blocks) + 2),
        out_specs=[vmem, vmem],
        out_shape=[jax.ShapeDtypeStruct((rows, cols), jnp.bfloat16)] * 2,
        scratch_shapes=[pltpu.VMEM((rows, width), jnp.bfloat16)],
        compiler_params=pltpu.CompilerParams(vmem_limit_bytes=16 * 2**20),
        cost_estimate=pl.CostEstimate(
            flops=4 * rows * width * cols,
            bytes_accessed=4 * width * cols + 2 * rows * width,
            transcendentals=0,
        ),
        name="project",
    )(*blocks, w_own, w_oth)


def dot_t(a, b):
    return lax.dot_general(a, b, (((1,), (1,)), ((), ())), preferred_element_type=jnp.float32)


TILE = 128


def used_slots(y, z):
    return (y * NZ + z) * NC < HEADS


def self_kernel(s_ref, q_ref, kv_ref, m_ref, o_ref, acc_ref, top_ref, values):
    y, z, core = s_ref[1], s_ref[2], s_ref[3]
    used = used_slots(y, z)
    values[:, :HD] = kv_ref[:, HD:]
    values[:, HD:] = jnp.ones((values.shape[0], HD), jnp.bfloat16)
    for t in range(q_ref.shape[0] // TILE):
        s = dot_t(q_ref[t * TILE : t * TILE + TILE, :], kv_ref[:, :HD])
        top = jnp.max(s, axis=1, keepdims=True)
        p = jnp.exp2(s - top).astype(jnp.bfloat16)
        acc = jnp.dot(p, values[...], preferred_element_type=jnp.float32)
        acc_ref[t * TILE : t * TILE + TILE, :] = acc
        top_ref[t * TILE : t * TILE + TILE, :] = jnp.broadcast_to(top, (TILE, 128))
        att = (acc[:, :HD] / acc[:, HD:]).astype(jnp.bfloat16)
        att = jnp.concatenate([att, att], axis=1)
        part = jnp.dot(att, m_ref[...], preferred_element_type=jnp.float32)
        part = jnp.where(used, part, 0.0).astype(jnp.bfloat16)
        for j in range(TILE // BLK):
            y_apart, core_apart, d = block_of(t * (TILE // BLK) + j)
            at = ((y ^ y_apart) * NZ + (z + d) % NZ) * NC + (core ^ core_apart)
            low, high = j * BLK, j * BLK + BLK // 2
            o_ref[at] = jnp.concatenate(
                [part[low:high, :], part[high : high + BLK // 2, :]], axis=1
            )


def self_attention(place, q, kv, matrix):
    pv = matrix.shape[1]
    rows = q.shape[0]
    return pl.pallas_call(
        self_kernel,
        grid_spec=pltpu.PrefetchScalarGridSpec(
            num_scalar_prefetch=1,
            grid=(1,),
            in_specs=[pl.BlockSpec(a.shape, lambda i, s: (0, 0)) for a in (q, kv, matrix)],
            out_specs=[
                pl.BlockSpec((rows // BLK, BLK // 2, 2 * pv), lambda i, s: (0, 0, 0)),
                pl.BlockSpec((rows, 2 * HD), lambda i, s: (0, 0)),
                pl.BlockSpec((rows, 128), lambda i, s: (0, 0)),
            ],
            scratch_shapes=[pltpu.VMEM((rows, 2 * HD), jnp.bfloat16)],
        ),
        out_shape=[
            jax.ShapeDtypeStruct((rows // BLK, BLK // 2, 2 * pv), jnp.bfloat16),
            jax.ShapeDtypeStruct((rows, 2 * HD), jnp.float32),
            jax.ShapeDtypeStruct((rows, 128), jnp.float32),
        ],
        compiler_params=pltpu.CompilerParams(vmem_limit_bytes=16 * 2**20),
        cost_estimate=pl.CostEstimate(
            flops=6 * rows * rows * HD, bytes_accessed=2**20, transcendentals=rows * rows
        ),
        name="self_attention",
    )(place, q, kv, matrix)


def visit(refs, q, values, acc, top):
    at = 0
    for ref in refs:
        values[at : at + ref.shape[0], :HD] = ref[:, HD:]
        at += ref.shape[0]
    values[:, HD:] = jnp.ones((values.shape[0], HD), jnp.bfloat16)
    for t in range(q.shape[0] // TILE):
        rows = slice(t * TILE, t * TILE + TILE)
        parts = [dot_t(q[rows, :], ref[:, :HD]) for ref in refs]
        old = top[rows, :1]
        new = old
        for s in parts:
            new = jnp.maximum(new, jnp.max(s, axis=1, keepdims=True))
        p = jnp.concatenate([jnp.exp2(s - new).astype(jnp.bfloat16) for s in parts], axis=1)
        acc[rows, :] = acc[rows, :] * jnp.exp2(old - new) + jnp.dot(
            p, values[...], preferred_element_type=jnp.float32
        )
        top[rows, :] = jnp.broadcast_to(new, (TILE, 128))


def sees(order_ref, s_ref, dh, dx):
    x, h = s_ref[4], s_ref[0]
    mine = order_ref[x * NH + (h ^ dh)]
    return order_ref[((x + dx) % NX) * NH + h] <= mine


def near_kernel(order_ref, s_ref, qa_ref, qb_ref, acc_in, top_in, k0, k1, k2, *refs):
    acc_ref, top_ref, q, values = refs
    dh = pl.program_id(0)
    q[...] = jnp.where(dh == 0, qa_ref[...], qb_ref[...])

    @pl.when(dh == 0)
    def _():
        acc_ref[0] = acc_in[...]
        top_ref[0] = top_in[...]

    @pl.when(dh == 1)
    def _():
        acc_ref[...] = jnp.zeros_like(acc_ref)
        top_ref[...] = jnp.full_like(top_ref, -NEG_LARGE)

    add = lambda ref: functools.partial(visit, (ref,), q, values, acc_ref.at[0], top_ref.at[0])
    pl.when((dh == 1) & sees(order_ref, s_ref, dh, 0))(add(k0))
    pl.when(sees(order_ref, s_ref, dh, NX - 1))(add(k1))
    pl.when(sees(order_ref, s_ref, dh, 1))(add(k2))


def far_kernel(order_ref, s_ref, qa_ref, qb_ref, acc_in, top_in, k3a, k3b, o_ref, *scratch):
    q, values, acc, top = scratch
    dh = pl.program_id(0)
    q[...] = jnp.where(dh == 0, qa_ref[...], qb_ref[...])
    acc[...] = acc_in[0]
    top[...] = top_in[0]
    pl.when(sees(order_ref, s_ref, dh, 2))(
        functools.partial(visit, (k3a, k3b), q, values, acc, top)
    )
    y, core = s_ref[1], s_ref[3]
    for quarter in range(4):
        starts = [block_at(quarter // 2, quarter % 2, d) * BLK for d in range(NZ)]
        gather = lambda ref, cols: jnp.concatenate([ref[i : i + BLK, cols] for i in starts], axis=0)
        total = gather(acc, slice(HD, 2 * HD))
        some = total > 0.0
        safe = jnp.where(some, total, 1.0)
        at = quarter ^ (y * 2 + core)
        o_ref[at, :QUARTER, :] = (gather(acc, slice(0, HD)) / safe).astype(jnp.bfloat16)
        lse = jnp.where(some, gather(top, slice(0, 128)) + jnp.log2(safe), -NEG_LARGE)
        row = lse.T[0:1, :]
        row = jnp.concatenate([row[:, :128], row[:, 128:]], axis=0)
        hi = row.astype(jnp.bfloat16).astype(jnp.float32)
        rest = row - hi
        mid = rest.astype(jnp.bfloat16).astype(jnp.float32)
        pad = jnp.zeros((TAIL - 6, 128), jnp.float32)
        o_ref[at, QUARTER:, :] = jnp.concatenate([hi, mid, rest - mid, pad], axis=0).astype(
            jnp.bfloat16
        )


def whole(a):
    return pl.BlockSpec(a.shape, lambda i, *s: (0,) * a.ndim)


def attention_cost(units, rows):
    pairs = 2 * units * rows * rows
    return pl.CostEstimate(flops=6 * pairs * HD, bytes_accessed=4 * 2**20, transcendentals=pairs)


def near_attention(order, place, qa, qb, acc, top, blocks):
    rows = qa.shape[0]
    out = lambda cols: pl.BlockSpec((1, rows, cols), lambda i, *s: (i, 0, 0))
    return pl.pallas_call(
        near_kernel,
        grid_spec=pltpu.PrefetchScalarGridSpec(
            num_scalar_prefetch=2,
            grid=(NH,),
            in_specs=[whole(a) for a in (qa, qb, acc, top, *blocks)],
            out_specs=[out(2 * HD), out(128)],
            scratch_shapes=[
                pltpu.VMEM((rows, HD), jnp.bfloat16),
                pltpu.VMEM((rows, 2 * HD), jnp.bfloat16),
            ],
        ),
        out_shape=[
            jax.ShapeDtypeStruct((NH, rows, 2 * HD), jnp.float32),
            jax.ShapeDtypeStruct((NH, rows, 128), jnp.float32),
        ],
        compiler_params=pltpu.CompilerParams(vmem_limit_bytes=20 * 2**20),
        cost_estimate=attention_cost(3, rows),
        name="near_attention",
    )(order, place, qa, qb, acc, top, *blocks)


def far_attention(order, place, qa, qb, acc, top, blocks):
    rows = qa.shape[0]
    chunk = QUARTER + TAIL
    part = lambda a: pl.BlockSpec((1,) + a.shape[1:], lambda i, *s: (i, 0, 0))
    return pl.pallas_call(
        far_kernel,
        grid_spec=pltpu.PrefetchScalarGridSpec(
            num_scalar_prefetch=2,
            grid=(NH,),
            in_specs=[whole(qa), whole(qb), part(acc), part(top)] + [whole(b) for b in blocks],
            out_specs=pl.BlockSpec((4, chunk, HD), lambda i, o, s: (i ^ s[0], 0, 0)),
            scratch_shapes=[
                pltpu.VMEM((rows, HD), jnp.bfloat16),
                pltpu.VMEM((rows, 2 * HD), jnp.bfloat16),
                pltpu.VMEM((rows, 2 * HD), jnp.float32),
                pltpu.VMEM((rows, 128), jnp.float32),
            ],
        ),
        out_shape=jax.ShapeDtypeStruct((NH * 4, chunk, HD), jnp.bfloat16),
        compiler_params=pltpu.CompilerParams(vmem_limit_bytes=20 * 2**20),
        cost_estimate=attention_cost(1, rows),
        name="far_attention",
    )(order, place, qa, qb, acc, top, *blocks)


def join_kernel(s_ref, in_ref, w0_ref, w1_ref, w2_ref, w3_ref, o_ref, a_ref, w_ref):
    h, y, z, core = s_ref[0], s_ref[1], s_ref[2], s_ref[3]
    place = h * 4 + y * 2 + core

    @pl.when(pl.program_id(0) == 0)
    def _():
        for r in range(4):
            used = used_slots(y ^ (r // 2), z)
            parts = []
            for dh in range(NH):
                at = (dh * 4 + r) ^ place
                rows = in_ref[at, QUARTER:, :].astype(jnp.float32)
                parts.append((at, rows[0:2] + rows[2:4] + rows[4:6]))
            top = jnp.maximum(parts[0][1], parts[1][1])
            e = [jnp.exp2(lse - top) for _, lse in parts]
            norm = e[0] + e[1]
            for half in range(2):
                out = None
                for (at, _), weight in zip(parts, e):
                    w = jnp.where(used, weight / norm, 0.0)[half : half + 1, :]
                    col = jnp.broadcast_to(w, (128, 128)).T
                    term = in_ref[at, half * 128 : half * 128 + 128, :].astype(jnp.float32) * col
                    out = term if out is None else out + term
                out = out.astype(jnp.bfloat16)
                for j in range(4):
                    start = pl.multiple_of(((z + half * 4 + j) % NZ) * BLK, BLK)
                    a_ref[pl.ds(start, BLK), r * HD : r * HD + HD] = out[j * BLK : j * BLK + BLK]

    for r, ref in enumerate((w0_ref, w1_ref, w2_ref, w3_ref)):
        w_ref[r * HD : r * HD + HD, :] = ref[...]
    o_ref[...] = jnp.dot(a_ref[...], w_ref[...], preferred_element_type=jnp.float32).astype(
        jnp.bfloat16
    )


def join_heads(place, received, weights):
    width = weights[0].shape[1]
    step = width // 4
    return pl.pallas_call(
        join_kernel,
        grid_spec=pltpu.PrefetchScalarGridSpec(
            num_scalar_prefetch=1,
            grid=(4,),
            in_specs=[whole(received)] + [pl.BlockSpec((HD, step), lambda i, s: (0, i))] * 4,
            out_specs=pl.BlockSpec((QUARTER, step), lambda i, s: (0, i)),
            scratch_shapes=[
                pltpu.VMEM((QUARTER, 4 * HD), jnp.bfloat16),
                pltpu.VMEM((4 * HD, step), jnp.bfloat16),
            ],
        ),
        out_shape=jax.ShapeDtypeStruct((QUARTER, width), jnp.bfloat16),
        compiler_params=pltpu.CompilerParams(vmem_limit_bytes=16 * 2**20),
        name="join_heads",
    )(place, received, *weights)


def decode(latents, root_kernel):
    seq_count = latents.shape[0]
    row_patches = seq_count // FR
    me = lax.axis_index("seq")
    ringed = jnp.concatenate([latents[-1:], latents, latents[:1]], axis=0)
    position = (me - row_patches // 2 + seq_count) % seq_count
    patch_row = position % row_patches
    frame_index = position // row_patches
    row_ids = jnp.arange(P_SIZE + 2, dtype=jnp.int32)
    keep = jnp.where(
        row_ids == 0,
        patch_row > 0,
        jnp.where(row_ids == P_SIZE + 1, patch_row < row_patches - 1, True),
    )
    width_cols = BLK * P_SIZE
    windows = []
    for lag in range(3):
        start = (me - lag * row_patches + seq_count) % seq_count
        three = lax.dynamic_slice_in_dim(ringed, start, 3, axis=0)
        pv = three.shape[2] // 2
        three = jnp.concatenate([three[:, :, :pv], three[:, :, pv:]], axis=1)
        slab = (
            three.reshape(3, BLK, P_SIZE, P_SIZE, C)
            .transpose(0, 2, 1, 3, 4)
            .reshape(3 * P_SIZE, width_cols, C)
        )[P_SIZE - 1 : 2 * P_SIZE + 1]
        ok = keep & (frame_index >= lag)
        slab = jnp.where(ok[:, None, None], slab, jnp.zeros_like(slab))
        framed = jnp.pad(slab, ((0, 0), (1, 1), (0, 0)))
        for row_off in range(3):
            for col_off in range(3):
                windows.append(framed[row_off : row_off + P_SIZE, col_off : col_off + width_cols])
    stacked = jnp.concatenate(windows, axis=-1).reshape(P_SIZE * width_cols, 27 * C)
    decoded = jnp.dot(stacked, root_kernel, preferred_element_type=jnp.float32)
    return decoded.reshape(P_SIZE, width_cols, root_kernel.shape[1]).astype(jnp.bfloat16)[None]


def after(value, earlier):
    return lax.optimization_barrier((value, earlier))[0]


def per_device(
    hidden, levels, span_order, modulation, in_weight, out_weight, latent_weight, decoder_weight
):
    span_me = lax.axis_index("span")
    seq_me = lax.axis_index("seq")
    x, h = span_me // NH, span_me % NH
    y, z, core = seq_me // (NZ * NC), (seq_me // NC) % NZ, seq_me % NC
    place = jnp.stack([h, y, z, core, x])
    seq_count = NY * NZ * NC

    normed, gate_row = normalize(levels, hidden[0], modulation)
    w_own = in_weight[0]
    own_blocks, other_blocks = gather_class(normed)
    w_oth = move_core(w_own)
    mine_a, theirs_a = project(own_blocks, w_own, w_oth)
    mine_b, theirs_b = project(other_blocks, w_own, w_oth)
    triples = jnp.concatenate([mine_a, move_core(theirs_a), mine_b, move_core(theirs_b)], axis=0)
    q = triples[:, :HD]
    kv = triples[:, HD:]

    half = kv.shape[0] // 2
    kv_up, kv_dn = move_x(kv, 1), move_x(kv, -1)
    q_hi = move_hi(q)
    kv_far = (move_x(kv_up[:half], 1), move_x(kv_dn[half:], -1))

    matrix = latent_matrix(after(out_weight[0], mine_b), gate_row, latent_weight)
    part, acc, top = self_attention(place, q, kv, matrix)
    part = lax.all_to_all(part, "seq", 0, 0, tiled=True)

    out_w = after(out_weight[0], mine_b)
    w_core, w_far = move_core(out_w), move_y(out_w)
    weights = (out_w, w_core, w_far, move_core(w_far))

    acc, top = near_attention(span_order, place, q, q_hi, acc, top, (kv, kv_up, kv_dn))
    acc = after(acc, part)
    chunks = far_attention(span_order, place, q, q_hi, acc, top, kv_far)
    groups = [
        [
            span_at(i, hh) * seq_count + seq_at(yy, j, cc)
            for hh in range(NH)
            for yy in range(NY)
            for cc in range(NC)
        ]
        for i in range(NX)
        for j in range(NZ)
    ]
    received = lax.all_to_all(
        chunks, ("span", "seq"), 0, 0, tiled=True, axis_index_groups=groups
    )
    partial = join_heads(place, received, weights)
    z_groups = [[seq_at(yy, j, cc) for j in range(NZ)] for yy in range(NY) for cc in range(NC)]
    part = after(part, partial)
    summed = lax.psum_scatter(
        partial, "seq", scatter_dimension=0, tiled=True, axis_index_groups=z_groups
    ).astype(jnp.float32)
    block_out = (hidden[0].astype(jnp.float32) + gate_row * summed).astype(jnp.bfloat16)[None]

    own_latents = jnp.dot(hidden[0], latent_weight, preferred_element_type=jnp.float32)
    own_latents = jnp.concatenate([own_latents[: BLK // 2], own_latents[BLK // 2 :]], axis=1)
    latents = (jnp.sum(part.astype(jnp.float32), axis=0) + own_latents).astype(jnp.bfloat16)
    group_ids = jnp.arange(span_order.shape[0], dtype=jnp.int32)
    root = jnp.sum(jnp.where(span_order == 0, group_ids, 0))
    spread = lax.all_to_all(
        jnp.broadcast_to(latents[None], (NX * NH,) + latents.shape), "span", 0, 0, tiled=True
    )
    latents = lax.dynamic_index_in_dim(spread, root, 0, keepdims=True)
    every = lax.all_to_all(
        jnp.broadcast_to(latents, (seq_count,) + latents.shape[1:]), "seq", 0, 0, tiled=True
    )
    decoded = decode(every, decoder_weight.reshape(27 * C, decoder_weight.shape[4]))
    return (block_out, decoded)


def solution(mesh):
    placed = (
        P("span", "seq", None),
        P("span"),
        P(),
        P(),
        P("seq", None, None),
        P("seq", None, None),
        P(),
        P(None, None, None, None, "span"),
    )
    return jax.shard_map(
        per_device,
        mesh=mesh,
        in_specs=placed,
        out_specs=(P("span", "seq", None), P("seq", None, None, "span")),
        check_vma=False,
    )
```

```python
import functools
import math

import jax
import jax.numpy as jnp
from jax import lax
from jax.experimental import pallas as pl
from jax.experimental.pallas import tpu as pltpu
from jax.sharding import PartitionSpec as P

HEADS = 24
FR = 4
P_SIZE = 2
C = 16
HD = 128

EPSILON = 1e-06
NEG_LARGE = 1e30

NX, NH, NY, NZ, NC = 4, 2, 2, 8, 2
BLK = 32
QUARTER = NZ * BLK
TAIL = 16


def seq_at(y, z, c):
    return ((y % NY) * NZ + z % NZ) * NC + c % NC


def span_at(x, h):
    return (x % NX) * NH + h % NH


def seq_route(dy=0, dz=0, dc=0):
    return [
        (seq_at(y, z, c), seq_at(y + dy, z + dz, c + dc))
        for y in range(NY)
        for z in range(NZ)
        for c in range(NC)
    ]


def span_route(dx=0, dh=0):
    return [(span_at(x, h), span_at(x + dx, h + dh)) for x in range(NX) for h in range(NH)]


def move_z(a, d):
    return lax.ppermute(a, "seq", seq_route(dz=d))


def move_y(a):
    return lax.ppermute(a, "seq", seq_route(dy=1))


def move_core(a):
    return lax.ppermute(a, "seq", seq_route(dc=1))


def move_x(a, d):
    return lax.ppermute(a, "span", span_route(dx=d))


def move_hi(a):
    return lax.ppermute(a, "span", span_route(dh=1))


HALVES = (
    ((0, 0), (0, 1), (0, 2), (0, 6), (0, 7), (1, 0), (1, 1), (1, 7)),
    ((0, 3), (0, 4), (0, 5), (1, 2), (1, 3), (1, 4), (1, 5), (1, 6)),
)


def block_at(y_apart, core_apart, d):
    half = 0 if (y_apart, d) in HALVES[0] else 1
    return half * 2 * NZ + core_apart * NZ + HALVES[half].index((y_apart, d))


def block_of(at):
    half, core_apart, i = at // (2 * NZ), at // NZ % 2, at % NZ
    y_apart, d = HALVES[half][i]
    return y_apart, core_apart, d


def gather_class(b):
    up1, dn1, y0 = move_z(b, 1), move_z(b, -1), move_y(b)
    up2, dn2 = move_z(up1, 1), move_z(dn1, -1)
    yu1, yd1 = move_y(up1), move_y(dn1)
    up3, dn3 = move_z(up2, 1), move_z(dn2, -1)
    yu2, yd2 = move_y(up2), move_y(dn2)
    far = move_z(up3, 1)
    yu3, yd3 = move_z(yu2, 1), move_z(yd2, -1)
    yfar = lax.ppermute(dn3, "seq", seq_route(dy=1, dz=-1))
    return (b, dn1, dn2, up2, up1, y0, yd1, yu1), (dn3, far, up3, yd2, yd3, yfar, yu3, yu2)


EXP_SCALE = math.log2(math.e) / math.sqrt(HD)


def norm_kernel(level_ref, hidden_ref, mod_ref, out_ref, gate_ref):
    values = hidden_ref[...].astype(jnp.float32)
    row = pl.ds(level_ref[0] % MOD_ROWS, 1)
    center = values - jnp.mean(values, axis=-1, keepdims=True)
    spread = jnp.mean(center * center, axis=-1, keepdims=True)
    scaled = center * lax.rsqrt(spread + EPSILON)
    out_ref[...] = (scaled * (1.0 + mod_ref[1, row, :]) + mod_ref[0, row, :]).astype(jnp.bfloat16)
    gate_ref[...] = mod_ref[2, row, :]


MOD_ROWS = 8


def normalize(levels, rows, modulation):
    width = rows.shape[1]
    return pl.pallas_call(
        norm_kernel,
        grid_spec=pltpu.PrefetchScalarGridSpec(
            num_scalar_prefetch=1,
            grid=(1,),
            in_specs=[
                pl.BlockSpec(rows.shape, lambda i, s: (0, 0)),
                pl.BlockSpec((3, MOD_ROWS, width), lambda i, s: (0, s[0] // MOD_ROWS, 0)),
            ],
            out_specs=[
                pl.BlockSpec(rows.shape, lambda i, s: (0, 0)),
                pl.BlockSpec((1, width), lambda i, s: (0, 0)),
            ],
        ),
        out_shape=[
            jax.ShapeDtypeStruct(rows.shape, jnp.bfloat16),
            jax.ShapeDtypeStruct((1, width), jnp.float32),
        ],
        name="normalize",
    )(levels, rows, modulation.transpose(1, 0, 2))


def latent_kernel(w_ref, gate_ref, lw_ref, o_ref):
    gated = w_ref[...].astype(jnp.float32) * gate_ref[...]
    hi = gated.astype(jnp.bfloat16)
    lo = (gated - hi.astype(jnp.float32)).astype(jnp.bfloat16)
    out = dot_t(hi, lw_ref[...]) + dot_t(lo, lw_ref[...])
    top = out.astype(jnp.bfloat16)
    o_ref[: w_ref.shape[0], :] = top
    o_ref[w_ref.shape[0] :, :] = (out - top.astype(jnp.float32)).astype(jnp.bfloat16)


def latent_matrix(w, gate_row, latent_weight):
    pv = latent_weight.shape[1]
    return pl.pallas_call(
        latent_kernel,
        out_shape=jax.ShapeDtypeStruct((2 * w.shape[0], pv), jnp.bfloat16),
        compiler_params=pltpu.CompilerParams(vmem_limit_bytes=16 * 2**20),
        name="latent_matrix",
    )(w, gate_row, latent_weight.T)


def project_kernel(*refs):
    blocks, (own_ref, oth_ref, q_ref, kv_ref, theirs_ref, rows) = refs[:NZ], refs[NZ:]
    for i, block in enumerate(blocks):
        rows[i * BLK : i * BLK + BLK, :] = block[...]
    out = jnp.dot(rows[...], oth_ref[...], preferred_element_type=jnp.float32)
    theirs_ref[:, :HD] = (out[:, :HD] * EXP_SCALE).astype(jnp.bfloat16)
    theirs_ref[:, HD:] = out[:, HD:].astype(jnp.bfloat16)
    out = jnp.dot(rows[...], own_ref[...], preferred_element_type=jnp.float32)
    q_ref[...] = (out[:, :HD] * EXP_SCALE).astype(jnp.bfloat16)
    kv_ref[...] = out[:, HD:].astype(jnp.bfloat16)


def project(blocks, w_own, w_oth):
    width, cols = w_own.shape
    rows = len(blocks) * BLK
    vmem = pl.BlockSpec(memory_space=pltpu.VMEM)
    return pl.pallas_call(
        project_kernel,
        in_specs=[vmem] * (len(blocks) + 2),
        out_specs=[vmem, vmem, vmem],
        out_shape=[jax.ShapeDtypeStruct((rows, n), jnp.bfloat16) for n in (HD, 2 * HD, cols)],
        scratch_shapes=[pltpu.VMEM((rows, width), jnp.bfloat16)],
        compiler_params=pltpu.CompilerParams(vmem_limit_bytes=16 * 2**20),
        cost_estimate=pl.CostEstimate(
            flops=4 * rows * width * cols,
            bytes_accessed=4 * width * cols + 2 * rows * width,
            transcendentals=0,
        ),
        name="project",
    )(*blocks, w_own, w_oth)


def dot_t(a, b):
    return lax.dot_general(a, b, (((1,), (1,)), ((), ())), preferred_element_type=jnp.float32)


TILE = 128


def used_slots(y, z):
    return (y * NZ + z) * NC < HEADS


def self_kernel(s_ref, q_ref, kv_ref, m_ref, o_ref, acc_ref, top_ref, values):
    y, z, core = s_ref[1], s_ref[2], s_ref[3]
    used = used_slots(y, z)
    values[:, :HD] = kv_ref[:, HD:]
    values[:, HD:] = jnp.ones((values.shape[0], HD), jnp.bfloat16)
    for t in range(q_ref.shape[0] // TILE):
        s = dot_t(q_ref[t * TILE : t * TILE + TILE, :], kv_ref[:, :HD])
        top = jnp.max(s, axis=1, keepdims=True)
        p = jnp.exp2(s - top).astype(jnp.bfloat16)
        acc = jnp.dot(p, values[...], preferred_element_type=jnp.float32)
        acc_ref[t * TILE : t * TILE + TILE, :] = acc
        top_ref[t * TILE : t * TILE + TILE, :] = jnp.broadcast_to(top, (TILE, 128))
        att = (acc[:, :HD] / acc[:, HD:]).astype(jnp.bfloat16)
        att = jnp.concatenate([att, att], axis=1)
        part = jnp.dot(att, m_ref[...], preferred_element_type=jnp.float32)
        part = jnp.where(used, part, 0.0).astype(jnp.bfloat16)
        for j in range(TILE // BLK):
            y_apart, core_apart, d = block_of(t * (TILE // BLK) + j)
            at = ((y ^ y_apart) * NZ + (z + d) % NZ) * NC + (core ^ core_apart)
            low, high = j * BLK, j * BLK + BLK // 2
            o_ref[at] = jnp.concatenate(
                [part[low:high, :], part[high : high + BLK // 2, :]], axis=1
            )


def self_attention(place, q, kv, matrix):
    pv = matrix.shape[1]
    rows = q.shape[0]
    return pl.pallas_call(
        self_kernel,
        grid_spec=pltpu.PrefetchScalarGridSpec(
            num_scalar_prefetch=1,
            grid=(1,),
            in_specs=[pl.BlockSpec(a.shape, lambda i, s: (0, 0)) for a in (q, kv, matrix)],
            out_specs=[
                pl.BlockSpec((rows // BLK, BLK // 2, 2 * pv), lambda i, s: (0, 0, 0)),
                pl.BlockSpec((rows, 2 * HD), lambda i, s: (0, 0)),
                pl.BlockSpec((rows, 128), lambda i, s: (0, 0)),
            ],
            scratch_shapes=[pltpu.VMEM((rows, 2 * HD), jnp.bfloat16)],
        ),
        out_shape=[
            jax.ShapeDtypeStruct((rows // BLK, BLK // 2, 2 * pv), jnp.bfloat16),
            jax.ShapeDtypeStruct((rows, 2 * HD), jnp.float32),
            jax.ShapeDtypeStruct((rows, 128), jnp.float32),
        ],
        compiler_params=pltpu.CompilerParams(vmem_limit_bytes=16 * 2**20),
        cost_estimate=pl.CostEstimate(
            flops=6 * rows * rows * HD, bytes_accessed=2**20, transcendentals=rows * rows
        ),
        name="self_attention",
    )(place, q, kv, matrix)


def visit(kv_ref, q, values, acc, top):
    values[:, :HD] = kv_ref[:, HD:]
    values[:, HD:] = jnp.ones((values.shape[0], HD), jnp.bfloat16)
    for t in range(q.shape[0] // TILE):
        rows = slice(t * TILE, t * TILE + TILE)
        s = dot_t(q[rows, :], kv_ref[:, :HD])
        old = top[rows, :1]
        new = jnp.maximum(old, jnp.max(s, axis=1, keepdims=True))
        p = jnp.exp2(s - new).astype(jnp.bfloat16)
        acc[rows, :] = acc[rows, :] * jnp.exp2(old - new) + jnp.dot(
            p, values[...], preferred_element_type=jnp.float32
        )
        top[rows, :] = jnp.broadcast_to(new, (TILE, 128))


def sees(order_ref, s_ref, dh, dx):
    x, h = s_ref[4], s_ref[0]
    mine = order_ref[x * NH + (h ^ dh)]
    return order_ref[((x + dx) % NX) * NH + h] <= mine


def other_kernel(order_ref, s_ref, qa_ref, qb_ref, acc_in, top_in, k0, k1, k2, k3, o_ref, *scratch):
    q, values, acc, top = scratch
    dh = pl.program_id(0)
    q[...] = jnp.where(dh == 0, qa_ref[...], qb_ref[...])

    @pl.when(dh == 0)
    def _():
        acc[...] = acc_in[...]
        top[...] = top_in[...]

    @pl.when(dh == 1)
    def _():
        acc[...] = jnp.zeros_like(acc)
        top[...] = jnp.full_like(top, -NEG_LARGE)

    pl.when((dh == 1) & sees(order_ref, s_ref, dh, 0))(
        functools.partial(visit, k0, q, values, acc, top)
    )
    for dx, ref in ((NX - 1, k1), (1, k2), (2, k3)):
        pl.when(sees(order_ref, s_ref, dh, dx))(
            functools.partial(visit, ref, q, values, acc, top)
        )
    y, core = s_ref[1], s_ref[3]
    for quarter in range(4):
        starts = [block_at(quarter // 2, quarter % 2, d) * BLK for d in range(NZ)]
        gather = lambda ref, cols: jnp.concatenate([ref[i : i + BLK, cols] for i in starts], axis=0)
        total = gather(acc, slice(HD, 2 * HD))
        some = total > 0.0
        safe = jnp.where(some, total, 1.0)
        at = quarter ^ (y * 2 + core)
        o_ref[at, :QUARTER, :] = (gather(acc, slice(0, HD)) / safe).astype(jnp.bfloat16)
        lse = jnp.where(some, gather(top, slice(0, 128)) + jnp.log2(safe), -NEG_LARGE)
        row = lse.T[0:1, :]
        row = jnp.concatenate([row[:, :128], row[:, 128:]], axis=0)
        hi = row.astype(jnp.bfloat16).astype(jnp.float32)
        rest = row - hi
        mid = rest.astype(jnp.bfloat16).astype(jnp.float32)
        pad = jnp.zeros((TAIL - 6, 128), jnp.float32)
        o_ref[at, QUARTER:, :] = jnp.concatenate([hi, mid, rest - mid, pad], axis=0).astype(
            jnp.bfloat16
        )


def whole(a):
    return pl.BlockSpec(a.shape, lambda i, *s: (0,) * a.ndim)


def attention_cost(units, rows):
    pairs = 2 * units * rows * rows
    return pl.CostEstimate(flops=6 * pairs * HD, bytes_accessed=4 * 2**20, transcendentals=pairs)


def other_attention(order, place, qa, qb, acc, top, blocks):
    rows = qa.shape[0]
    chunk = QUARTER + TAIL
    return pl.pallas_call(
        other_kernel,
        grid_spec=pltpu.PrefetchScalarGridSpec(
            num_scalar_prefetch=2,
            grid=(NH,),
            in_specs=[whole(a) for a in (qa, qb, acc, top, *blocks)],
            out_specs=pl.BlockSpec((4, chunk, HD), lambda i, o, s: (i ^ s[0], 0, 0)),
            scratch_shapes=[
                pltpu.VMEM((rows, HD), jnp.bfloat16),
                pltpu.VMEM((rows, 2 * HD), jnp.bfloat16),
                pltpu.VMEM((rows, 2 * HD), jnp.float32),
                pltpu.VMEM((rows, 128), jnp.float32),
            ],
        ),
        out_shape=jax.ShapeDtypeStruct((NH * 4, chunk, HD), jnp.bfloat16),
        compiler_params=pltpu.CompilerParams(vmem_limit_bytes=24 * 2**20),
        cost_estimate=attention_cost(3, rows),
        name="other_attention",
    )(order, place, qa, qb, acc, top, *blocks)


def join_kernel(s_ref, in_ref, w0_ref, w1_ref, w2_ref, w3_ref, o_ref, a_ref, w_ref):
    h, y, z, core = s_ref[0], s_ref[1], s_ref[2], s_ref[3]
    place = h * 4 + y * 2 + core

    @pl.when(pl.program_id(0) == 0)
    def _():
        for r in range(4):
            used = used_slots(y ^ (r // 2), z)
            parts = []
            for dh in range(NH):
                at = (dh * 4 + r) ^ place
                rows = in_ref[at, QUARTER:, :].astype(jnp.float32)
                parts.append((at, rows[0:2] + rows[2:4] + rows[4:6]))
            top = jnp.maximum(parts[0][1], parts[1][1])
            e = [jnp.exp2(lse - top) for _, lse in parts]
            norm = e[0] + e[1]
            for half in range(2):
                out = None
                for (at, _), weight in zip(parts, e):
                    w = jnp.where(used, weight / norm, 0.0)[half : half + 1, :]
                    col = jnp.broadcast_to(w, (128, 128)).T
                    term = in_ref[at, half * 128 : half * 128 + 128, :].astype(jnp.float32) * col
                    out = term if out is None else out + term
                out = out.astype(jnp.bfloat16)
                for j in range(4):
                    start = pl.multiple_of(((z + half * 4 + j) % NZ) * BLK, BLK)
                    a_ref[pl.ds(start, BLK), r * HD : r * HD + HD] = out[j * BLK : j * BLK + BLK]

    for r, ref in enumerate((w0_ref, w1_ref, w2_ref, w3_ref)):
        w_ref[r * HD : r * HD + HD, :] = ref[...]
    o_ref[...] = jnp.dot(a_ref[...], w_ref[...], preferred_element_type=jnp.float32).astype(
        jnp.bfloat16
    )


def join_heads(place, received, weights):
    width = weights[0].shape[1]
    step = width // 4
    return pl.pallas_call(
        join_kernel,
        grid_spec=pltpu.PrefetchScalarGridSpec(
            num_scalar_prefetch=1,
            grid=(4,),
            in_specs=[whole(received)] + [pl.BlockSpec((HD, step), lambda i, s: (0, i))] * 4,
            out_specs=pl.BlockSpec((QUARTER, step), lambda i, s: (0, i)),
            scratch_shapes=[
                pltpu.VMEM((QUARTER, 4 * HD), jnp.bfloat16),
                pltpu.VMEM((4 * HD, step), jnp.bfloat16),
            ],
        ),
        out_shape=jax.ShapeDtypeStruct((QUARTER, width), jnp.bfloat16),
        compiler_params=pltpu.CompilerParams(vmem_limit_bytes=16 * 2**20),
        name="join_heads",
    )(place, received, *weights)


def decode(latents, root_kernel):
    seq_count = latents.shape[0]
    row_patches = seq_count // FR
    me = lax.axis_index("seq")
    ringed = jnp.concatenate([latents[-1:], latents, latents[:1]], axis=0)
    position = (me - row_patches // 2 + seq_count) % seq_count
    patch_row = position % row_patches
    frame_index = position // row_patches
    row_ids = jnp.arange(P_SIZE + 2, dtype=jnp.int32)
    keep = jnp.where(
        row_ids == 0,
        patch_row > 0,
        jnp.where(row_ids == P_SIZE + 1, patch_row < row_patches - 1, True),
    )
    width_cols = BLK * P_SIZE
    windows = []
    for lag in range(3):
        start = (me - lag * row_patches + seq_count) % seq_count
        three = lax.dynamic_slice_in_dim(ringed, start, 3, axis=0)
        pv = three.shape[2] // 2
        three = jnp.concatenate([three[:, :, :pv], three[:, :, pv:]], axis=1)
        slab = (
            three.reshape(3, BLK, P_SIZE, P_SIZE, C)
            .transpose(0, 2, 1, 3, 4)
            .reshape(3 * P_SIZE, width_cols, C)
        )[P_SIZE - 1 : 2 * P_SIZE + 1]
        ok = keep & (frame_index >= lag)
        slab = jnp.where(ok[:, None, None], slab, jnp.zeros_like(slab))
        framed = jnp.pad(slab, ((0, 0), (1, 1), (0, 0)))
        for row_off in range(3):
            for col_off in range(3):
                windows.append(framed[row_off : row_off + P_SIZE, col_off : col_off + width_cols])
    stacked = jnp.concatenate(windows, axis=-1).reshape(P_SIZE * width_cols, 27 * C)
    decoded = jnp.dot(stacked, root_kernel, preferred_element_type=jnp.float32)
    return decoded.reshape(P_SIZE, width_cols, root_kernel.shape[1]).astype(jnp.bfloat16)[None]


def after(value, earlier):
    return lax.optimization_barrier((value, earlier))[0]


def per_device(
    hidden, levels, span_order, modulation, in_weight, out_weight, latent_weight, decoder_weight
):
    span_me = lax.axis_index("span")
    seq_me = lax.axis_index("seq")
    x, h = span_me // NH, span_me % NH
    y, z, core = seq_me // (NZ * NC), (seq_me // NC) % NZ, seq_me % NC
    place = jnp.stack([h, y, z, core, x])
    seq_count = NY * NZ * NC

    normed, gate_row = normalize(levels, hidden[0], modulation)
    w_own = in_weight[0]
    own_blocks, other_blocks = gather_class(normed)
    w_oth = move_core(w_own)
    q_a, kv_a, theirs_a = project(own_blocks, w_own, w_oth)
    q_b, kv_b, theirs_b = project(other_blocks, w_own, w_oth)
    theirs_a, theirs_b = move_core(theirs_a), move_core(theirs_b)
    q = jnp.concatenate([q_a, theirs_a[:, :HD], q_b, theirs_b[:, :HD]], axis=0)
    kv = jnp.concatenate([kv_a, theirs_a[:, HD:], kv_b, theirs_b[:, HD:]], axis=0)

    others = tuple(move_x(kv, d) for d in (1, NX - 1, 2))
    q_hi = move_hi(q)

    matrix = latent_matrix(after(out_weight[0], q_b), gate_row, latent_weight)
    part, acc, top = self_attention(place, q, kv, matrix)
    part = lax.all_to_all(part, "seq", 0, 0, tiled=True)

    out_w = after(out_weight[0], q_b)
    w_core, w_far = move_core(out_w), move_y(out_w)
    weights = (out_w, w_core, w_far, move_core(w_far))

    acc = after(acc, part)
    chunks = other_attention(span_order, place, q, q_hi, acc, top, (kv, *others))
    groups = [
        [
            span_at(i, hh) * seq_count + seq_at(yy, j, cc)
            for hh in range(NH)
            for yy in range(NY)
            for cc in range(NC)
        ]
        for i in range(NX)
        for j in range(NZ)
    ]
    received = lax.all_to_all(
        chunks, ("span", "seq"), 0, 0, tiled=True, axis_index_groups=groups
    )
    partial = join_heads(place, received, weights)
    z_groups = [[seq_at(yy, j, cc) for j in range(NZ)] for yy in range(NY) for cc in range(NC)]
    part = after(part, partial)
    summed = lax.psum_scatter(
        partial, "seq", scatter_dimension=0, tiled=True, axis_index_groups=z_groups
    ).astype(jnp.float32)
    block_out = (hidden[0].astype(jnp.float32) + gate_row * summed).astype(jnp.bfloat16)[None]

    own_latents = jnp.dot(hidden[0], latent_weight, preferred_element_type=jnp.float32)
    own_latents = jnp.concatenate([own_latents[: BLK // 2], own_latents[BLK // 2 :]], axis=1)
    latents = (jnp.sum(part.astype(jnp.float32), axis=0) + own_latents).astype(jnp.bfloat16)
    group_ids = jnp.arange(span_order.shape[0], dtype=jnp.int32)
    root = jnp.sum(jnp.where(span_order == 0, group_ids, 0))
    spread = lax.all_to_all(
        jnp.broadcast_to(latents[None], (NX * NH,) + latents.shape), "span", 0, 0, tiled=True
    )
    latents = lax.dynamic_index_in_dim(spread, root, 0, keepdims=True)
    every = lax.all_to_all(
        jnp.broadcast_to(latents, (seq_count,) + latents.shape[1:]), "seq", 0, 0, tiled=True
    )
    decoded = decode(every, decoder_weight.reshape(27 * C, decoder_weight.shape[4]))
    return (block_out, decoded)


def solution(mesh):
    placed = (
        P("span", "seq", None),
        P("span"),
        P(),
        P(),
        P("seq", None, None),
        P("seq", None, None),
        P(),
        P(None, None, None, None, "span"),
    )
    return jax.shard_map(
        per_device,
        mesh=mesh,
        in_specs=placed,
        out_specs=(P("span", "seq", None), P("seq", None, None, "span")),
        check_vma=False,
    )
```

```python
import functools
import math

import jax
import jax.numpy as jnp
from jax import lax
from jax.experimental import pallas as pl
from jax.experimental.pallas import tpu as pltpu
from jax.sharding import PartitionSpec as P

HEADS = 24
FR = 4
P_SIZE = 2
C = 16
HD = 128

EPSILON = 1e-06
NEG_LARGE = 1e30

NX, NH, NY, NZ, NC = 4, 2, 2, 8, 2
BLK = 32
QUARTER = NZ * BLK
TAIL = 16


def seq_at(y, z, c):
    return ((y % NY) * NZ + z % NZ) * NC + c % NC


def span_at(x, h):
    return (x % NX) * NH + h % NH


def seq_route(dy=0, dz=0, dc=0):
    return [
        (seq_at(y, z, c), seq_at(y + dy, z + dz, c + dc))
        for y in range(NY)
        for z in range(NZ)
        for c in range(NC)
    ]


def span_route(dx=0, dh=0):
    return [(span_at(x, h), span_at(x + dx, h + dh)) for x in range(NX) for h in range(NH)]


def move_z(a, d):
    return lax.ppermute(a, "seq", seq_route(dz=d))


def move_y(a):
    return lax.ppermute(a, "seq", seq_route(dy=1))


def move_core(a):
    return lax.ppermute(a, "seq", seq_route(dc=1))


def move_x(a, d):
    return lax.ppermute(a, "span", span_route(dx=d))


def move_hi(a):
    return lax.ppermute(a, "span", span_route(dh=1))


HALVES = (
    ((0, 0), (0, 1), (0, 2), (0, 6), (0, 7), (1, 0), (1, 1), (1, 7)),
    ((0, 3), (0, 4), (0, 5), (1, 2), (1, 3), (1, 4), (1, 5), (1, 6)),
)


def block_at(y_apart, core_apart, d):
    half = 0 if (y_apart, d) in HALVES[0] else 1
    return half * 2 * NZ + core_apart * NZ + HALVES[half].index((y_apart, d))


def block_of(at):
    half, core_apart, i = at // (2 * NZ), at // NZ % 2, at % NZ
    y_apart, d = HALVES[half][i]
    return y_apart, core_apart, d


def gather_class(b):
    up1, dn1, y0 = move_z(b, 1), move_z(b, -1), move_y(b)
    up2, dn2 = move_z(after(up1, y0), 1), move_z(dn1, -1)
    yu1, yd1 = move_y(up1), move_y(dn1)
    up3, dn3 = move_z(up2, 1), move_z(dn2, -1)
    yu2, yd2 = move_y(up2), move_y(dn2)
    far = move_z(after(up3, yu1), 1)
    yu3, yd3 = move_z(yu2, 1), move_z(yd2, -1)
    yfar = lax.ppermute(after(dn3, yd1), "seq", seq_route(dy=1, dz=-1))
    return (b, dn1, dn2, up2, up1, y0, yd1, yu1), (dn3, far, up3, yd2, yd3, yfar, yu3, yu2)


EXP_SCALE = math.log2(math.e) / math.sqrt(HD)


def norm_kernel(level_ref, hidden_ref, mod_ref, out_ref, gate_ref):
    values = hidden_ref[...].astype(jnp.float32)
    row = pl.ds(level_ref[0] % MOD_ROWS, 1)
    center = values - jnp.mean(values, axis=-1, keepdims=True)
    spread = jnp.mean(center * center, axis=-1, keepdims=True)
    scaled = center * lax.rsqrt(spread + EPSILON)
    out_ref[...] = (scaled * (1.0 + mod_ref[1, row, :]) + mod_ref[0, row, :]).astype(jnp.bfloat16)
    gate_ref[...] = mod_ref[2, row, :]


MOD_ROWS = 8


def normalize(levels, rows, modulation):
    width = rows.shape[1]
    return pl.pallas_call(
        norm_kernel,
        grid_spec=pltpu.PrefetchScalarGridSpec(
            num_scalar_prefetch=1,
            grid=(1,),
            in_specs=[
                pl.BlockSpec(rows.shape, lambda i, s: (0, 0)),
                pl.BlockSpec((3, MOD_ROWS, width), lambda i, s: (0, s[0] // MOD_ROWS, 0)),
            ],
            out_specs=[
                pl.BlockSpec(rows.shape, lambda i, s: (0, 0)),
                pl.BlockSpec((1, width), lambda i, s: (0, 0)),
            ],
        ),
        out_shape=[
            jax.ShapeDtypeStruct(rows.shape, jnp.bfloat16),
            jax.ShapeDtypeStruct((1, width), jnp.float32),
        ],
        name="normalize",
    )(levels, rows, modulation.transpose(1, 0, 2))


def latent_kernel(w_ref, gate_ref, lw_ref, o_ref):
    gated = w_ref[...].astype(jnp.float32) * gate_ref[...]
    hi = gated.astype(jnp.bfloat16)
    lo = (gated - hi.astype(jnp.float32)).astype(jnp.bfloat16)
    out = dot_t(hi, lw_ref[...]) + dot_t(lo, lw_ref[...])
    top = out.astype(jnp.bfloat16)
    o_ref[: w_ref.shape[0], :] = top
    o_ref[w_ref.shape[0] :, :] = (out - top.astype(jnp.float32)).astype(jnp.bfloat16)


def latent_matrix(w, gate_row, latent_weight):
    pv = latent_weight.shape[1]
    return pl.pallas_call(
        latent_kernel,
        out_shape=jax.ShapeDtypeStruct((2 * w.shape[0], pv), jnp.bfloat16),
        compiler_params=pltpu.CompilerParams(vmem_limit_bytes=16 * 2**20),
        name="latent_matrix",
    )(w, gate_row, latent_weight.T)


def project_kernel(*refs):
    blocks, (own_ref, oth_ref, mine_ref, theirs_ref, rows) = refs[:NZ], refs[NZ:]
    for i, block in enumerate(blocks):
        rows[i * BLK : i * BLK + BLK, :] = block[...]
    for w_ref, o_ref in ((oth_ref, theirs_ref), (own_ref, mine_ref)):
        out = jnp.dot(rows[...], w_ref[...], preferred_element_type=jnp.float32)
        o_ref[:, :HD] = (out[:, :HD] * EXP_SCALE).astype(jnp.bfloat16)
        o_ref[:, HD:] = out[:, HD:].astype(jnp.bfloat16)


def project(blocks, w_own, w_oth):
    width, cols = w_own.shape
    rows = len(blocks) * BLK
    vmem = pl.BlockSpec(memory_space=pltpu.VMEM)
    return pl.pallas_call(
        project_kernel,
        in_specs=[vmem] * (len(blocks) + 2),
        out_specs=[vmem, vmem],
        out_shape=[jax.ShapeDtypeStruct((rows, cols), jnp.bfloat16)] * 2,
        scratch_shapes=[pltpu.VMEM((rows, width), jnp.bfloat16)],
        compiler_params=pltpu.CompilerParams(vmem_limit_bytes=16 * 2**20),
        cost_estimate=pl.CostEstimate(
            flops=4 * rows * width * cols,
            bytes_accessed=4 * width * cols + 2 * rows * width,
            transcendentals=0,
        ),
        name="project",
    )(*blocks, w_own, w_oth)


def dot_t(a, b):
    return lax.dot_general(a, b, (((1,), (1,)), ((), ())), preferred_element_type=jnp.float32)


TILE = 128


def used_slots(y, z):
    return (y * NZ + z) * NC < HEADS


def self_kernel(s_ref, q_ref, kv_ref, m_ref, o_ref, acc_ref, top_ref, values):
    y, z, core = s_ref[1], s_ref[2], s_ref[3]
    used = used_slots(y, z)
    values[:, :HD] = kv_ref[:, HD:]
    values[:, HD:] = jnp.ones((values.shape[0], HD), jnp.bfloat16)
    for t in range(q_ref.shape[0] // TILE):
        s = dot_t(q_ref[t * TILE : t * TILE + TILE, :], kv_ref[:, :HD])
        top = jnp.max(s, axis=1, keepdims=True)
        p = jnp.exp2(s - top).astype(jnp.bfloat16)
        acc = jnp.dot(p, values[...], preferred_element_type=jnp.float32)
        acc_ref[t * TILE : t * TILE + TILE, :] = acc
        top_ref[t * TILE : t * TILE + TILE, :] = jnp.broadcast_to(top, (TILE, 128))
        att = (acc[:, :HD] / acc[:, HD:]).astype(jnp.bfloat16)
        att = jnp.concatenate([att, att], axis=1)
        part = jnp.dot(att, m_ref[...], preferred_element_type=jnp.float32)
        part = jnp.where(used, part, 0.0).astype(jnp.bfloat16)
        for j in range(TILE // BLK):
            y_apart, core_apart, d = block_of(t * (TILE // BLK) + j)
            at = ((y ^ y_apart) * NZ + (z + d) % NZ) * NC + (core ^ core_apart)
            low, high = j * BLK, j * BLK + BLK // 2
            o_ref[at] = jnp.concatenate(
                [part[low:high, :], part[high : high + BLK // 2, :]], axis=1
            )


def self_attention(place, q, kv, matrix):
    pv = matrix.shape[1]
    rows = q.shape[0]
    return pl.pallas_call(
        self_kernel,
        grid_spec=pltpu.PrefetchScalarGridSpec(
            num_scalar_prefetch=1,
            grid=(1,),
            in_specs=[pl.BlockSpec(a.shape, lambda i, s: (0, 0)) for a in (q, kv, matrix)],
            out_specs=[
                pl.BlockSpec((rows // BLK, BLK // 2, 2 * pv), lambda i, s: (0, 0, 0)),
                pl.BlockSpec((rows, 2 * HD), lambda i, s: (0, 0)),
                pl.BlockSpec((rows, 128), lambda i, s: (0, 0)),
            ],
            scratch_shapes=[pltpu.VMEM((rows, 2 * HD), jnp.bfloat16)],
        ),
        out_shape=[
            jax.ShapeDtypeStruct((rows // BLK, BLK // 2, 2 * pv), jnp.bfloat16),
            jax.ShapeDtypeStruct((rows, 2 * HD), jnp.float32),
            jax.ShapeDtypeStruct((rows, 128), jnp.float32),
        ],
        compiler_params=pltpu.CompilerParams(vmem_limit_bytes=16 * 2**20),
        cost_estimate=pl.CostEstimate(
            flops=6 * rows * rows * HD, bytes_accessed=2**20, transcendentals=rows * rows
        ),
        name="self_attention",
    )(place, q, kv, matrix)


def visit(kv_ref, q, values, acc, top):
    values[:, :HD] = kv_ref[:, HD:]
    values[:, HD:] = jnp.ones((values.shape[0], HD), jnp.bfloat16)
    for t in range(q.shape[0] // TILE):
        rows = slice(t * TILE, t * TILE + TILE)
        s = dot_t(q[rows, :], kv_ref[:, :HD])
        old = top[rows, :1]
        new = jnp.maximum(old, jnp.max(s, axis=1, keepdims=True))
        p = jnp.exp2(s - new).astype(jnp.bfloat16)
        acc[rows, :] = acc[rows, :] * jnp.exp2(old - new) + jnp.dot(
            p, values[...], preferred_element_type=jnp.float32
        )
        top[rows, :] = jnp.broadcast_to(new, (TILE, 128))


def sees(order_ref, s_ref, dh, dx):
    x, h = s_ref[4], s_ref[0]
    mine = order_ref[x * NH + (h ^ dh)]
    return order_ref[((x + dx) % NX) * NH + h] <= mine


def other_kernel(order_ref, s_ref, qa_ref, qb_ref, acc_in, top_in, k0, k1, k2, k3, o_ref, *scratch):
    q, values, acc, top = scratch
    dh = pl.program_id(0)
    q[...] = jnp.where(dh == 0, qa_ref[...], qb_ref[...])

    @pl.when(dh == 0)
    def _():
        acc[...] = acc_in[...]
        top[...] = top_in[...]

    @pl.when(dh == 1)
    def _():
        acc[...] = jnp.zeros_like(acc)
        top[...] = jnp.full_like(top, -NEG_LARGE)

    pl.when((dh == 1) & sees(order_ref, s_ref, dh, 0))(
        functools.partial(visit, k0, q, values, acc, top)
    )
    for dx, ref in ((NX - 1, k1), (1, k2), (2, k3)):
        pl.when(sees(order_ref, s_ref, dh, dx))(
            functools.partial(visit, ref, q, values, acc, top)
        )
    y, core = s_ref[1], s_ref[3]
    for quarter in range(4):
        starts = [block_at(quarter // 2, quarter % 2, d) * BLK for d in range(NZ)]
        gather = lambda ref, cols: jnp.concatenate([ref[i : i + BLK, cols] for i in starts], axis=0)
        total = gather(acc, slice(HD, 2 * HD))
        some = total > 0.0
        safe = jnp.where(some, total, 1.0)
        at = quarter ^ (y * 2 + core)
        o_ref[at, :QUARTER, :] = (gather(acc, slice(0, HD)) / safe).astype(jnp.bfloat16)
        lse = jnp.where(some, gather(top, slice(0, 128)) + jnp.log2(safe), -NEG_LARGE)
        row = lse.T[0:1, :]
        row = jnp.concatenate([row[:, :128], row[:, 128:]], axis=0)
        hi = row.astype(jnp.bfloat16).astype(jnp.float32)
        rest = row - hi
        mid = rest.astype(jnp.bfloat16).astype(jnp.float32)
        pad = jnp.zeros((TAIL - 6, 128), jnp.float32)
        o_ref[at, QUARTER:, :] = jnp.concatenate([hi, mid, rest - mid, pad], axis=0).astype(
            jnp.bfloat16
        )


def whole(a):
    return pl.BlockSpec(a.shape, lambda i, *s: (0,) * a.ndim)


def attention_cost(units, rows):
    pairs = 2 * units * rows * rows
    return pl.CostEstimate(flops=6 * pairs * HD, bytes_accessed=4 * 2**20, transcendentals=pairs)


def other_attention(order, place, qa, qb, acc, top, blocks):
    rows = qa.shape[0]
    chunk = QUARTER + TAIL
    return pl.pallas_call(
        other_kernel,
        grid_spec=pltpu.PrefetchScalarGridSpec(
            num_scalar_prefetch=2,
            grid=(NH,),
            in_specs=[whole(a) for a in (qa, qb, acc, top, *blocks)],
            out_specs=pl.BlockSpec((4, chunk, HD), lambda i, o, s: (i ^ s[0], 0, 0)),
            scratch_shapes=[
                pltpu.VMEM((rows, HD), jnp.bfloat16),
                pltpu.VMEM((rows, 2 * HD), jnp.bfloat16),
                pltpu.VMEM((rows, 2 * HD), jnp.float32),
                pltpu.VMEM((rows, 128), jnp.float32),
            ],
        ),
        out_shape=jax.ShapeDtypeStruct((NH * 4, chunk, HD), jnp.bfloat16),
        compiler_params=pltpu.CompilerParams(vmem_limit_bytes=24 * 2**20),
        cost_estimate=attention_cost(3, rows),
        name="other_attention",
    )(order, place, qa, qb, acc, top, *blocks)


def join_kernel(s_ref, in_ref, w0_ref, w1_ref, w2_ref, w3_ref, o_ref, a_ref, w_ref):
    h, y, z, core = s_ref[0], s_ref[1], s_ref[2], s_ref[3]
    place = h * 4 + y * 2 + core

    @pl.when(pl.program_id(0) == 0)
    def _():
        for r in range(4):
            used = used_slots(y ^ (r // 2), z)
            parts = []
            for dh in range(NH):
                at = (dh * 4 + r) ^ place
                rows = in_ref[at, QUARTER:, :].astype(jnp.float32)
                parts.append((at, rows[0:2] + rows[2:4] + rows[4:6]))
            top = jnp.maximum(parts[0][1], parts[1][1])
            e = [jnp.exp2(lse - top) for _, lse in parts]
            norm = e[0] + e[1]
            for half in range(2):
                out = None
                for (at, _), weight in zip(parts, e):
                    w = jnp.where(used, weight / norm, 0.0)[half : half + 1, :]
                    col = jnp.broadcast_to(w, (128, 128)).T
                    term = in_ref[at, half * 128 : half * 128 + 128, :].astype(jnp.float32) * col
                    out = term if out is None else out + term
                out = out.astype(jnp.bfloat16)
                for j in range(4):
                    start = pl.multiple_of(((z + half * 4 + j) % NZ) * BLK, BLK)
                    a_ref[pl.ds(start, BLK), r * HD : r * HD + HD] = out[j * BLK : j * BLK + BLK]

    for r, ref in enumerate((w0_ref, w1_ref, w2_ref, w3_ref)):
        w_ref[r * HD : r * HD + HD, :] = ref[...]
    o_ref[...] = jnp.dot(a_ref[...], w_ref[...], preferred_element_type=jnp.float32).astype(
        jnp.bfloat16
    )


def join_heads(place, received, weights):
    width = weights[0].shape[1]
    step = width // 4
    return pl.pallas_call(
        join_kernel,
        grid_spec=pltpu.PrefetchScalarGridSpec(
            num_scalar_prefetch=1,
            grid=(4,),
            in_specs=[whole(received)] + [pl.BlockSpec((HD, step), lambda i, s: (0, i))] * 4,
            out_specs=pl.BlockSpec((QUARTER, step), lambda i, s: (0, i)),
            scratch_shapes=[
                pltpu.VMEM((QUARTER, 4 * HD), jnp.bfloat16),
                pltpu.VMEM((4 * HD, step), jnp.bfloat16),
            ],
        ),
        out_shape=jax.ShapeDtypeStruct((QUARTER, width), jnp.bfloat16),
        compiler_params=pltpu.CompilerParams(vmem_limit_bytes=16 * 2**20),
        name="join_heads",
    )(place, received, *weights)


def decode(latents, root_kernel):
    seq_count = latents.shape[0]
    row_patches = seq_count // FR
    me = lax.axis_index("seq")
    ringed = jnp.concatenate([latents[-1:], latents, latents[:1]], axis=0)
    position = (me - row_patches // 2 + seq_count) % seq_count
    patch_row = position % row_patches
    frame_index = position // row_patches
    row_ids = jnp.arange(P_SIZE + 2, dtype=jnp.int32)
    keep = jnp.where(
        row_ids == 0,
        patch_row > 0,
        jnp.where(row_ids == P_SIZE + 1, patch_row < row_patches - 1, True),
    )
    width_cols = BLK * P_SIZE
    windows = []
    for lag in range(3):
        start = (me - lag * row_patches + seq_count) % seq_count
        three = lax.dynamic_slice_in_dim(ringed, start, 3, axis=0)
        pv = three.shape[2] // 2
        three = jnp.concatenate([three[:, :, :pv], three[:, :, pv:]], axis=1)
        slab = (
            three.reshape(3, BLK, P_SIZE, P_SIZE, C)
            .transpose(0, 2, 1, 3, 4)
            .reshape(3 * P_SIZE, width_cols, C)
        )[P_SIZE - 1 : 2 * P_SIZE + 1]
        ok = keep & (frame_index >= lag)
        slab = jnp.where(ok[:, None, None], slab, jnp.zeros_like(slab))
        framed = jnp.pad(slab, ((0, 0), (1, 1), (0, 0)))
        for row_off in range(3):
            for col_off in range(3):
                windows.append(framed[row_off : row_off + P_SIZE, col_off : col_off + width_cols])
    stacked = jnp.concatenate(windows, axis=-1).reshape(P_SIZE * width_cols, 27 * C)
    decoded = jnp.dot(stacked, root_kernel, preferred_element_type=jnp.float32)
    return decoded.reshape(P_SIZE, width_cols, root_kernel.shape[1]).astype(jnp.bfloat16)[None]


def after(value, earlier):
    return lax.optimization_barrier((value, earlier))[0]


def per_device(
    hidden, levels, span_order, modulation, in_weight, out_weight, latent_weight, decoder_weight
):
    span_me = lax.axis_index("span")
    seq_me = lax.axis_index("seq")
    x, h = span_me // NH, span_me % NH
    y, z, core = seq_me // (NZ * NC), (seq_me // NC) % NZ, seq_me % NC
    place = jnp.stack([h, y, z, core, x])
    seq_count = NY * NZ * NC

    normed, gate_row = normalize(levels, hidden[0], modulation)
    w_own = in_weight[0]
    own_blocks, other_blocks = gather_class(normed)
    w_oth = move_core(w_own)
    mine_a, theirs_a = project(own_blocks, w_own, w_oth)
    mine_b, theirs_b = project(other_blocks, w_own, w_oth)
    triples = jnp.concatenate([mine_a, move_core(theirs_a), mine_b, move_core(theirs_b)], axis=0)
    q = triples[:, :HD]
    kv = triples[:, HD:]

    others = tuple(move_x(kv, d) for d in (1, NX - 1, 2))
    q_hi = move_hi(q)

    matrix = latent_matrix(after(out_weight[0], mine_b), gate_row, latent_weight)
    part, acc, top = self_attention(place, q, kv, matrix)
    part = lax.all_to_all(part, "seq", 0, 0, tiled=True)

    out_w = after(out_weight[0], mine_b)
    w_core, w_far = move_core(out_w), move_y(out_w)
    weights = (out_w, w_core, w_far, move_core(w_far))

    acc = after(acc, part)
    chunks = other_attention(span_order, place, q, q_hi, acc, top, (kv, *others))
    groups = [
        [
            span_at(i, hh) * seq_count + seq_at(yy, j, cc)
            for hh in range(NH)
            for yy in range(NY)
            for cc in range(NC)
        ]
        for i in range(NX)
        for j in range(NZ)
    ]
    received = lax.all_to_all(
        chunks, ("span", "seq"), 0, 0, tiled=True, axis_index_groups=groups
    )
    partial = join_heads(place, received, weights)
    z_groups = [[seq_at(yy, j, cc) for j in range(NZ)] for yy in range(NY) for cc in range(NC)]
    part = after(part, partial)
    summed = lax.psum_scatter(
        partial, "seq", scatter_dimension=0, tiled=True, axis_index_groups=z_groups
    ).astype(jnp.float32)
    block_out = (hidden[0].astype(jnp.float32) + gate_row * summed).astype(jnp.bfloat16)[None]

    own_latents = jnp.dot(hidden[0], latent_weight, preferred_element_type=jnp.float32)
    own_latents = jnp.concatenate([own_latents[: BLK // 2], own_latents[BLK // 2 :]], axis=1)
    latents = (jnp.sum(part.astype(jnp.float32), axis=0) + own_latents).astype(jnp.bfloat16)
    group_ids = jnp.arange(span_order.shape[0], dtype=jnp.int32)
    root = jnp.sum(jnp.where(span_order == 0, group_ids, 0))
    spread = lax.all_to_all(
        jnp.broadcast_to(latents[None], (NX * NH,) + latents.shape), "span", 0, 0, tiled=True
    )
    latents = lax.dynamic_index_in_dim(spread, root, 0, keepdims=True)
    every = lax.all_to_all(
        jnp.broadcast_to(latents, (seq_count,) + latents.shape[1:]), "seq", 0, 0, tiled=True
    )
    decoded = decode(every, decoder_weight.reshape(27 * C, decoder_weight.shape[4]))
    return (block_out, decoded)


def solution(mesh):
    placed = (
        P("span", "seq", None),
        P("span"),
        P(),
        P(),
        P("seq", None, None),
        P("seq", None, None),
        P(),
        P(None, None, None, None, "span"),
    )
    return jax.shard_map(
        per_device,
        mesh=mesh,
        in_specs=placed,
        out_specs=(P("span", "seq", None), P("seq", None, None, "span")),
        check_vma=False,
    )
```

```python
import functools
import math

import jax
import jax.numpy as jnp
from jax import lax
from jax.experimental import pallas as pl
from jax.experimental.pallas import tpu as pltpu
from jax.sharding import PartitionSpec as P

HEADS = 24
FR = 4
P_SIZE = 2
C = 16
HD = 128

EPSILON = 1e-06
NEG_LARGE = 1e30

NX, NH, NY, NZ, NC = 4, 2, 2, 8, 2
BLK = 32
QUARTER = NZ * BLK
TAIL = 16


def seq_at(y, z, c):
    return ((y % NY) * NZ + z % NZ) * NC + c % NC


def span_at(x, h):
    return (x % NX) * NH + h % NH


def seq_route(dy=0, dz=0, dc=0):
    return [
        (seq_at(y, z, c), seq_at(y + dy, z + dz, c + dc))
        for y in range(NY)
        for z in range(NZ)
        for c in range(NC)
    ]


def span_route(dx=0, dh=0):
    return [(span_at(x, h), span_at(x + dx, h + dh)) for x in range(NX) for h in range(NH)]


def move_z(a, d):
    return lax.ppermute(a, "seq", seq_route(dz=d))


def move_y(a):
    return lax.ppermute(a, "seq", seq_route(dy=1))


def move_core(a):
    return lax.ppermute(a, "seq", seq_route(dc=1))


def move_x(a, d):
    return lax.ppermute(a, "span", span_route(dx=d))


def move_hi(a):
    return lax.ppermute(a, "span", span_route(dh=1))


HALVES = (
    ((0, 0), (0, 1), (0, 2), (0, 6), (0, 7), (1, 0), (1, 1), (1, 7)),
    ((0, 3), (0, 4), (0, 5), (1, 2), (1, 3), (1, 4), (1, 5), (1, 6)),
)


def block_at(y_apart, core_apart, d):
    half = 0 if (y_apart, d) in HALVES[0] else 1
    return half * 2 * NZ + core_apart * NZ + HALVES[half].index((y_apart, d))


def block_of(at):
    half, core_apart, i = at // (2 * NZ), at // NZ % 2, at % NZ
    y_apart, d = HALVES[half][i]
    return y_apart, core_apart, d


def gather_class(b):
    up1, dn1, y0 = move_z(b, 1), move_z(b, -1), move_y(b)
    up2, dn2 = move_z(up1, 1), move_z(dn1, -1)
    yu1, yd1 = move_y(up1), move_y(dn1)
    up3, dn3 = move_z(up2, 1), move_z(dn2, -1)
    yu2, yd2 = move_y(up2), move_y(dn2)
    far = move_z(up3, 1)
    yu3, yd3 = move_z(yu2, 1), move_z(yd2, -1)
    yfar = lax.ppermute(dn3, "seq", seq_route(dy=1, dz=-1))
    return (b, dn1, dn2, up2, up1, y0, yd1, yu1), (dn3, far, up3, yd2, yd3, yfar, yu3, yu2)


EXP_SCALE = math.log2(math.e) / math.sqrt(HD)


def norm_kernel(level_ref, hidden_ref, mod_ref, out_ref, gate_ref):
    values = hidden_ref[...].astype(jnp.float32)
    row = pl.ds(level_ref[0] % MOD_ROWS, 1)
    center = values - jnp.mean(values, axis=-1, keepdims=True)
    spread = jnp.mean(center * center, axis=-1, keepdims=True)
    scaled = center * lax.rsqrt(spread + EPSILON)
    out_ref[...] = (scaled * (1.0 + mod_ref[1, row, :]) + mod_ref[0, row, :]).astype(jnp.bfloat16)
    gate_ref[...] = mod_ref[2, row, :]


MOD_ROWS = 8


def normalize(levels, rows, modulation):
    width = rows.shape[1]
    return pl.pallas_call(
        norm_kernel,
        grid_spec=pltpu.PrefetchScalarGridSpec(
            num_scalar_prefetch=1,
            grid=(1,),
            in_specs=[
                pl.BlockSpec(rows.shape, lambda i, s: (0, 0)),
                pl.BlockSpec((3, MOD_ROWS, width), lambda i, s: (0, s[0] // MOD_ROWS, 0)),
            ],
            out_specs=[
                pl.BlockSpec(rows.shape, lambda i, s: (0, 0)),
                pl.BlockSpec((1, width), lambda i, s: (0, 0)),
            ],
        ),
        out_shape=[
            jax.ShapeDtypeStruct(rows.shape, jnp.bfloat16),
            jax.ShapeDtypeStruct((1, width), jnp.float32),
        ],
        name="normalize",
    )(levels, rows, modulation.transpose(1, 0, 2))


def latent_kernel(w_ref, gate_ref, lw_ref, o_ref):
    gated = w_ref[...].astype(jnp.float32) * gate_ref[...]
    hi = gated.astype(jnp.bfloat16)
    lo = (gated - hi.astype(jnp.float32)).astype(jnp.bfloat16)
    out = dot_t(hi, lw_ref[...]) + dot_t(lo, lw_ref[...])
    top = out.astype(jnp.bfloat16)
    o_ref[: w_ref.shape[0], :] = top
    o_ref[w_ref.shape[0] :, :] = (out - top.astype(jnp.float32)).astype(jnp.bfloat16)


def latent_matrix(w, gate_row, latent_weight):
    pv = latent_weight.shape[1]
    return pl.pallas_call(
        latent_kernel,
        out_shape=jax.ShapeDtypeStruct((2 * w.shape[0], pv), jnp.bfloat16),
        compiler_params=pltpu.CompilerParams(vmem_limit_bytes=16 * 2**20),
        name="latent_matrix",
    )(w, gate_row, latent_weight.T)


def project_kernel(*refs):
    blocks, (own_ref, oth_ref, mine_ref, theirs_ref, rows) = refs[:NZ], refs[NZ:]
    for i, block in enumerate(blocks):
        rows[i * BLK : i * BLK + BLK, :] = block[...]
    for w_ref, o_ref in ((oth_ref, theirs_ref), (own_ref, mine_ref)):
        out = jnp.dot(rows[...], w_ref[...], preferred_element_type=jnp.float32)
        o_ref[:, :HD] = (out[:, :HD] * EXP_SCALE).astype(jnp.bfloat16)
        o_ref[:, HD:] = out[:, HD:].astype(jnp.bfloat16)


def project(blocks, w_own, w_oth):
    width, cols = w_own.shape
    rows = len(blocks) * BLK
    vmem = pl.BlockSpec(memory_space=pltpu.VMEM)
    return pl.pallas_call(
        project_kernel,
        in_specs=[vmem] * (len(blocks) + 2),
        out_specs=[vmem, vmem],
        out_shape=[jax.ShapeDtypeStruct((rows, cols), jnp.bfloat16)] * 2,
        scratch_shapes=[pltpu.VMEM((rows, width), jnp.bfloat16)],
        compiler_params=pltpu.CompilerParams(vmem_limit_bytes=16 * 2**20),
        cost_estimate=pl.CostEstimate(
            flops=4 * rows * width * cols,
            bytes_accessed=4 * width * cols + 2 * rows * width,
            transcendentals=0,
        ),
        name="project",
    )(*blocks, w_own, w_oth)


def dot_t(a, b):
    return lax.dot_general(a, b, (((1,), (1,)), ((), ())), preferred_element_type=jnp.float32)


TILE = 128


def used_slots(y, z):
    return (y * NZ + z) * NC < HEADS


def self_kernel(s_ref, q_ref, kv_ref, m_ref, o_ref, acc_ref, top_ref, values):
    y, z, core = s_ref[1], s_ref[2], s_ref[3]
    used = used_slots(y, z)
    values[:, :HD] = kv_ref[:, HD:]
    values[:, HD:] = jnp.ones((values.shape[0], HD), jnp.bfloat16)
    for t in range(q_ref.shape[0] // TILE):
        s = dot_t(q_ref[t * TILE : t * TILE + TILE, :], kv_ref[:, :HD])
        top = jnp.max(s, axis=1, keepdims=True)
        p = jnp.exp2(s - top).astype(jnp.bfloat16)
        acc = jnp.dot(p, values[...], preferred_element_type=jnp.float32)
        acc_ref[t * TILE : t * TILE + TILE, :] = acc
        top_ref[t * TILE : t * TILE + TILE, :] = jnp.broadcast_to(top, (TILE, 128))
        att = (acc[:, :HD] / acc[:, HD:]).astype(jnp.bfloat16)
        att = jnp.concatenate([att, att], axis=1)
        part = jnp.dot(att, m_ref[...], preferred_element_type=jnp.float32)
        part = jnp.where(used, part, 0.0).astype(jnp.bfloat16)
        for j in range(TILE // BLK):
            y_apart, core_apart, d = block_of(t * (TILE // BLK) + j)
            at = ((y ^ y_apart) * NZ + (z + d) % NZ) * NC + (core ^ core_apart)
            low, high = j * BLK, j * BLK + BLK // 2
            o_ref[at] = jnp.concatenate(
                [part[low:high, :], part[high : high + BLK // 2, :]], axis=1
            )


def self_attention(place, q, kv, matrix):
    pv = matrix.shape[1]
    rows = q.shape[0]
    return pl.pallas_call(
        self_kernel,
        grid_spec=pltpu.PrefetchScalarGridSpec(
            num_scalar_prefetch=1,
            grid=(1,),
            in_specs=[pl.BlockSpec(a.shape, lambda i, s: (0, 0)) for a in (q, kv, matrix)],
            out_specs=[
                pl.BlockSpec((rows // BLK, BLK // 2, 2 * pv), lambda i, s: (0, 0, 0)),
                pl.BlockSpec((rows, 2 * HD), lambda i, s: (0, 0)),
                pl.BlockSpec((rows, 128), lambda i, s: (0, 0)),
            ],
            scratch_shapes=[pltpu.VMEM((rows, 2 * HD), jnp.bfloat16)],
        ),
        out_shape=[
            jax.ShapeDtypeStruct((rows // BLK, BLK // 2, 2 * pv), jnp.bfloat16),
            jax.ShapeDtypeStruct((rows, 2 * HD), jnp.float32),
            jax.ShapeDtypeStruct((rows, 128), jnp.float32),
        ],
        compiler_params=pltpu.CompilerParams(vmem_limit_bytes=16 * 2**20),
        cost_estimate=pl.CostEstimate(
            flops=6 * rows * rows * HD, bytes_accessed=2**20, transcendentals=rows * rows
        ),
        name="self_attention",
    )(place, q, kv, matrix)


def visit(kv_ref, q, values, acc, top):
    values[:, :HD] = kv_ref[:, HD:]
    values[:, HD:] = jnp.ones((values.shape[0], HD), jnp.bfloat16)
    for t in range(q.shape[0] // TILE):
        rows = slice(t * TILE, t * TILE + TILE)
        s = dot_t(q[rows, :], kv_ref[:, :HD])
        old = top[rows, :1]
        new = jnp.maximum(old, jnp.max(s, axis=1, keepdims=True))
        p = jnp.exp2(s - new).astype(jnp.bfloat16)
        acc[rows, :] = acc[rows, :] * jnp.exp2(old - new) + jnp.dot(
            p, values[...], preferred_element_type=jnp.float32
        )
        top[rows, :] = jnp.broadcast_to(new, (TILE, 128))


def sees(order_ref, s_ref, dh, dx):
    x, h = s_ref[4], s_ref[0]
    mine = order_ref[x * NH + (h ^ dh)]
    return order_ref[((x + dx) % NX) * NH + h] <= mine


def other_kernel(order_ref, s_ref, qa_ref, qb_ref, acc_in, top_in, k0, k1, k2, k3, o_ref, *scratch):
    q, values, acc, top = scratch
    dh = pl.program_id(0)
    q[...] = jnp.where(dh == 0, qa_ref[...], qb_ref[...])

    @pl.when(dh == 0)
    def _():
        acc[...] = acc_in[...]
        top[...] = top_in[...]

    @pl.when(dh == 1)
    def _():
        acc[...] = jnp.zeros_like(acc)
        top[...] = jnp.full_like(top, -NEG_LARGE)

    pl.when((dh == 1) & sees(order_ref, s_ref, dh, 0))(
        functools.partial(visit, k0, q, values, acc, top)
    )
    for dx, ref in ((NX - 1, k1), (1, k2), (2, k3)):
        pl.when(sees(order_ref, s_ref, dh, dx))(
            functools.partial(visit, ref, q, values, acc, top)
        )
    y, core = s_ref[1], s_ref[3]
    for quarter in range(4):
        starts = [block_at(quarter // 2, quarter % 2, d) * BLK for d in range(NZ)]
        gather = lambda ref, cols: jnp.concatenate([ref[i : i + BLK, cols] for i in starts], axis=0)
        total = gather(acc, slice(HD, 2 * HD))
        some = total > 0.0
        safe = jnp.where(some, total, 1.0)
        at = quarter ^ (y * 2 + core)
        o_ref[at, :QUARTER, :] = (gather(acc, slice(0, HD)) / safe).astype(jnp.bfloat16)
        lse = jnp.where(some, gather(top, slice(0, 128)) + jnp.log2(safe), -NEG_LARGE)
        row = lse.T[0:1, :]
        row = jnp.concatenate([row[:, :128], row[:, 128:]], axis=0)
        hi = row.astype(jnp.bfloat16).astype(jnp.float32)
        rest = row - hi
        mid = rest.astype(jnp.bfloat16).astype(jnp.float32)
        pad = jnp.zeros((TAIL - 6, 128), jnp.float32)
        o_ref[at, QUARTER:, :] = jnp.concatenate([hi, mid, rest - mid, pad], axis=0).astype(
            jnp.bfloat16
        )


def whole(a):
    return pl.BlockSpec(a.shape, lambda i, *s: (0,) * a.ndim)


def attention_cost(units, rows):
    pairs = 2 * units * rows * rows
    return pl.CostEstimate(flops=6 * pairs * HD, bytes_accessed=4 * 2**20, transcendentals=pairs)


def other_attention(order, place, qa, qb, acc, top, blocks):
    rows = qa.shape[0]
    chunk = QUARTER + TAIL
    return pl.pallas_call(
        other_kernel,
        grid_spec=pltpu.PrefetchScalarGridSpec(
            num_scalar_prefetch=2,
            grid=(NH,),
            in_specs=[whole(a) for a in (qa, qb, acc, top, *blocks)],
            out_specs=pl.BlockSpec((4, chunk, HD), lambda i, o, s: (i ^ s[0], 0, 0)),
            scratch_shapes=[
                pltpu.VMEM((rows, HD), jnp.bfloat16),
                pltpu.VMEM((rows, 2 * HD), jnp.bfloat16),
                pltpu.VMEM((rows, 2 * HD), jnp.float32),
                pltpu.VMEM((rows, 128), jnp.float32),
            ],
        ),
        out_shape=jax.ShapeDtypeStruct((NH * 4, chunk, HD), jnp.bfloat16),
        compiler_params=pltpu.CompilerParams(vmem_limit_bytes=24 * 2**20),
        cost_estimate=attention_cost(3, rows),
        name="other_attention",
    )(order, place, qa, qb, acc, top, *blocks)


def join_kernel(s_ref, in_ref, w0_ref, w1_ref, w2_ref, w3_ref, o_ref, a_ref, w_ref):
    h, y, z, core = s_ref[0], s_ref[1], s_ref[2], s_ref[3]
    place = h * 4 + y * 2 + core

    @pl.when(pl.program_id(0) == 0)
    def _():
        for r in range(4):
            used = used_slots(y ^ (r // 2), z)
            parts = []
            for dh in range(NH):
                at = (dh * 4 + r) ^ place
                rows = in_ref[at, QUARTER:, :].astype(jnp.float32)
                parts.append((at, rows[0:2] + rows[2:4] + rows[4:6]))
            top = jnp.maximum(parts[0][1], parts[1][1])
            e = [jnp.exp2(lse - top) for _, lse in parts]
            norm = e[0] + e[1]
            for half in range(2):
                out = None
                for (at, _), weight in zip(parts, e):
                    w = jnp.where(used, weight / norm, 0.0)[half : half + 1, :]
                    col = jnp.broadcast_to(w, (128, 128)).T
                    term = in_ref[at, half * 128 : half * 128 + 128, :].astype(jnp.float32) * col
                    out = term if out is None else out + term
                out = out.astype(jnp.bfloat16)
                for j in range(4):
                    start = pl.multiple_of(((z + half * 4 + j) % NZ) * BLK, BLK)
                    a_ref[pl.ds(start, BLK), r * HD : r * HD + HD] = out[j * BLK : j * BLK + BLK]

    for r, ref in enumerate((w0_ref, w1_ref, w2_ref, w3_ref)):
        w_ref[r * HD : r * HD + HD, :] = ref[...]
    o_ref[...] = jnp.dot(a_ref[...], w_ref[...], preferred_element_type=jnp.float32).astype(
        jnp.bfloat16
    )


def join_heads(place, received, weights):
    width = weights[0].shape[1]
    step = width // 4
    return pl.pallas_call(
        join_kernel,
        grid_spec=pltpu.PrefetchScalarGridSpec(
            num_scalar_prefetch=1,
            grid=(4,),
            in_specs=[whole(received)] + [pl.BlockSpec((HD, step), lambda i, s: (0, i))] * 4,
            out_specs=pl.BlockSpec((QUARTER, step), lambda i, s: (0, i)),
            scratch_shapes=[
                pltpu.VMEM((QUARTER, 4 * HD), jnp.bfloat16),
                pltpu.VMEM((4 * HD, step), jnp.bfloat16),
            ],
        ),
        out_shape=jax.ShapeDtypeStruct((QUARTER, width), jnp.bfloat16),
        compiler_params=pltpu.CompilerParams(vmem_limit_bytes=16 * 2**20),
        name="join_heads",
    )(place, received, *weights)


def decode(latents, root_kernel):
    seq_count = latents.shape[0]
    row_patches = seq_count // FR
    me = lax.axis_index("seq")
    ringed = jnp.concatenate([latents[-1:], latents, latents[:1]], axis=0)
    position = (me - row_patches // 2 + seq_count) % seq_count
    patch_row = position % row_patches
    frame_index = position // row_patches
    row_ids = jnp.arange(P_SIZE + 2, dtype=jnp.int32)
    keep = jnp.where(
        row_ids == 0,
        patch_row > 0,
        jnp.where(row_ids == P_SIZE + 1, patch_row < row_patches - 1, True),
    )
    width_cols = BLK * P_SIZE
    windows = []
    for lag in range(3):
        start = (me - lag * row_patches + seq_count) % seq_count
        three = lax.dynamic_slice_in_dim(ringed, start, 3, axis=0)
        pv = three.shape[2] // 2
        three = jnp.concatenate([three[:, :, :pv], three[:, :, pv:]], axis=1)
        slab = (
            three.reshape(3, BLK, P_SIZE, P_SIZE, C)
            .transpose(0, 2, 1, 3, 4)
            .reshape(3 * P_SIZE, width_cols, C)
        )[P_SIZE - 1 : 2 * P_SIZE + 1]
        ok = keep & (frame_index >= lag)
        slab = jnp.where(ok[:, None, None], slab, jnp.zeros_like(slab))
        framed = jnp.pad(slab, ((0, 0), (1, 1), (0, 0)))
        for row_off in range(3):
            for col_off in range(3):
                windows.append(framed[row_off : row_off + P_SIZE, col_off : col_off + width_cols])
    stacked = jnp.concatenate(windows, axis=-1).reshape(P_SIZE * width_cols, 27 * C)
    decoded = jnp.dot(stacked, root_kernel, preferred_element_type=jnp.float32)
    return decoded.reshape(P_SIZE, width_cols, root_kernel.shape[1]).astype(jnp.bfloat16)[None]


def after(value, earlier):
    return lax.optimization_barrier((value, earlier))[0]


def per_device(
    hidden, levels, span_order, modulation, in_weight, out_weight, latent_weight, decoder_weight
):
    span_me = lax.axis_index("span")
    seq_me = lax.axis_index("seq")
    x, h = span_me // NH, span_me % NH
    y, z, core = seq_me // (NZ * NC), (seq_me // NC) % NZ, seq_me % NC
    place = jnp.stack([h, y, z, core, x])
    seq_count = NY * NZ * NC

    normed, gate_row = normalize(levels, hidden[0], modulation)
    w_own = in_weight[0]
    own_blocks, other_blocks = gather_class(normed)
    w_oth = move_core(w_own)
    mine_a, theirs_a = project(own_blocks, w_own, w_oth)
    mine_b, theirs_b = project(other_blocks, w_own, w_oth)
    triples = jnp.concatenate([mine_a, move_core(theirs_a), mine_b, move_core(theirs_b)], axis=0)
    q = triples[:, :HD]
    kv = triples[:, HD:]

    others = tuple(move_x(kv, d) for d in (1, NX - 1, 2))
    q_hi = move_hi(q)

    matrix = latent_matrix(after(out_weight[0], mine_b), gate_row, latent_weight)
    part, acc, top = self_attention(place, q, kv, matrix)
    part = lax.all_to_all(part, "seq", 0, 0, tiled=True)

    out_w = after(out_weight[0], mine_b)
    w_core, w_far = move_core(out_w), move_y(out_w)
    weights = (out_w, w_core, w_far, move_core(w_far))

    chunks = other_attention(span_order, place, q, q_hi, acc, top, (kv, *others))
    chunks = after(chunks, part)
    groups = [
        [
            span_at(i, hh) * seq_count + seq_at(yy, j, cc)
            for hh in range(NH)
            for yy in range(NY)
            for cc in range(NC)
        ]
        for i in range(NX)
        for j in range(NZ)
    ]
    received = lax.all_to_all(
        chunks, ("span", "seq"), 0, 0, tiled=True, axis_index_groups=groups
    )
    partial = join_heads(place, received, weights)
    z_groups = [[seq_at(yy, j, cc) for j in range(NZ)] for yy in range(NY) for cc in range(NC)]
    part = after(part, partial)
    summed = lax.psum_scatter(
        partial, "seq", scatter_dimension=0, tiled=True, axis_index_groups=z_groups
    ).astype(jnp.float32)
    block_out = (hidden[0].astype(jnp.float32) + gate_row * summed).astype(jnp.bfloat16)[None]

    own_latents = jnp.dot(hidden[0], latent_weight, preferred_element_type=jnp.float32)
    own_latents = jnp.concatenate([own_latents[: BLK // 2], own_latents[BLK // 2 :]], axis=1)
    latents = (jnp.sum(part.astype(jnp.float32), axis=0) + own_latents).astype(jnp.bfloat16)
    group_ids = jnp.arange(span_order.shape[0], dtype=jnp.int32)
    root = jnp.sum(jnp.where(span_order == 0, group_ids, 0))
    spread = lax.all_to_all(
        jnp.broadcast_to(latents[None], (NX * NH,) + latents.shape), "span", 0, 0, tiled=True
    )
    latents = lax.dynamic_index_in_dim(spread, root, 0, keepdims=True)
    every = lax.all_to_all(
        jnp.broadcast_to(latents, (seq_count,) + latents.shape[1:]), "seq", 0, 0, tiled=True
    )
    decoded = decode(every, decoder_weight.reshape(27 * C, decoder_weight.shape[4]))
    return (block_out, decoded)


def solution(mesh):
    placed = (
        P("span", "seq", None),
        P("span"),
        P(),
        P(),
        P("seq", None, None),
        P("seq", None, None),
        P(),
        P(None, None, None, None, "span"),
    )
    return jax.shard_map(
        per_device,
        mesh=mesh,
        in_specs=placed,
        out_specs=(P("span", "seq", None), P("seq", None, None, "span")),
        check_vma=False,
    )
```
